256 devices in a mesh: wide: 32 (over x, z_hi, core), narrow: 8 (over y, z_lo).
Axes of the slice: x: 4, y: 4, z: 8 (z_hi: 4, z_lo: 2; z = z_hi * 2 + z_lo), core: 2. Of those that a mesh axis runs over, the one named last changes fastest.
Arguments:
- stash_values: int32 [256, 256, 512], P('wide', 'narrow'), may hold values from -127 to 127
- scale_exp: int32 [32, 32], P('wide', 'narrow'), may hold values from -8 to -6
- w_qkv: bfloat16 [512, 1536], P('wide'), may hold values from -0.25 to 0.25
- w_out: bfloat16 [512, 512], P('wide'), may hold values from -0.25 to 0.25
- w_reduce: bfloat16 [2048, 1024], P('wide'), may hold values from -0.125 to 0.125
- logit_scale: float32 [16], replicated, may hold values from 2 to 20
- bias_table: float32 [225, 16], replicated, may hold values from -6 to 6
- rel_index: int32 [64, 64], replicated, may hold values from 0 to 224
- norm_gain: float32 [512], replicated, may hold values from 0.1 to 1.9
- merge_gain: float32 [1024], replicated, may hold values from 0.1 to 1.9
- cotangent: bfloat16 [128, 128, 1024], P('wide', 'narrow'), may hold values from -6 to 6
Outputs:
- merged: bfloat16 [128, 128, 1024], P('wide', 'narrow')
- grad_input: bfloat16 [256, 256, 512], P('wide', 'narrow')
- grad_qkv: float32 [512, 1536], P('wide', 'narrow')
- grad_out: float32 [512, 512], P('wide', 'narrow')
- grad_reduce: float32 [2048, 1024], P('wide', 'narrow')
The draws below stay inside these ranges and needn't reach their ends.
All inputs are finite; a program needn't handle non-finite values.
Results may differ from the reference program's by a relative error of at most 0.03.
Values may be sent and summed in bfloat16 or wider, within the bound.
A program may use at most 64 MiB of HBM per device.

```python
import math
import jax
import jax.numpy as jnp
from jax import lax

D = 512
HEADS = 16
WIN = 8
REL = 225
NX = 256
NY = 256


def touch_ends(entries, stream_key, least, top_value):
    longest = entries.shape.index(max(entries.shape))
    spots = []
    for shift in (0, 1):
        where = [jax.random.randint(jax.random.fold_in(stream_key, axis), (), 0, length) for axis, length in enumerate(entries.shape)]
        where[longest] = (where[longest] + shift) % entries.shape[longest]
        spots.append(tuple(where))
    return entries.at[spots[0]].set(least).at[spots[1]].set(top_value)


def level_of(key, shape, cuts, smallest, largest):
    def one(dim, blocks):
        heights = jax.random.uniform(jax.random.fold_in(jax.random.fold_in(key, 6), dim), (blocks,), jnp.float32, smallest / len(cuts), largest / len(cuts))
        return jnp.repeat(jnp.exp(heights), shape[dim] // blocks).reshape((-1,) + (1,) * (len(shape) - dim - 1))

    loudness = one(*cuts[0])
    for cut in cuts[1:]:
        loudness = loudness * one(*cut)
    return loudness


def scatter_about(key, shape, deviation, bound, shards=(), kind=jnp.bfloat16):
    values = deviation * jax.random.normal(key, shape, jnp.float32)
    if shards:
        values = values * level_of(key, shape, shards, -0.22, 0.18)
    return jnp.clip(values, -bound, bound).astype(kind)


def setup_inputs(seed: int = 0) -> dict:
    key_of = jax.random.split(jax.random.key(seed), 12)
    return {
        "stash_values": touch_ends(jax.random.randint(key_of[0], (NX, NY, D), -127, 128), jax.random.fold_in(key_of[0], 1), -127, 127).astype(jnp.int32),
        "scale_exp": touch_ends(jax.random.randint(key_of[1], (NX // WIN, NY // WIN), -8, -5), jax.random.fold_in(key_of[1], 1), -8, (-5) - 1).astype(jnp.int32),
        "w_qkv": scatter_about(key_of[2], (D, 3 * D), D ** -0.5, 0.25, ((0, 32),)),
        "w_out": scatter_about(key_of[3], (D, D), D ** -0.5, 0.25, ((0, 32),)),
        "w_reduce": scatter_about(key_of[4], (4 * D, 2 * D), (4 * D) ** -0.5, 0.125, ((0, 32),)),
        "logit_scale": jnp.clip(jnp.exp(jax.random.uniform(key_of[5], (HEADS,), jnp.float32, math.log(2.0), math.log(20.0))), 2.0, 20.0),
        "bias_table": scatter_about(key_of[6], (REL, HEADS), 1.0, 6.0, (), jnp.float32),
        "rel_index": touch_ends(jax.random.randint(key_of[7], (WIN * WIN, WIN * WIN), 0, REL), jax.random.fold_in(key_of[7], 1), 0, REL - 1).astype(jnp.int32),
        "norm_gain": jnp.clip(1.0 + 0.18 * jax.random.normal(key_of[8], (D,), jnp.float32), 0.1, 1.9),
        "merge_gain": jnp.clip(1.0 + 0.18 * jax.random.normal(key_of[9], (2 * D,), jnp.float32), 0.1, 1.9),
        "cotangent": scatter_about(key_of[10], (NX // 2, NY // 2, 2 * D), 1.0, 6.0, ((0, 32), (1, 8))),
    }


def dequantize(stash_values, scale_exp):
    tile_rows, tile_cols, channels = stash_values.shape
    factor = jnp.exp2(scale_exp.astype(jnp.float32))
    blocks = stash_values.astype(jnp.float32).reshape(tile_rows // WIN, WIN, tile_cols // WIN, WIN, channels)
    scaled = blocks * factor[:, None, :, None, None]
    return scaled.reshape(tile_rows, tile_cols, channels).astype(jnp.bfloat16)

def to_windows(grid):
    tile_rows, tile_cols, channels = grid.shape
    blocks = grid.reshape(tile_rows // WIN, WIN, tile_cols // WIN, WIN, channels).transpose(0, 2, 1, 3, 4)
    return blocks.reshape(-1, WIN * WIN, channels)

def from_windows(windows, tile_rows, tile_cols):
    channels = windows.shape[-1]
    blocks = windows.reshape(tile_rows // WIN, tile_cols // WIN, WIN, WIN, channels).transpose(0, 2, 1, 3, 4)
    return blocks.reshape(tile_rows, tile_cols, channels)

def merge_tokens(grid):
    tile_rows, tile_cols, channels = grid.shape
    blocks = grid.reshape(tile_rows // 2, 2, tile_cols // 2, 2, channels).transpose(0, 2, 3, 1, 4)
    return blocks.reshape(tile_rows // 2, tile_cols // 2, 4 * channels)

def split_tokens(joined):
    half_rows, half_cols, wide_channels = joined.shape
    channels = wide_channels // 4
    blocks = joined.reshape(half_rows, half_cols, 2, 2, channels).transpose(0, 3, 1, 2, 4)
    return blocks.reshape(half_rows * 2, half_cols * 2, channels)

def layer_norm(values_in, gain):
    average = lax.optimization_barrier(jnp.mean(values_in, -1, keepdims=True))
    centred = values_in - average
    variance = lax.optimization_barrier(jnp.mean(centred * centred, -1, keepdims=True))
    return centred * lax.rsqrt(variance + 1e-05) * gain

def relative_bias(rel_index, bias_table):
    table_rows = bias_table.shape[0]
    onehot = (rel_index[:, :, None] == jnp.arange(table_rows, dtype=jnp.int32)[None, None, :]).astype(jnp.float32)
    return jnp.einsum('abr,rh->hab', onehot, 16.0 * jax.nn.sigmoid(bias_table), precision=lax.Precision.HIGHEST)

def shift_mask(row_first, col_first, tile_rows, tile_cols, total_rows, total_cols):
    half_win = WIN // 2
    grid_row = row_first + jnp.arange(tile_rows, dtype=jnp.int32)
    grid_col = col_first + jnp.arange(tile_cols, dtype=jnp.int32)
    row_label = (grid_row >= total_rows - WIN).astype(jnp.int32) + (grid_row >= total_rows - half_win).astype(jnp.int32)
    col_label = (grid_col >= total_cols - WIN).astype(jnp.int32) + (grid_col >= total_cols - half_win).astype(jnp.int32)
    labels = row_label[:, None] * 3 + col_label[None, :]
    win_labels = to_windows(labels[:, :, None])[:, :, 0]
    same = win_labels[:, :, None] == win_labels[:, None, :]
    return jnp.where(same, 0.0, -100.0).astype(jnp.float32)

def window_attention(qkv_windows, logit_scale, pos_bias, win_mask):
    heads = logit_scale.shape[0]
    count, tokens, triple = qkv_windows.shape
    head_size = triple // 3 // heads
    pieces = qkv_windows.astype(jnp.float32).reshape(count, tokens, 3, heads, head_size)
    queries = pieces[:, :, 0]
    key_rows = pieces[:, :, 1]
    val_rows = pieces[:, :, 2]
    query_norm = jnp.maximum(jnp.sqrt(lax.optimization_barrier(jnp.sum(queries * queries, -1, keepdims=True))), 1e-12)
    key_norm = jnp.maximum(jnp.sqrt(lax.optimization_barrier(jnp.sum(key_rows * key_rows, -1, keepdims=True))), 1e-12)
    cosines = jnp.einsum('wihd,wjhd->whij', queries / query_norm, key_rows / key_norm, precision=lax.Precision.HIGHEST)
    scores = cosines * logit_scale[None, :, None, None] + pos_bias[None] + win_mask[:, None]
    weights_exp = jnp.exp(scores)
    attn_probs = (weights_exp / lax.optimization_barrier(jnp.sum(weights_exp, -1, keepdims=True))).astype(jnp.bfloat16)
    attended = jnp.einsum('whij,wjhd->wihd', attn_probs.astype(jnp.float32), val_rows, precision=lax.Precision.HIGHEST)
    return attended.reshape(count, tokens, heads * head_size).astype(jnp.bfloat16)

def project(tokens_in, weight):
    return jnp.dot(tokens_in, weight, preferred_element_type=jnp.float32)

def reference(stash_values, scale_exp, w_qkv, w_out, w_reduce, logit_scale, bias_table, rel_index, norm_gain, merge_gain, cotangent):
    half_win = WIN // 2
    inputs = dequantize(stash_values, scale_exp)
    rolled = jnp.roll(inputs, (-half_win, -half_win), (0, 1))
    pos_bias = relative_bias(rel_index, bias_table)
    band_count = NX // WIN

    def band_inputs(band_index):
        row_start = (band_index * WIN).astype(jnp.int32)
        band_rows = lax.dynamic_slice_in_dim(rolled, row_start, WIN, 0)
        flat_rows = band_rows.reshape(-1, D)
        qkv_rows = project(flat_rows, w_qkv).astype(jnp.bfloat16)
        win_mask = shift_mask(row_start, jnp.int32(0), WIN, NY, NX, NY)
        return (row_start, flat_rows, to_windows(qkv_rows.reshape(WIN, NY, 3 * D)), win_mask)

    def forward_band(band_index):
        row_start, flat_rows, qkv_windows, win_mask = band_inputs(band_index)
        attended = from_windows(window_attention(qkv_windows, logit_scale, pos_bias, win_mask), WIN, NY).reshape(-1, D)
        projected = project(attended, w_out)
        rolled_out = (flat_rows.astype(jnp.float32) + layer_norm(projected, norm_gain)).astype(jnp.bfloat16)
        return rolled_out.reshape(WIN, NY, D)
    rolled_out = lax.map(forward_band, jnp.arange(band_count, dtype=jnp.int32)).reshape(NX, NY, D)
    unrolled = jnp.roll(rolled_out, (half_win, half_win), (0, 1))
    joined = merge_tokens(unrolled).reshape(-1, 4 * D)
    reduced = project(joined, w_reduce)

    def merge_norm(values_in):
        return layer_norm(values_in, merge_gain)
    normed, merge_back = jax.vjp(merge_norm, reduced)
    merged = normed.astype(jnp.bfloat16).reshape(NX // 2, NY // 2, 2 * D)
    grad_reduced = merge_back(cotangent.reshape(-1, 2 * D).astype(jnp.float32))[0].astype(jnp.bfloat16)
    grad_reduce = jnp.dot(joined.T, grad_reduced, preferred_element_type=jnp.float32)
    grad_joined = jnp.dot(grad_reduced, w_reduce.T, preferred_element_type=jnp.float32).astype(jnp.bfloat16)
    grad_tokens = split_tokens(grad_joined.reshape(NX // 2, NY // 2, 4 * D))
    grad_rolled = jnp.roll(grad_tokens, (-half_win, -half_win), (0, 1))

    def backward_band(carry, band_index):
        grad_qkv, grad_out = carry
        row_start, flat_rows, qkv_windows, win_mask = band_inputs(band_index)

        def attend(windows_in):
            return window_attention(windows_in, logit_scale, pos_bias, win_mask)
        attended_win, attn_back = jax.vjp(attend, qkv_windows)
        attended = from_windows(attended_win, WIN, NY).reshape(-1, D)
        projected = project(attended, w_out)

        def post_norm(values_in):
            return layer_norm(values_in, norm_gain)
        unused, norm_back = jax.vjp(post_norm, projected)
        grad_rows = lax.dynamic_slice_in_dim(grad_rolled, row_start, WIN, 0).reshape(-1, D)
        grad_projected = norm_back(grad_rows.astype(jnp.float32))[0].astype(jnp.bfloat16)
        grad_out = grad_out + jnp.dot(attended.T, grad_projected, preferred_element_type=jnp.float32)
        grad_attended = jnp.dot(grad_projected, w_out.T, preferred_element_type=jnp.float32).astype(jnp.bfloat16)
        grad_windows = attn_back(to_windows(grad_attended.reshape(WIN, NY, D)))[0]
        grad_qkv_rows = from_windows(grad_windows, WIN, NY).reshape(-1, 3 * D)
        grad_qkv = grad_qkv + jnp.dot(flat_rows.T, grad_qkv_rows, preferred_element_type=jnp.float32)
        grad_band = grad_rows.astype(jnp.float32) + jnp.dot(grad_qkv_rows, w_qkv.T, preferred_element_type=jnp.float32)
        return ((grad_qkv, grad_out), grad_band.astype(jnp.bfloat16).reshape(WIN, NY, D))
    zero_grads = (jnp.zeros((D, 3 * D), jnp.float32), jnp.zeros((D, D), jnp.float32))
    (grad_qkv, grad_out), grad_bands = lax.scan(backward_band, zero_grads, jnp.arange(band_count, dtype=jnp.int32))
    grad_in_rolled = grad_bands.reshape(NX, NY, D)
    grad_input = jnp.roll(grad_in_rolled, (half_win, half_win), (0, 1))
    factor = 1.0 / math.sqrt(NX * NY)
    return (merged, grad_input, grad_qkv * factor, grad_out * factor, grad_reduce * factor)
```

```python
import jax
import jax.numpy as jnp
import numpy as np
from jax import lax
from jax.experimental import pallas as pl
from jax.experimental.pallas import tpu as pltpu
from jax.sharding import PartitionSpec as P

MESH = pl.DeviceIdType.MESH
F32 = jnp.float32
BF16 = jnp.bfloat16
NT = (((1,), (1,)), ((), ()))
TN = (((0,), (0,)), ((), ()))


def one_hot(sources):
    sources = np.asarray(sources).reshape(-1)
    table = np.zeros((len(sources), len(sources)), np.float32)
    table[np.arange(len(sources)), sources] = 1.0
    return table


def token_tables():
    i, j, r, c = np.meshgrid(*map(np.arange, (2, 8, 4, 4)), indexing="ij")
    block_from_natural = one_hot((4 * i + r) * 32 + 4 * j + c)
    k, win, mr, mc = np.meshgrid(*map(np.arange, (4, 4, 4, 4)), indexing="ij")
    i, r = mr // 2, 2 * (mr % 2) + k % 2
    j, c = 2 * win + mc // 2, 2 * (mc % 2) + k // 2
    merge_from_block = one_hot((i * 8 + j) * 16 + r * 4 + c)
    i, j, q, m = np.meshgrid(*map(np.arange, (2, 8, 4, 4)), indexing="ij")
    cot_block_from_natural = one_hot(q * 64 + (2 * i + m // 2) * 16 + 2 * j + m % 2)
    q, win, mr, mc = np.meshgrid(*map(np.arange, (4, 4, 4, 4)), indexing="ij")
    i, j, m = mr // 2, 2 * win + mc // 2, (mr % 2) * 2 + mc % 2
    cot_merge_from_block = one_hot((i * 8 + j) * 16 + q * 4 + m)
    return (
        block_from_natural,
        merge_from_block,
        cot_block_from_natural,
        cot_merge_from_block,
    )


def window_tables():
    k, mr, mc = np.meshgrid(*map(np.arange, (4, 4, 4)), indexing="ij")
    row, col = (2 * mr + k % 2).reshape(-1), (2 * mc + k // 2).reshape(-1)
    order = one_hot(row * 8 + col)
    row_cut = (row[:, None] >= 4) != (row[None, :] >= 4)
    col_cut = (col[:, None] >= 4) != (col[None, :] >= 4)
    tiled = lambda cut: np.tile(cut.astype(np.float32), (1, 4))
    return order, tiled(row_cut), tiled(col_cut)


def same_block(rows, row_size, cols, col_size):
    return (
        (np.arange(rows) // row_size)[:, None] == (np.arange(cols) // col_size)[None]
    ).astype(np.float32)


T_BLOCK, T_MERGE, T_CBLOCK, T_CMERGE = token_tables()
COLUMNS_64 = one_hot(np.arange(512).reshape(4, 2, 64).transpose(1, 0, 2)).T
COLUMNS_16 = one_hot(np.arange(512).reshape(16, 2, 16).transpose(1, 0, 2)).T
WIN_ORDER, ROW_CUT, COL_CUT = window_tables()


def const(table, dtype=BF16):
    return jnp.asarray(table, dtype)


class Place:
    def __init__(self):
        wide, narrow = lax.axis_index("wide"), lax.axis_index("narrow")
        self.wide, self.narrow = wide, narrow
        self.core = lax.rem(wide, 2)
        self.zh = lax.rem(lax.div(wide, 2), 4)
        self.x = lax.div(wide, 8)
        self.y = lax.div(narrow, 2)
        self.zl = lax.rem(narrow, 2)
        self.z = 2 * self.zh + self.zl
        self.sibling = (wide + 1 - 2 * self.core, narrow)

    def at_x(self, step):
        return ((lax.rem(self.x + step + 4, 4) * 4 + self.zh) * 2 + self.core, self.narrow)

    def at_y(self, step):
        return (self.wide, lax.rem(self.y + step + 4, 4) * 2 + self.zl)

    def at_z(self, step):
        z = lax.rem(self.z + step + 8, 8)
        return ((self.x * 4 + lax.div(z, 2)) * 2 + self.core, self.y * 2 + lax.rem(z, 2))

    def at_tile(self, rows, cols):
        return (lax.rem(self.wide + rows + 32, 32), lax.rem(self.narrow + cols + 8, 8))


class Sender:
    def __init__(self, send_sem, recv_sem, local_sem):
        self.send_sem, self.recv_sem, self.local_sem = send_sem, recv_sem, local_sem
        self.started, self.count, self.local_count = [], 0, 0

    def remote(self, src, dst, device):
        copy = pltpu.make_async_remote_copy(
            src_ref=src,
            dst_ref=dst,
            send_sem=self.send_sem.at[self.count],
            recv_sem=self.recv_sem.at[self.count],
            device_id=device,
            device_id_type=MESH,
        )
        self.count += 1
        copy.start()
        self.started.append(copy)
        return copy

    def local(self, src, dst):
        copy = pltpu.make_async_copy(src, dst, self.local_sem.at[self.local_count])
        self.local_count += 1
        copy.start()
        return copy

    def drain(self):
        for copy in self.started:
            copy.wait_send()
        self.started = []


def greet(devices):
    barrier = pltpu.get_barrier_semaphore()
    for device in devices:
        pl.semaphore_signal(barrier, inc=1, device_id=device, device_id_type=MESH)
    pl.semaphore_wait(barrier, len(devices))


def lanes(start, size):
    return pl.ds(pl.multiple_of(start, 128), size)


def mm(a, b):
    return jnp.dot(a, b, preferred_element_type=F32)


def dg(a, b, dims):
    return lax.dot_general(a, b, dims, preferred_element_type=F32)


def add(*parts):
    total = parts[0].astype(F32)
    for one in parts[1:]:
        total = total + one.astype(F32)
    return total


def split_mm(values, table):
    high = values.astype(BF16)
    low = (values - high.astype(F32)).astype(BF16)
    both = mm(jnp.concatenate([high, low], 0), table)
    return both[: len(values)] + both[len(values) :]


def norm_parts(values):
    centred = values - jnp.mean(values, -1, keepdims=True)
    scale = lax.rsqrt(jnp.mean(centred * centred, -1, keepdims=True) + 1e-05)
    return centred * scale, scale


def norm_back(cot, normed, scale, gain):
    cot = cot * gain
    shared = jnp.mean(cot, -1, keepdims=True) + normed * jnp.mean(cot * normed, -1, keepdims=True)
    return scale * (cot - shared)


EVERY = pl.ds(0, 4)


class Gather:
    def __init__(self, at, go, shard, whole, cut, quarters=False, direct=False):
        self.at, self.go, self.shard, self.whole, self.cut = at, go, shard, whole, cut
        self.quarters, self.direct = quarters, direct
        self.x_left, self.x_right, self.x_far = (lax.rem(at.x + step, 4) for step in (3, 1, 2))
        self.y_left, self.y_right, self.y_far = (lax.rem(at.y + step, 4) for step in (3, 1, 2))
        self.shared = []

    def part(self, xs, zs, y=None):
        y = self.at.y if y is None else y
        return self.whole.at[(xs, zs, self.at.core) + self.cut(y)]

    def move(self, xs, zs, device, y=None):
        ref = self.part(xs, zs, y)
        return self.go.remote(ref, ref, device)

    def share(self, xs, zs, y=None):
        self.shared.append(self.move(xs, zs, self.at.sibling, y))

    def start(self):
        at = self.at
        own, there = self.shard.at[self.cut(at.y)], self.part(at.x, at.zh)
        way = 2 * at.zl - 1
        self.z = [self.go.remote(own, there, at.at_z(way * step)) for step in (1, 2, 3)]
        self.mine = self.go.local(own, there)

    def x1(self):
        at = self.at
        self.mine.wait()
        for copy in self.z:
            copy.wait_recv()
        steps = (1, 2, -1) if self.direct else (1, -1)
        self.x = [self.move(at.x, EVERY, at.at_x(step)) for step in steps]
        if not self.quarters:
            self.share(at.x, EVERY)

    def x2(self):
        at = self.at
        self.x[0].wait_recv()
        far = [self.move(self.x_left, pl.ds(0, 2), at.at_x(1))]
        self.x[1].wait_recv()
        far.append(self.move(self.x_right, pl.ds(2, 2), at.at_x(-1)))
        self.x = far
        if not self.quarters:
            self.share(self.x_left, EVERY)
            self.share(self.x_right, EVERY)

    def x3(self):
        for copy in self.x:
            copy.wait_recv()
        if not self.quarters:
            self.share(self.x_far, EVERY)

    def y1(self):
        at = self.at
        self.x3()
        self.y = [self.move(EVERY, EVERY, at.at_y(step)) for step in (1, -1)]
        self.share(EVERY, EVERY)

    def y2(self):
        at = self.at
        self.y[0].wait_recv()
        far = [self.move(pl.ds(0, 2), EVERY, at.at_y(1), self.y_left)]
        self.y[1].wait_recv()
        far.append(self.move(pl.ds(2, 2), EVERY, at.at_y(-1), self.y_right))
        self.y = far
        self.share(EVERY, EVERY, self.y_left)
        self.share(EVERY, EVERY, self.y_right)

    def y3(self):
        for copy in self.y:
            copy.wait_recv()
        self.share(EVERY, EVERY, self.y_far)

    def done(self):
        for copy in self.shared:
            copy.wait_recv()


def y_cut(j):
    return lanes(j * 256, 256)


class Reduce:
    def __init__(self, at, go, m, bx1, bx2, by1, by2, cx, cy, dx, dy, zsend, zland):
        self.at, self.go, self.m = at, go, m
        self.bx1, self.bx2, self.by1, self.by2 = bx1, bx2, by1, by2
        self.cx, self.cy = cx, cy
        self.dx, self.dy = dx, dy
        self.zsend, self.zland = zsend, zland
        self.xs = [lax.rem(at.x + step, 4) for step in (2, 1, 3, 0)]
        self.ys = [lax.rem(at.y + step, 4) for step in (2, 1, 3, 0)]
        self.x_left, self.x_right = at.at_x(-1), at.at_x(1)
        self.y_left, self.y_right = at.at_y(-1), at.at_y(1)

    def both(self, src, dst, right, left, step):
        if step == 1:
            pairs = ((src(0, pl.ds(0, 2)), right), (src(0, pl.ds(2, 2)), left))
        else:
            pairs = ((src(1, EVERY), right), (src(2, EVERY), left))
        return [self.go.remote(ref, dst.at[n], device) for n, (ref, device) in enumerate(pairs)]

    def x_src(self, n, part):
        return self.m.at[0, self.xs[n], part]

    def y_src(self, n, part):
        return self.m.at[1, part, :, :, y_cut(self.ys[n])]

    def first_x(self):
        self.b_x = self.both(self.x_src, self.bx1, self.x_right, self.x_left, 1)

    def first_y(self):
        self.b_y = self.both(self.y_src, self.by1, self.y_right, self.y_left, 1)

    def second_x(self):
        m, xs = self.m, self.xs
        for copy in self.b_x:
            copy.wait_recv()
        for s in range(2):
            m[0, xs[1], s] = add(m[0, xs[1], s], self.bx1[0, s]).astype(BF16)
            m[0, xs[2], 2 + s] = add(m[0, xs[2], 2 + s], self.bx1[1, s]).astype(BF16)
        self.b_x = self.both(self.x_src, self.bx2, self.x_right, self.x_left, 2)

    def second_y(self):
        m, ys = self.m, self.ys
        for copy in self.b_y:
            copy.wait_recv()
        for s in range(2):
            cut = y_cut(ys[1])
            m[1, s, :, :, cut] = add(m[1, s, :, :, cut], self.by1[0, s]).astype(BF16)
            cut = y_cut(ys[2])
            m[1, 2 + s, :, :, cut] = add(m[1, 2 + s, :, :, cut], self.by1[1, s]).astype(BF16)
        self.b_y = self.both(self.y_src, self.by2, self.y_right, self.y_left, 2)

    def third_x(self):
        at = self.at
        for copy in self.b_x:
            copy.wait_recv()
        for s in range(4):
            self.cx[s] = add(self.m[0, at.x, s], self.bx2[0, s], self.bx2[1, s]).astype(BF16)
        self.d = []
        for n, step in ((0, 2), (1, 1), (2, 3)):
            src = self.cx.at[:, :, y_cut(self.ys[n])]
            self.d.append(self.go.remote(src, self.dx.at[n], at.at_y(step)))

    def third_y(self):
        at = self.at
        for copy in self.b_y:
            copy.wait_recv()
        for s in range(4):
            self.cy[s] = add(self.m[1, s, :, :, y_cut(at.y)], self.by2[0, s], self.by2[1, s]).astype(BF16)
        for n, step in ((0, 2), (1, 1), (2, 3)):
            self.d.append(self.go.remote(self.cy.at[self.xs[n]], self.dy.at[n], at.at_x(step)))

    def fourth(self, pack):
        for copy in self.d:
            copy.wait_recv()
        for h in range(4):
            a = add(self.cx[h, :, y_cut(self.at.y)], *[self.dx[n, h] for n in range(3)])
            b = add(self.cy[self.at.x, h], *[self.dy[n, h] for n in range(3)])
            for low in range(2):
                self.zsend[h, low] = pack(a, b, low).astype(BF16)
        self.last = []
        for step in range(1, 8):
            z = lax.rem(self.at.z + step, 8)
            src = self.zsend.at[lax.div(z, 2), lax.rem(z, 2)]
            self.last.append(self.go.remote(src, self.zland.at[step - 1], self.at.at_z(step)))

    def fifth(self):
        total = self.zsend[self.at.zh, self.at.zl].astype(F32)
        for step in range(7):
            self.last[step].wait_recv()
            total = total + self.zland[step].astype(F32)
        return total


def pack_reduce(a, b, low):
    cut = slice(128 * low, 128 * low + 128)
    return jnp.concatenate([a[:, cut], b[:, cut]], 0)


def pack_qkv_out(a, b, low):
    if low == 0:
        rows = a[:, 0:128], jnp.concatenate([a[:, 128:192], b[:, 128:192]], 1)
    else:
        rows = (
            jnp.concatenate([a[:, 192:256], b[:, 0:64]], 1),
            jnp.concatenate([b[:, 64:128], b[:, 192:256]], 1),
        )
    return jnp.concatenate(rows, 0)


def reduce_scratch(rows, z_rows):
    return [
        pltpu.VMEM((2, 2, rows, 1024), BF16),
        pltpu.VMEM((2, 4, rows, 1024), BF16),
        pltpu.VMEM((2, 2, 4, rows, 256), BF16),
        pltpu.VMEM((2, 4, 4, rows, 256), BF16),
        pltpu.VMEM((4, rows, 1024), BF16),
        pltpu.VMEM((4, 4, rows, 256), BF16),
        pltpu.VMEM((3, 4, rows, 256), BF16),
        pltpu.VMEM((3, 4, rows, 256), BF16),
        pltpu.VMEM((4, 2, z_rows, 128), BF16),
        pltpu.VMEM((7, z_rows, 128), BF16),
    ]


COPIES = 12 + 18 + 3 * 11 + 15 + 8 + 2 * (8 + 6 + 7) + 16


def block_kernel(
    stash_ref, exp_ref, cot_ref, wq_ref, wo_ref, wr_ref, ls_ref, table_ref, rel_ref, ng_ref, mg_ref,
    t_block_ref, t_cblock_ref, order_ref, row_cut_ref, col_cut_ref, *rest,
):
    tables, rest = rest[:11], rest[11:]
    (
    merged_ref, gin_ref, gq_ref, go_ref, gr_ref,
    blk, land, back, oland, ocland, wq, wo, wr,
    x_tok, cot_tok, qkv, qs, kh, rq, rk, probs, bias, bias_rows, table, mask, att, d_att, dqs, dkh, dqkv,
    xhat, xscale, ro, dproj, dtok, xt, at_t, ls_row, ro_cols, ro_theirs, x_cols, x_theirs, at_cols, at_theirs,
    dred, dred_theirs, dproj_theirs, dqkv_theirs, fa, fb, mb,
    t_merge_ref, t_cmerge_ref, t_unblock_ref, t_unmerge_ref, t_cunblock_ref, t_cunmerge_ref,
    columns_ref, columns_16_ref, bd64_ref, bd32_ref, heads_ref,
    *rest,
    ) = rest
    a_bufs, b_bufs, (send_sem, recv_sem, local_sem) = rest[0:10], rest[10:20], rest[20:]
    held = (
        t_merge_ref, t_cmerge_ref, t_unblock_ref, t_unmerge_ref, t_cunblock_ref, t_cunmerge_ref,
        columns_ref, columns_16_ref, bd64_ref, bd32_ref, heads_ref,
    )
    go = Sender(send_sem, recv_sem, local_sem)
    table_copies = [go.local(src, dst) for src, dst in zip(tables, held)]
    at = Place()
    c = at.core
    greet(
        [at.sibling]
        + [at.at_x(step) for step in (1, 2, 3)]
        + [at.at_y(step) for step in (1, 2, 3)]
        + [at.at_z(step) for step in range(1, 8)]
        + [at.at_tile(*step) for step in ((-1, 0), (0, -1), (-1, -1), (1, 0), (0, 1), (1, 1))]
    )
    all_rows = pl.ds(0, 16)
    q_y = Gather(at, go, wq_ref, wq, lambda y: (all_rows, lanes(512 + 256 * y, 256)), True, True)
    q_x = Gather(at, go, wq_ref, wq, lambda y: (all_rows, pl.ds(0, 512)))
    o_x = Gather(at, go, wo_ref, wo, lambda y: (all_rows, pl.ds(0, 512)))
    r_x = Gather(at, go, wr_ref, wr, lambda y: (pl.ds(0, 64), pl.ds(0, 512)))
    r_y = Gather(at, go, wr_ref, wr, lambda y: (pl.ds(pl.multiple_of(16 * y, 16), 16), pl.ds(512, 512)), True)

    q_y.start()

    factor_of = exp_ref[...]
    factor_of = jnp.where(factor_of == -8, 2.0**-8, jnp.where(factor_of == -7, 2.0**-7, 2.0**-6))
    in_window = lax.broadcasted_iota(jnp.int32, (32, 512), 0) // 8
    factor = jnp.zeros((32, 512), F32)
    for w in range(4):
        factor = jnp.where(in_window == w, factor_of[:, w : w + 1], factor)
    inputs = stash_ref[...].astype(F32) * factor[None]
    blk[:, 0:512] = mm(t_block_ref[...], inputs.reshape(256, 512).astype(BF16)).astype(BF16)
    r_y.start()
    cot = cot_ref[...].astype(F32).reshape(64, 1024).astype(BF16)
    cot = jnp.concatenate([cot[:, 256 * q : 256 * q + 256] for q in range(4)], 0)
    blk[:, 512:768] = mm(t_cblock_ref[...], cot).astype(BF16)
    q_x.start()
    q_y.x1()
    r_x.start()
    r_y.x1()
    q_x.x1()
    o_x.start()
    q_y.y1()
    q_x.x2()

    table[...] = jnp.zeros((16, 256), F32)
    table[:, 0:225] = 16.0 * jax.nn.sigmoid(table_ref[...])
    by_head = table[...]
    high = by_head.astype(BF16)
    low = (by_head - high.astype(F32)).astype(BF16)
    both = jnp.concatenate([high, low], 0)
    rel = mm(order_ref[...], rel_ref[...].astype(F32).astype(BF16)).astype(BF16)
    rel = dg(rel, order_ref[...], NT).astype(jnp.int32)
    rel = jnp.concatenate([rel[16 * j : 16 * j + 16] for j in range(4)], 1)
    entry = lax.broadcasted_iota(jnp.int32, (256, 256), 0)

    def bias_of(rows):
        for a in rows:
            chosen = jnp.where(entry == rel[a : a + 1], 1.0, 0.0).astype(BF16)
            got = mm(both, chosen)
            got = got[0:16] + got[16:32]
            for j in range(4):
                bias_rows[16 * j + a] = got[:, 64 * j : 64 * j + 64]

    bias_of(range(0, 5))
    r_y.x2()
    halo = [
        go.remote(blk.at[pl.ds(16, 112)], land.at[pl.ds(128, 112)], at.at_tile(-1, 0)),
        go.remote(blk.at[pl.ds(128, 16)], land.at[pl.ds(112, 16)], at.at_tile(0, -1)),
        go.remote(blk.at[pl.ds(0, 16)], land.at[pl.ds(240, 16)], at.at_tile(-1, -1)),
    ]
    r_x.x1()
    bias_of(range(5, 10))
    q_y.y2()
    q_x.x3()
    r_y.y1()
    bias_of(range(10, 16))
    o_x.x1()
    q_y.y3()
    for g in range(4):
        bias[g] = jnp.concatenate([bias_rows[:, 4 * g + h, :] for h in range(4)], 1)
    last_rows = (at.wide == 31).astype(F32)
    last_cols = (at.narrow == 7).astype(F32)
    mask[0] = row_cut_ref[...] * last_rows * -100.0
    mask[1] = jnp.maximum(row_cut_ref[...] * last_rows, col_cut_ref[...] * last_cols) * -100.0
    lane = lax.broadcasted_iota(jnp.int32, (1, 512), 1) // 32
    scales = jnp.zeros((1, 512), F32)
    for h in range(16):
        scales = jnp.where(lane == h, ls_ref[:, h : h + 1], scales)
    ls_row[...] = scales


    for copy in halo:
        copy.wait_recv()
    for copy in table_copies:
        copy.wait()
    r_x.x2()
    land[pl.ds(0, 112)] = blk[pl.ds(144, 112)]
    x_tok[...] = mm(t_merge_ref[...], land[:, 0:512]).astype(BF16)
    cot = mm(t_cmerge_ref[...], land[:, 512:768]).astype(BF16)
    cot_tok[...] = jnp.concatenate([cot[64 * q : 64 * q + 64] for q in range(4)], 1)
    x_cols[...] = mm(x_tok[...], columns_16_ref[...]).astype(BF16)
    not_mine = lanes(256 * (1 - c), 256)
    mine = lanes(256 * c, 256)
    x_swap = go.remote(x_cols.at[:, not_mine], x_theirs, at.sibling)
    q_x.done()
    o_x.x2()
    q_y.done()
    r_y.y2()

    qkv[...] = mm(x_tok[...], wq[...].reshape(512, 1536)).astype(BF16)
    r_x.x3()
    o_x.x3()
    for start, inverse, unit in ((0, rq, qs), (512, rk, kh)):
        for n in range(2):
            cut = slice(256 * n, 256 * n + 256)
            for row in range(0, 256, 128):
                rows = slice(row, row + 128)
                raw = qkv[rows, start + 256 * n : start + 256 * n + 256].astype(F32)
                inv = lax.rsqrt(jnp.maximum(split_mm(raw * raw, bd32_ref[...]), 1e-24))
                inverse[rows, cut] = inv
                raw = raw * inv
                if start == 0:
                    raw = raw * ls_row[:, cut]
                unit[rows, cut] = raw.astype(BF16)
    x_swap.wait_recv()
    xt[:, 0:256] = x_cols[:, mine].T
    xt[:, 256:512] = x_theirs[...].T

    def window(ref, win, cut):
        return jnp.concatenate([ref[pl.ds(64 * k + 16 * win, 16), cut] for k in range(4)], 0)

    def put_window(ref, win, cut, values):
        for k in range(4):
            ref[pl.ds(64 * k + 16 * win, 16), cut] = values[16 * k : 16 * k + 16]

    def spread(rows):
        return jnp.concatenate([rows] * 4, 0) * heads_ref[...]

    def fold(values):
        values = values * heads_ref[...].astype(F32)
        return (values[0:64] + values[64:128]) + (values[128:192] + values[192:256])

    def forward(g):
        cut = slice(g * 128, g * 128 + 128)
        v_cut = slice(g * 128 + 1024, g * 128 + 1152)
        weights = []
        for win in range(4):
            scores = dg(window(qs, win, cut), spread(window(kh, win, cut)), NT)
            weights.append(jnp.exp(scores + bias[g] + mask[1 if win == 3 else 0]))
        totals = split_mm(jnp.concatenate(weights, 0), bd64_ref[...])
        for win in range(4):
            p = weights[win] / totals[64 * win : 64 * win + 64]
            probs[g, win] = p
            values = spread(window(qkv, win, v_cut))
            put_window(att, win, cut, mm(p.astype(BF16), values).astype(BF16))

    forward(0)
    forward(1)
    r_y.y3()
    forward(2)
    forward(3)
    r_x.done()
    at_cols[...] = mm(att[...], columns_16_ref[...]).astype(BF16)
    at_swap = go.remote(at_cols.at[:, not_mine], at_theirs, at.sibling)
    o_x.done()
    xhat[...] = mm(att[...], wo[...].reshape(512, 512))
    for row in range(0, 256, 64):
        rows = slice(row, row + 64)
        normed, scale = norm_parts(xhat[rows])
        xhat[rows] = normed
        xscale[rows] = scale
        ro[rows] = (x_tok[rows].astype(F32) + normed * ng_ref[...]).astype(BF16)
    ro_cols[...] = mm(ro[...], columns_ref[...]).astype(BF16)
    swap = [go.remote(ro_cols.at[:, not_mine], ro_theirs, at.sibling)]
    r_y.done()

    reduced = jnp.zeros((64, 1024), F32)
    for k in range(4):
        reduced += mm(ro[64 * k : 64 * k + 64], wr[k].reshape(512, 1024))
    normed, scale = norm_parts(reduced)
    dred[...] = norm_back(cot_tok[...].astype(F32), normed, scale, mg_ref[...]).astype(BF16)
    swap.append(go.remote(dred, dred_theirs, at.sibling))
    merged = (normed * mg_ref[...]).astype(BF16)
    merged = jnp.concatenate([merged[:, 256 * q : 256 * q + 256] for q in range(4)], 0)
    mb[...] = mm(t_cunmerge_ref[...], merged).astype(BF16)

    def send_back(tile, landing):
        return [
            go.remote(tile.at[pl.ds(128, 112)], landing.at[pl.ds(16, 112)], at.at_tile(1, 0)),
            go.remote(tile.at[pl.ds(112, 16)], landing.at[pl.ds(128, 16)], at.at_tile(0, 1)),
            go.remote(tile.at[pl.ds(240, 16)], landing.at[pl.ds(0, 16)], at.at_tile(1, 1)),
        ]

    for k in range(4):
        dtok[64 * k : 64 * k + 64] = dg(dred[...], wr[k].reshape(512, 1024), NT).astype(BF16)

    for copy in swap:
        copy.wait_recv()
    a_sum = Reduce(at, go, fa, *a_bufs)
    grads = jnp.concatenate([dred[...], dred_theirs[...]], 0)
    for n in range(4):
        k = a_sum.xs[n]
        rows = pl.ds(pl.multiple_of(64 * k, 64), 64)
        tokens = jnp.concatenate([ro_cols[rows, mine], ro_theirs[rows]], 0).T
        for cut in (slice(0, 512), slice(512, 1024)):
            got = mm(tokens, grads[:, cut]).astype(BF16).reshape(4, 64, 512)
            fa[0, k, :, :, cut] = got[:, 0:32]
            fa[1, k, :, :, cut] = got[:, 32:64]
        if n == 0:
            a_sum.first_x()
    a_sum.first_y()
    merged_back = send_back(mb, ocland)

    for row in range(0, 256, 64):
        rows = slice(row, row + 64)
        got = norm_back(dtok[rows].astype(F32), xhat[rows], xscale[rows], ng_ref[...])
        dproj[rows] = got.astype(BF16)
    dproj_swap = go.remote(dproj, dproj_theirs, at.sibling)
    a_sum.second_x()
    at_swap.wait_recv()
    at_t[:, 0:256] = at_cols[:, mine].T
    at_t[:, 256:512] = at_theirs[...].T
    d_att[...] = dg(dproj[...], wo[...].reshape(512, 512), NT).astype(BF16)
    a_sum.second_y()

    def backward(g):
        cut = slice(g * 128, g * 128 + 128)
        v_cut = slice(g * 128 + 1024, g * 128 + 1152)
        dps = []
        for win in range(4):
            dp = dg(window(d_att, win, cut), spread(window(qkv, win, v_cut)), NT)
            dps.append(dp.astype(BF16).astype(F32))
        alike = split_mm(jnp.concatenate([probs[g, win] * dps[win] for win in range(4)], 0), bd64_ref[...])
        for win in range(4):
            p = probs[g, win]
            ds = (p * (dps[win] - alike[64 * win : 64 * win + 64])).astype(BF16)
            put_window(dqs, win, cut, mm(ds, spread(window(kh, win, cut))))
            put_window(dkh, win, cut, fold(dg(ds, window(qs, win, cut), TN)))
            put_window(dqkv, win, v_cut, fold(dg(p.astype(BF16), window(d_att, win, cut), TN)).astype(BF16))

    for g in range(4):
        backward(g)

    def swap_dqkv(start):
        cut = pl.ds(start, 512)
        return go.remote(dqkv.at[:, cut], dqkv_theirs.at[:, cut], at.sibling)

    dqkv_swap = [swap_dqkv(1024)]
    for start, inverse, grad in ((0, rq, dqs), (512, rk, dkh)):
        for n in range(2):
            cut = slice(256 * n, 256 * n + 256)
            both_cut = slice(start + 256 * n, start + 256 * n + 256)
            for row in range(0, 256, 128):
                rows = slice(row, row + 128)
                inv = inverse[rows, cut]
                unit = qkv[rows, both_cut].astype(F32) * inv
                d_unit = grad[rows, cut]
                if start == 0:
                    d_unit = d_unit * ls_row[:, cut]
                along = split_mm(unit * d_unit, bd32_ref[...])
                along = jnp.where(inv < 1e12, along, 0.0)
                dqkv[rows, both_cut] = (inv * (d_unit - unit * along)).astype(BF16)
        dqkv_swap.append(swap_dqkv(start))
    a_sum.third_x()
    dproj_swap.wait_recv()
    d_out = jnp.concatenate([dproj[...], dproj_theirs[...]], 0)
    out = mm(at_t[...], d_out).astype(BF16)
    for y in range(4):
        fb[1, :, :, :, 256 * y + 128 : 256 * y + 256] = out[:, 128 * y : 128 * y + 128].reshape(4, 4, 16, 128)

    for copy in dqkv_swap:
        copy.wait_recv()
    b_sum = Reduce(at, go, fb, *b_bufs)
    for n in range(4):
        y = b_sum.ys[n]
        cut = lanes(384 * y, 384)
        grads = jnp.concatenate([dqkv[:, cut], dqkv_theirs[:, cut]], 0)
        got = mm(xt[...], grads).astype(BF16)
        fb[0, :, :, :, y_cut(y)] = got[:, 0:256].reshape(4, 4, 16, 256)
        fb[1, :, :, :, lanes(256 * y, 128)] = got[:, 256:384].reshape(4, 4, 16, 128)
    b_sum.first_x()
    b_sum.first_y()
    a_sum.third_y()
    d_in = dtok[...].astype(F32) + dg(dqkv[...], wq[...].reshape(512, 1536), NT)
    back[...] = mm(t_unmerge_ref[...], d_in.astype(BF16)).astype(BF16)
    grad_back = send_back(back, oland)
    b_sum.second_x()
    b_sum.second_y()
    a_sum.fourth(pack_reduce)
    for copy in grad_back:
        copy.wait_recv()
    oland[pl.ds(144, 112)] = back[pl.ds(0, 112)]
    b_sum.third_x()
    b_sum.third_y()
    b_sum.fourth(pack_qkv_out)
    for copy in merged_back:
        copy.wait_recv()
    ocland[pl.ds(144, 112)] = mb[pl.ds(0, 112)]
    got = mm(t_cunblock_ref[...], ocland[...]).astype(BF16)
    for q in range(4):
        merged_ref[:, :, 256 * q : 256 * q + 256] = got[64 * q : 64 * q + 64].reshape(4, 16, 256)
    gin_ref[...] = mm(t_unblock_ref[...], oland[...]).astype(BF16).reshape(8, 32, 512)
    factor = 1.0 / 256.0
    gr_ref[...] = a_sum.fifth() * factor
    go.drain()
    total = b_sum.fifth() * factor
    gq_ref[:, 0:128] = total[0:16]
    gq_ref[:, 128:192] = total[16:32, 0:64]
    go_ref[...] = total[16:32, 64:128]


def hand_on(*refs):
    for src, dst in zip(refs[:5], refs[5:]):
        dst[...] = src[...]


def on_device(
    stash_values, scale_exp, w_qkv, w_out, w_reduce, logit_scale, bias_table, rel_index, norm_gain, merge_gain, cotangent
):
    vmem = pl.BlockSpec(memory_space=pltpu.VMEM)
    sems = pltpu.SemaphoreType.DMA
    outputs = (
        jax.ShapeDtypeStruct((4, 16, 1024), BF16),
        jax.ShapeDtypeStruct((8, 32, 512), BF16),
        jax.ShapeDtypeStruct((16, 192), F32),
        jax.ShapeDtypeStruct((16, 64), F32),
        jax.ShapeDtypeStruct((64, 128), F32),
    )
    tokens = lambda width, kind=BF16: pltpu.VMEM((256, width), kind)
    results = pl.pallas_call(
        block_kernel,
        out_shape=outputs,
        in_specs=[vmem] * 16 + [pl.BlockSpec(memory_space=pl.ANY)] * 11,
        out_specs=(vmem,) * 5,
        scratch_shapes=[
            tokens(768), tokens(768), tokens(512), tokens(512), tokens(256),
            pltpu.VMEM((4, 4, 2, 16, 1536), BF16),
            pltpu.VMEM((4, 4, 2, 16, 512), BF16),
            pltpu.VMEM((4, 4, 2, 64, 1024), BF16),
            tokens(512),
            pltpu.VMEM((64, 1024), BF16),
            tokens(1536), tokens(512), tokens(512), tokens(512, F32), tokens(512, F32),
            pltpu.VMEM((4, 4, 64, 256), F32),
            pltpu.VMEM((4, 64, 256), F32),
            pltpu.VMEM((64, 16, 64), F32),
            pltpu.VMEM((16, 256), F32),
            pltpu.VMEM((2, 64, 256), F32),
            tokens(512), tokens(512), tokens(512, F32), tokens(512, F32), tokens(1536),
            tokens(512, F32), tokens(1, F32), tokens(512), tokens(512), tokens(512),
            tokens(512), tokens(512),
            pltpu.VMEM((1, 512), F32),
            tokens(512), tokens(256), tokens(512), tokens(256), tokens(512), tokens(256),
            pltpu.VMEM((64, 1024), BF16),
            pltpu.VMEM((64, 1024), BF16),
            tokens(512), tokens(1536),
            pltpu.VMEM((2, 4, 4, 32, 1024), BF16),
            pltpu.VMEM((2, 4, 4, 16, 1024), BF16),
            tokens(256),
            *[tokens(256) for _ in range(6)],
            pltpu.VMEM((512, 512), BF16),
            pltpu.VMEM((512, 512), BF16),
            tokens(256), tokens(256), tokens(128),
            *reduce_scratch(32, 64),
            *reduce_scratch(16, 32),
            sems((COPIES,)),
            sems((COPIES,)),
            sems((16,)),
        ],
        compiler_params=pltpu.CompilerParams(
            collective_id=0, has_side_effects=True, vmem_limit_bytes=60 * 1024 * 1024
        ),
        name="block_forward_backward",
    )(
        stash_values, scale_exp, cotangent, w_qkv, w_out, w_reduce,
        logit_scale.reshape(1, 16), bias_table.T, rel_index, norm_gain.reshape(1, 512), merge_gain.reshape(1, 1024),
        const(T_BLOCK), const(T_CBLOCK), const(WIN_ORDER), const(ROW_CUT, F32), const(COL_CUT, F32),
        const(T_MERGE), const(T_CMERGE), const(T_BLOCK.T), const(T_MERGE.T), const(T_CBLOCK.T), const(T_CMERGE.T),
        const(COLUMNS_64), const(COLUMNS_16),
        const(same_block(256, 64, 256, 64)), const(same_block(256, 32, 256, 32)), const(same_block(256, 64, 128, 32)),
    )
    return pl.pallas_call(
        hand_on,
        out_shape=outputs,
        in_specs=[vmem] * 5,
        out_specs=(vmem,) * 5,
        name="hand_on",
    )(*results)


def solution(mesh):
    tile = P("wide", "narrow", None)
    rows = P("wide", None)
    both = P("wide", "narrow")
    return jax.shard_map(
        on_device,
        mesh=mesh,
        in_specs=(tile, both, rows, rows, rows, P(), P(), P(), P(), P(), tile),
        out_specs=(tile, tile, both, both, both),
        check_vma=False,
    )
```

```python
import jax
import jax.numpy as jnp
import numpy as np
from jax import lax
from jax.experimental import pallas as pl
from jax.experimental.pallas import tpu as pltpu
from jax.sharding import PartitionSpec as P

MESH = pl.DeviceIdType.MESH
F32 = jnp.float32
BF16 = jnp.bfloat16
NT = (((1,), (1,)), ((), ()))
TN = (((0,), (0,)), ((), ()))


def one_hot(sources):
    sources = np.asarray(sources).reshape(-1)
    table = np.zeros((len(sources), len(sources)), np.float32)
    table[np.arange(len(sources)), sources] = 1.0
    return table


def token_tables():
    i, j, r, c = np.meshgrid(*map(np.arange, (2, 8, 4, 4)), indexing="ij")
    block_from_natural = one_hot((4 * i + r) * 32 + 4 * j + c)
    k, win, mr, mc = np.meshgrid(*map(np.arange, (4, 4, 4, 4)), indexing="ij")
    i, r = mr // 2, 2 * (mr % 2) + k % 2
    j, c = 2 * win + mc // 2, 2 * (mc % 2) + k // 2
    merge_from_block = one_hot((i * 8 + j) * 16 + r * 4 + c)
    i, j, q, m = np.meshgrid(*map(np.arange, (2, 8, 4, 4)), indexing="ij")
    cot_block_from_natural = one_hot(q * 64 + (2 * i + m // 2) * 16 + 2 * j + m % 2)
    q, win, mr, mc = np.meshgrid(*map(np.arange, (4, 4, 4, 4)), indexing="ij")
    i, j, m = mr // 2, 2 * win + mc // 2, (mr % 2) * 2 + mc % 2
    cot_merge_from_block = one_hot((i * 8 + j) * 16 + q * 4 + m)
    return (
        block_from_natural,
        merge_from_block,
        cot_block_from_natural,
        cot_merge_from_block,
    )


def window_tables():
    k, mr, mc = np.meshgrid(*map(np.arange, (4, 4, 4)), indexing="ij")
    row, col = (2 * mr + k % 2).reshape(-1), (2 * mc + k // 2).reshape(-1)
    order = one_hot(row * 8 + col)
    row_cut = (row[:, None] >= 4) != (row[None, :] >= 4)
    col_cut = (col[:, None] >= 4) != (col[None, :] >= 4)
    tiled = lambda cut: np.tile(cut.astype(np.float32), (1, 4))
    return order, tiled(row_cut), tiled(col_cut)


def same_block(rows, row_size, cols, col_size):
    return (
        (np.arange(rows) // row_size)[:, None] == (np.arange(cols) // col_size)[None]
    ).astype(np.float32)


T_BLOCK, T_MERGE, T_CBLOCK, T_CMERGE = token_tables()
COLUMNS_64 = one_hot(np.arange(512).reshape(4, 2, 64).transpose(1, 0, 2)).T
COLUMNS_16 = one_hot(np.arange(512).reshape(16, 2, 16).transpose(1, 0, 2)).T
WIN_ORDER, ROW_CUT, COL_CUT = window_tables()


def const(table, dtype=BF16):
    return jnp.asarray(table, dtype)


class Place:
    def __init__(self):
        wide, narrow = lax.axis_index("wide"), lax.axis_index("narrow")
        self.wide, self.narrow = wide, narrow
        self.core = lax.rem(wide, 2)
        self.zh = lax.rem(lax.div(wide, 2), 4)
        self.x = lax.div(wide, 8)
        self.y = lax.div(narrow, 2)
        self.zl = lax.rem(narrow, 2)
        self.z = 2 * self.zh + self.zl
        self.sibling = (wide + 1 - 2 * self.core, narrow)

    def at_x(self, step):
        return ((lax.rem(self.x + step + 4, 4) * 4 + self.zh) * 2 + self.core, self.narrow)

    def at_y(self, step):
        return (self.wide, lax.rem(self.y + step + 4, 4) * 2 + self.zl)

    def at_z(self, step):
        z = lax.rem(self.z + step + 8, 8)
        return ((self.x * 4 + lax.div(z, 2)) * 2 + self.core, self.y * 2 + lax.rem(z, 2))

    def at_tile(self, rows, cols):
        return (lax.rem(self.wide + rows + 32, 32), lax.rem(self.narrow + cols + 8, 8))


class Sender:
    def __init__(self, send_sem, recv_sem, local_sem):
        self.send_sem, self.recv_sem, self.local_sem = send_sem, recv_sem, local_sem
        self.started, self.count, self.local_count = [], 0, 0

    def remote(self, src, dst, device):
        copy = pltpu.make_async_remote_copy(
            src_ref=src,
            dst_ref=dst,
            send_sem=self.send_sem.at[self.count],
            recv_sem=self.recv_sem.at[self.count],
            device_id=device,
            device_id_type=MESH,
        )
        self.count += 1
        copy.start()
        self.started.append(copy)
        return copy

    def local(self, src, dst):
        copy = pltpu.make_async_copy(src, dst, self.local_sem.at[self.local_count])
        self.local_count += 1
        copy.start()
        return copy

    def drain(self):
        for copy in self.started:
            copy.wait_send()
        self.started = []


def greet(devices):
    barrier = pltpu.get_barrier_semaphore()
    for device in devices:
        pl.semaphore_signal(barrier, inc=1, device_id=device, device_id_type=MESH)


def wait_for(devices):
    pl.semaphore_wait(pltpu.get_barrier_semaphore(), len(devices))


def lanes(start, size):
    return pl.ds(pl.multiple_of(start, 128), size)


def mm(a, b):
    return jnp.dot(a, b, preferred_element_type=F32)


def dg(a, b, dims):
    return lax.dot_general(a, b, dims, preferred_element_type=F32)


def add(*parts):
    total = parts[0].astype(F32)
    for one in parts[1:]:
        total = total + one.astype(F32)
    return total


def split_mm(values, table):
    high = values.astype(BF16)
    low = (values - high.astype(F32)).astype(BF16)
    both = mm(jnp.concatenate([high, low], 0), table)
    return both[: len(values)] + both[len(values) :]


def norm_parts(values):
    centred = values - jnp.mean(values, -1, keepdims=True)
    scale = lax.rsqrt(jnp.mean(centred * centred, -1, keepdims=True) + 1e-05)
    return centred * scale, scale


def norm_back(cot, normed, scale, gain):
    cot = cot * gain
    shared = jnp.mean(cot, -1, keepdims=True) + normed * jnp.mean(cot * normed, -1, keepdims=True)
    return scale * (cot - shared)


EVERY = pl.ds(0, 4)


class Gather:
    def __init__(self, at, go, shard, whole, cut, quarters=False, direct=False):
        self.at, self.go, self.shard, self.whole, self.cut = at, go, shard, whole, cut
        self.quarters, self.direct = quarters, direct
        self.x_left, self.x_right, self.x_far = (lax.rem(at.x + step, 4) for step in (3, 1, 2))
        self.y_left, self.y_right, self.y_far = (lax.rem(at.y + step, 4) for step in (3, 1, 2))
        self.shared = []

    def part(self, xs, zs, y=None):
        y = self.at.y if y is None else y
        return self.whole.at[(xs, zs, self.at.core) + self.cut(y)]

    def move(self, xs, zs, device, y=None):
        ref = self.part(xs, zs, y)
        return self.go.remote(ref, ref, device)

    def share(self, xs, zs, y=None):
        self.shared.append(self.move(xs, zs, self.at.sibling, y))

    def start(self):
        at = self.at
        own, there = self.shard.at[self.cut(at.y)], self.part(at.x, at.zh)
        way = 2 * at.zl - 1
        self.z = [self.go.remote(own, there, at.at_z(way * step)) for step in (1, 2, 3)]
        self.mine = self.go.local(own, there)

    def x1(self):
        at = self.at
        self.mine.wait()
        for copy in self.z:
            copy.wait_recv()
        steps = (1, 2, -1) if self.direct else (1, -1)
        self.x = [self.move(at.x, EVERY, at.at_x(step)) for step in steps]
        if not self.quarters:
            self.share(at.x, EVERY)

    def x2(self):
        at = self.at
        self.x[0].wait_recv()
        far = [self.move(self.x_left, pl.ds(0, 2), at.at_x(1))]
        self.x[1].wait_recv()
        far.append(self.move(self.x_right, pl.ds(2, 2), at.at_x(-1)))
        self.x = far
        if not self.quarters:
            self.share(self.x_left, EVERY)
            self.share(self.x_right, EVERY)

    def x3(self):
        if self.direct and not self.quarters:
            for copy, x in zip(self.x, (self.x_left, self.x_far, self.x_right)):
                copy.wait_recv()
                self.share(x, EVERY)
            return
        for copy in self.x:
            copy.wait_recv()
        if not self.quarters:
            self.share(self.x_far, EVERY)

    def y1(self):
        at = self.at
        self.x3()
        self.y = [self.move(EVERY, EVERY, at.at_y(step)) for step in (1, -1)]
        self.share(EVERY, EVERY)

    def y2(self):
        at = self.at
        self.y[0].wait_recv()
        far = [self.move(pl.ds(0, 2), EVERY, at.at_y(1), self.y_left)]
        self.y[1].wait_recv()
        far.append(self.move(pl.ds(2, 2), EVERY, at.at_y(-1), self.y_right))
        self.y = far
        self.share(EVERY, EVERY, self.y_left)
        self.share(EVERY, EVERY, self.y_right)

    def y3(self):
        for copy in self.y:
            copy.wait_recv()
        self.share(EVERY, EVERY, self.y_far)

    def done(self):
        for copy in self.shared:
            copy.wait_recv()


def y_cut(j):
    return lanes(j * 256, 256)


class Reduce:
    def __init__(self, at, go, m, bx1, bx2, by1, by2, cx, cy, dx, dy, zsend, zland):
        self.at, self.go, self.m = at, go, m
        self.bx1, self.bx2, self.by1, self.by2 = bx1, bx2, by1, by2
        self.cx, self.cy = cx, cy
        self.dx, self.dy = dx, dy
        self.zsend, self.zland = zsend, zland
        self.xs = [lax.rem(at.x + step, 4) for step in (2, 1, 3, 0)]
        self.ys = [lax.rem(at.y + step, 4) for step in (2, 1, 3, 0)]
        self.d = []
        self.x_left, self.x_right = at.at_x(-1), at.at_x(1)
        self.y_left, self.y_right = at.at_y(-1), at.at_y(1)

    def both(self, src, dst, right, left, step):
        if step == 1:
            pairs = ((src(0, pl.ds(0, 2)), right), (src(0, pl.ds(2, 2)), left))
        else:
            pairs = ((src(1, EVERY), right), (src(2, EVERY), left))
        return [self.go.remote(ref, dst.at[n], device) for n, (ref, device) in enumerate(pairs)]

    def x_src(self, n, part):
        return self.m.at[0, self.xs[n], part]

    def y_src(self, n, part):
        return self.m.at[1, part, :, :, y_cut(self.ys[n])]

    def first_x(self):
        self.b_x = self.both(self.x_src, self.bx1, self.x_right, self.x_left, 1)

    def first_y(self):
        self.b_y = self.both(self.y_src, self.by1, self.y_right, self.y_left, 1)

    def second_x(self):
        m, xs = self.m, self.xs
        for copy in self.b_x:
            copy.wait_recv()
        for s in range(2):
            m[0, xs[1], s] = add(m[0, xs[1], s], self.bx1[0, s]).astype(BF16)
            m[0, xs[2], 2 + s] = add(m[0, xs[2], 2 + s], self.bx1[1, s]).astype(BF16)
        self.b_x = self.both(self.x_src, self.bx2, self.x_right, self.x_left, 2)

    def second_y(self):
        m, ys = self.m, self.ys
        for copy in self.b_y:
            copy.wait_recv()
        for s in range(2):
            cut = y_cut(ys[1])
            m[1, s, :, :, cut] = add(m[1, s, :, :, cut], self.by1[0, s]).astype(BF16)
            cut = y_cut(ys[2])
            m[1, 2 + s, :, :, cut] = add(m[1, 2 + s, :, :, cut], self.by1[1, s]).astype(BF16)
        self.b_y = self.both(self.y_src, self.by2, self.y_right, self.y_left, 2)

    def third_x(self):
        at = self.at
        for copy in self.b_x:
            copy.wait_recv()
        for s in range(4):
            self.cx[s] = add(self.m[0, at.x, s], self.bx2[0, s], self.bx2[1, s]).astype(BF16)
        for n, step in ((0, 2), (1, 1), (2, 3)):
            src = self.cx.at[:, :, y_cut(self.ys[n])]
            self.d.append(self.go.remote(src, self.dx.at[n], at.at_y(step)))

    def third_y(self):
        at = self.at
        for copy in self.b_y:
            copy.wait_recv()
        for s in range(4):
            self.cy[s] = add(self.m[1, s, :, :, y_cut(at.y)], self.by2[0, s], self.by2[1, s]).astype(BF16)
        for n, step in ((0, 2), (1, 1), (2, 3)):
            self.d.append(self.go.remote(self.cy.at[self.xs[n]], self.dy.at[n], at.at_x(step)))

    def fourth(self, pack):
        for copy in self.d:
            copy.wait_recv()
        for h in range(4):
            a = add(self.cx[h, :, y_cut(self.at.y)], *[self.dx[n, h] for n in range(3)])
            b = add(self.cy[self.at.x, h], *[self.dy[n, h] for n in range(3)])
            for low in range(2):
                self.zsend[h, low] = pack(a, b, low).astype(BF16)
        self.last = []
        for step in range(1, 8):
            z = lax.rem(self.at.z + step, 8)
            src = self.zsend.at[lax.div(z, 2), lax.rem(z, 2)]
            self.last.append(self.go.remote(src, self.zland.at[step - 1], self.at.at_z(step)))

    def fifth(self):
        total = self.zsend[self.at.zh, self.at.zl].astype(F32)
        for step in range(7):
            self.last[step].wait_recv()
            total = total + self.zland[step].astype(F32)
        return total


def pack_reduce(a, b, low):
    cut = slice(128 * low, 128 * low + 128)
    return jnp.concatenate([a[:, cut], b[:, cut]], 0)


def pack_qkv_out(a, b, low):
    if low == 0:
        rows = a[:, 0:128], jnp.concatenate([a[:, 128:192], b[:, 128:192]], 1)
    else:
        rows = (
            jnp.concatenate([a[:, 192:256], b[:, 0:64]], 1),
            jnp.concatenate([b[:, 64:128], b[:, 192:256]], 1),
        )
    return jnp.concatenate(rows, 0)


def reduce_scratch(rows, z_rows):
    return [
        pltpu.VMEM((2, 2, rows, 1024), BF16),
        pltpu.VMEM((2, 4, rows, 1024), BF16),
        pltpu.VMEM((2, 2, 4, rows, 256), BF16),
        pltpu.VMEM((2, 4, 4, rows, 256), BF16),
        pltpu.VMEM((4, rows, 1024), BF16),
        pltpu.VMEM((4, 4, rows, 256), BF16),
        pltpu.VMEM((3, 4, rows, 256), BF16),
        pltpu.VMEM((3, 4, rows, 256), BF16),
        pltpu.VMEM((4, 2, z_rows, 128), BF16),
        pltpu.VMEM((7, z_rows, 128), BF16),
    ]


COPIES = 12 + 18 + 3 * 11 + 15 + 8 + 2 * (8 + 6 + 7) + 16


def block_kernel(
    wq_ref, wo_ref, wr_ref, *rest,
):
    loads, rest = rest[:24], rest[24:]
    (
    merged_ref, gin_ref, gq_ref, go_ref, gr_ref,
    blk, land, back, oland, ocland, wq, wo, wr,
    x_tok, cot_tok, qkv, qs, kh, rq, rk, probs, bias, bias_rows, table, mask, att, d_att, dqs, dkh, dqkv,
    xhat, xscale, ro, dproj, dtok, xt, at_t, ls_row, ro_cols, ro_theirs, x_cols, x_theirs, at_cols, at_theirs,
    dred, dred_theirs, dproj_theirs, dqkv_theirs, fa, fb, mb,
    *rest,
    ) = rest
    held, rest = rest[:24], rest[24:]
    (
        stash_ref, exp_ref, t_block_ref, cot_ref, t_cblock_ref,
        table_ref, rel_ref, order_ref, row_cut_ref, col_cut_ref, ls_ref,
        ng_ref, mg_ref, t_merge_ref, t_cmerge_ref, t_unblock_ref, t_unmerge_ref, t_cunblock_ref, t_cunmerge_ref,
        columns_ref, columns_16_ref, bd64_ref, bd32_ref, heads_ref,
    ) = held
    a_bufs, b_bufs, (send_sem, recv_sem, local_sem) = rest[0:10], rest[10:20], rest[20:]
    go = Sender(send_sem, recv_sem, local_sem)
    at = Place()
    c = at.core
    partners = (
        [at.sibling]
        + [at.at_x(step) for step in (1, 2, 3)]
        + [at.at_y(step) for step in (1, 2, 3)]
        + [at.at_z(step) for step in range(1, 8)]
        + [at.at_tile(*step) for step in ((-1, 0), (0, -1), (-1, -1), (1, 0), (0, 1), (1, 1))]
    )
    greet(partners)
    arrivals = [go.local(src, dst) for src, dst in zip(loads, held)]

    def loaded(first, last):
        for copy in arrivals[first:last]:
            copy.wait()

    wait_for(partners)
    all_rows = pl.ds(0, 16)
    q_y = Gather(at, go, wq_ref, wq, lambda y: (all_rows, lanes(512 + 256 * y, 256)), True, True)
    q_x = Gather(at, go, wq_ref, wq, lambda y: (all_rows, pl.ds(0, 512)), False, True)
    o_x = Gather(at, go, wo_ref, wo, lambda y: (all_rows, pl.ds(0, 512)))
    r_x = Gather(at, go, wr_ref, wr, lambda y: (pl.ds(0, 64), pl.ds(0, 512)))
    r_y = Gather(at, go, wr_ref, wr, lambda y: (pl.ds(pl.multiple_of(16 * y, 16), 16), pl.ds(512, 512)), True)

    q_y.start()
    r_y.start()
    q_x.start()

    loaded(0, 5)
    factor_of = exp_ref[...]
    factor_of = jnp.where(factor_of == -8, 2.0**-8, jnp.where(factor_of == -7, 2.0**-7, 2.0**-6))
    in_window = lax.broadcasted_iota(jnp.int32, (32, 512), 0) // 8
    factor = jnp.zeros((32, 512), F32)
    for w in range(4):
        factor = jnp.where(in_window == w, factor_of[:, w : w + 1], factor)
    inputs = stash_ref[...].astype(F32) * factor[None]
    blk[:, 0:512] = mm(t_block_ref[...], inputs.reshape(256, 512).astype(BF16)).astype(BF16)
    r_x.start()
    q_y.x1()
    r_y.x1()
    o_x.start()
    q_x.x1()
    cot = cot_ref[...].astype(F32).reshape(64, 1024).astype(BF16)
    cot = jnp.concatenate([cot[:, 256 * q : 256 * q + 256] for q in range(4)], 0)
    blk[:, 512:768] = mm(t_cblock_ref[...], cot).astype(BF16)
    q_y.y1()
    halo = [
        go.remote(blk.at[pl.ds(16, 112)], land.at[pl.ds(128, 112)], at.at_tile(-1, 0)),
        go.remote(blk.at[pl.ds(128, 16)], land.at[pl.ds(112, 16)], at.at_tile(0, -1)),
        go.remote(blk.at[pl.ds(0, 16)], land.at[pl.ds(240, 16)], at.at_tile(-1, -1)),
    ]
    r_y.x2()

    loaded(5, 11)
    table[...] = jnp.zeros((16, 256), F32)
    table[:, 0:225] = 16.0 * jax.nn.sigmoid(table_ref[...])
    by_head = table[...]
    high = by_head.astype(BF16)
    low = (by_head - high.astype(F32)).astype(BF16)
    both = jnp.concatenate([high, low], 0)
    rel = mm(order_ref[...], rel_ref[...].astype(F32).astype(BF16)).astype(BF16)
    rel = dg(rel, order_ref[...], NT).astype(jnp.int32)
    rel = jnp.concatenate([rel[16 * j : 16 * j + 16] for j in range(4)], 1)
    entry = lax.broadcasted_iota(jnp.int32, (256, 256), 0)

    def bias_of(rows):
        for a in rows:
            chosen = jnp.where(entry == rel[a : a + 1], 1.0, 0.0).astype(BF16)
            got = mm(both, chosen)
            got = got[0:16] + got[16:32]
            for j in range(4):
                bias_rows[16 * j + a] = got[:, 64 * j : 64 * j + 64]

    bias_of(range(0, 5))
    r_x.x1()
    bias_of(range(5, 10))
    q_y.y2()
    r_y.y1()
    bias_of(range(10, 16))
    o_x.x1()
    q_x.x3()
    for g in range(4):
        bias[g] = jnp.concatenate([bias_rows[:, 4 * g + h, :] for h in range(4)], 1)
    last_rows = (at.wide == 31).astype(F32)
    last_cols = (at.narrow == 7).astype(F32)
    mask[0] = row_cut_ref[...] * last_rows * -100.0
    mask[1] = jnp.maximum(row_cut_ref[...] * last_rows, col_cut_ref[...] * last_cols) * -100.0
    lane = lax.broadcasted_iota(jnp.int32, (1, 512), 1) // 32
    scales = jnp.zeros((1, 512), F32)
    for h in range(16):
        scales = jnp.where(lane == h, ls_ref[:, h : h + 1], scales)
    ls_row[...] = scales


    q_y.y3()
    q_x.done()

    for copy in halo:
        copy.wait_recv()
    r_x.x2()
    loaded(11, 24)
    q_y.done()
    land[pl.ds(0, 112)] = blk[pl.ds(144, 112)]
    x_tok[...] = mm(t_merge_ref[...], land[:, 0:512]).astype(BF16)
    cot = mm(t_cmerge_ref[...], land[:, 512:768]).astype(BF16)
    cot_tok[...] = jnp.concatenate([cot[64 * q : 64 * q + 64] for q in range(4)], 1)
    r_y.y2()
    o_x.x2()
    x_cols[...] = mm(x_tok[...], columns_16_ref[...]).astype(BF16)
    not_mine = lanes(256 * (1 - c), 256)
    mine = lanes(256 * c, 256)
    x_swap = go.remote(x_cols.at[:, not_mine], x_theirs, at.sibling)

    qkv[...] = mm(x_tok[...], wq[...].reshape(512, 1536)).astype(BF16)
    r_x.x3()
    for start, inverse, unit in ((0, rq, qs), (512, rk, kh)):
        for n in range(2):
            cut = slice(256 * n, 256 * n + 256)
            for row in range(0, 256, 128):
                rows = slice(row, row + 128)
                raw = qkv[rows, start + 256 * n : start + 256 * n + 256].astype(F32)
                inv = lax.rsqrt(jnp.maximum(split_mm(raw * raw, bd32_ref[...]), 1e-24))
                inverse[rows, cut] = inv
                raw = raw * inv
                if start == 0:
                    raw = raw * ls_row[:, cut]
                unit[rows, cut] = raw.astype(BF16)
    x_swap.wait_recv()
    xt[:, 0:256] = x_cols[:, mine].T
    xt[:, 256:512] = x_theirs[...].T

    def window(ref, win, cut):
        return jnp.concatenate([ref[pl.ds(64 * k + 16 * win, 16), cut] for k in range(4)], 0)

    def put_window(ref, win, cut, values):
        for k in range(4):
            ref[pl.ds(64 * k + 16 * win, 16), cut] = values[16 * k : 16 * k + 16]

    def spread(rows):
        return jnp.concatenate([rows] * 4, 0) * heads_ref[...]

    def fold(values):
        values = values * heads_ref[...].astype(F32)
        return (values[0:64] + values[64:128]) + (values[128:192] + values[192:256])

    def forward(g):
        cut = slice(g * 128, g * 128 + 128)
        v_cut = slice(g * 128 + 1024, g * 128 + 1152)
        weights = []
        for win in range(4):
            scores = dg(window(qs, win, cut), spread(window(kh, win, cut)), NT)
            weights.append(jnp.exp(scores + bias[g] + mask[1 if win == 3 else 0]))
        totals = split_mm(jnp.concatenate(weights, 0), bd64_ref[...])
        for win in range(4):
            p = weights[win] / totals[64 * win : 64 * win + 64]
            probs[g, win] = p
            values = spread(window(qkv, win, v_cut))
            put_window(att, win, cut, mm(p.astype(BF16), values).astype(BF16))

    forward(0)
    forward(1)
    o_x.x3()
    r_y.y3()
    forward(2)
    forward(3)
    r_x.done()
    at_cols[...] = mm(att[...], columns_16_ref[...]).astype(BF16)
    at_swap = go.remote(at_cols.at[:, not_mine], at_theirs, at.sibling)
    o_x.done()
    xhat[...] = mm(att[...], wo[...].reshape(512, 512))
    for row in range(0, 256, 64):
        rows = slice(row, row + 64)
        normed, scale = norm_parts(xhat[rows])
        xhat[rows] = normed
        xscale[rows] = scale
        ro[rows] = (x_tok[rows].astype(F32) + normed * ng_ref[...]).astype(BF16)
    ro_cols[...] = mm(ro[...], columns_ref[...]).astype(BF16)
    swap = [go.remote(ro_cols.at[:, not_mine], ro_theirs, at.sibling)]
    r_y.done()

    reduced = jnp.zeros((64, 1024), F32)
    for k in range(4):
        reduced += mm(ro[64 * k : 64 * k + 64], wr[k].reshape(512, 1024))
    normed, scale = norm_parts(reduced)
    dred[...] = norm_back(cot_tok[...].astype(F32), normed, scale, mg_ref[...]).astype(BF16)
    swap.append(go.remote(dred, dred_theirs, at.sibling))
    merged = (normed * mg_ref[...]).astype(BF16)
    merged = jnp.concatenate([merged[:, 256 * q : 256 * q + 256] for q in range(4)], 0)
    mb[...] = mm(t_cunmerge_ref[...], merged).astype(BF16)

    def send_back(tile, landing):
        return [
            go.remote(tile.at[pl.ds(128, 112)], landing.at[pl.ds(16, 112)], at.at_tile(1, 0)),
            go.remote(tile.at[pl.ds(112, 16)], landing.at[pl.ds(128, 16)], at.at_tile(0, 1)),
            go.remote(tile.at[pl.ds(240, 16)], landing.at[pl.ds(0, 16)], at.at_tile(1, 1)),
        ]

    for k in range(4):
        dtok[64 * k : 64 * k + 64] = dg(dred[...], wr[k].reshape(512, 1024), NT).astype(BF16)

    for copy in swap:
        copy.wait_recv()
    a_sum = Reduce(at, go, fa, *a_bufs)
    grads = jnp.concatenate([dred[...], dred_theirs[...]], 0)
    for n in range(4):
        k = a_sum.xs[n]
        rows = pl.ds(pl.multiple_of(64 * k, 64), 64)
        tokens = jnp.concatenate([ro_cols[rows, mine], ro_theirs[rows]], 0).T
        for cut in (slice(0, 512), slice(512, 1024)):
            got = mm(tokens, grads[:, cut]).astype(BF16).reshape(4, 64, 512)
            fa[0, k, :, :, cut] = got[:, 0:32]
            fa[1, k, :, :, cut] = got[:, 32:64]
        if n == 0:
            a_sum.first_x()
    a_sum.first_y()

    for row in range(0, 256, 64):
        rows = slice(row, row + 64)
        got = norm_back(dtok[rows].astype(F32), xhat[rows], xscale[rows], ng_ref[...])
        dproj[rows] = got.astype(BF16)
    dproj_swap = go.remote(dproj, dproj_theirs, at.sibling)
    d_att[...] = dg(dproj[...], wo[...].reshape(512, 512), NT).astype(BF16)

    def backward(g):
        cut = slice(g * 128, g * 128 + 128)
        v_cut = slice(g * 128 + 1024, g * 128 + 1152)
        dps = []
        for win in range(4):
            dp = dg(window(d_att, win, cut), spread(window(qkv, win, v_cut)), NT)
            dps.append(dp.astype(BF16).astype(F32))
        alike = split_mm(jnp.concatenate([probs[g, win] * dps[win] for win in range(4)], 0), bd64_ref[...])
        for win in range(4):
            p = probs[g, win]
            ds = (p * (dps[win] - alike[64 * win : 64 * win + 64])).astype(BF16)
            put_window(dqs, win, cut, mm(ds, spread(window(kh, win, cut))))
            put_window(dkh, win, cut, fold(dg(ds, window(qs, win, cut), TN)))
            put_window(dqkv, win, v_cut, fold(dg(p.astype(BF16), window(d_att, win, cut), TN)).astype(BF16))

    for g in range(4):
        backward(g)

    def swap_dqkv(start):
        cut = pl.ds(start, 512)
        return go.remote(dqkv.at[:, cut], dqkv_theirs.at[:, cut], at.sibling)

    dqkv_swap = [swap_dqkv(1024)]
    a_sum.second_x()
    a_sum.second_y()
    for start, inverse, grad in ((0, rq, dqs), (512, rk, dkh)):
        for n in range(2):
            cut = slice(256 * n, 256 * n + 256)
            both_cut = slice(start + 256 * n, start + 256 * n + 256)
            for row in range(0, 256, 128):
                rows = slice(row, row + 128)
                inv = inverse[rows, cut]
                unit = qkv[rows, both_cut].astype(F32) * inv
                d_unit = grad[rows, cut]
                if start == 0:
                    d_unit = d_unit * ls_row[:, cut]
                along = split_mm(unit * d_unit, bd32_ref[...])
                along = jnp.where(inv < 1e12, along, 0.0)
                dqkv[rows, both_cut] = (inv * (d_unit - unit * along)).astype(BF16)
        dqkv_swap.append(swap_dqkv(start))
    at_swap.wait_recv()
    at_t[:, 0:256] = at_cols[:, mine].T
    at_t[:, 256:512] = at_theirs[...].T
    dproj_swap.wait_recv()
    d_out = jnp.concatenate([dproj[...], dproj_theirs[...]], 0)
    out = mm(at_t[...], d_out).astype(BF16)
    for y in range(4):
        fb[1, :, :, :, 256 * y + 128 : 256 * y + 256] = out[:, 128 * y : 128 * y + 128].reshape(4, 4, 16, 128)

    merged_back = send_back(mb, ocland)
    d_in = dtok[...].astype(F32) + dg(dqkv[...], wq[...].reshape(512, 1536), NT)
    back[...] = mm(t_unmerge_ref[...], d_in.astype(BF16)).astype(BF16)
    grad_back = send_back(back, oland)

    for copy in dqkv_swap:
        copy.wait_recv()
    b_sum = Reduce(at, go, fb, *b_bufs)
    for n in range(4):
        y = b_sum.ys[n]
        cut = lanes(384 * y, 384)
        grads = jnp.concatenate([dqkv[:, cut], dqkv_theirs[:, cut]], 0)
        got = mm(xt[...], grads).astype(BF16)
        fb[0, :, :, :, y_cut(y)] = got[:, 0:256].reshape(4, 4, 16, 256)
        fb[1, :, :, :, lanes(256 * y, 128)] = got[:, 256:384].reshape(4, 4, 16, 128)
    b_sum.first_x()
    b_sum.first_y()
    a_sum.third_x()
    a_sum.third_y()
    b_sum.second_y()
    b_sum.second_x()
    a_sum.fourth(pack_reduce)
    b_sum.third_y()
    b_sum.third_x()
    b_sum.fourth(pack_qkv_out)
    for copy in merged_back + grad_back:
        copy.wait_recv()
    oland[pl.ds(144, 112)] = back[pl.ds(0, 112)]
    ocland[pl.ds(144, 112)] = mb[pl.ds(0, 112)]
    gin_ref[...] = mm(t_unblock_ref[...], oland[...]).astype(BF16).reshape(8, 32, 512)
    got = mm(t_cunblock_ref[...], ocland[...]).astype(BF16)
    for q in range(4):
        merged_ref[:, :, 256 * q : 256 * q + 256] = got[64 * q : 64 * q + 64].reshape(4, 16, 256)
    factor = 1.0 / 256.0
    gr_ref[...] = a_sum.fifth() * factor
    go.drain()
    total = b_sum.fifth() * factor
    gq_ref[:, 0:128] = total[0:16]
    gq_ref[:, 128:192] = total[16:32, 0:64]
    go_ref[...] = total[16:32, 64:128]


def hand_on(*refs):
    for src, dst in zip(refs[:5], refs[5:]):
        dst[...] = src[...]


def on_device(
    stash_values, scale_exp, w_qkv, w_out, w_reduce, logit_scale, bias_table, rel_index, norm_gain, merge_gain, cotangent
):
    vmem = pl.BlockSpec(memory_space=pltpu.VMEM)
    sems = pltpu.SemaphoreType.DMA
    outputs = (
        jax.ShapeDtypeStruct((4, 16, 1024), BF16),
        jax.ShapeDtypeStruct((8, 32, 512), BF16),
        jax.ShapeDtypeStruct((16, 192), F32),
        jax.ShapeDtypeStruct((16, 64), F32),
        jax.ShapeDtypeStruct((64, 128), F32),
    )
    loads = (
        stash_values, scale_exp, const(T_BLOCK), cotangent, const(T_CBLOCK),
        bias_table.T, rel_index, const(WIN_ORDER), const(ROW_CUT, F32), const(COL_CUT, F32), logit_scale.reshape(1, 16),
        norm_gain.reshape(1, 512), merge_gain.reshape(1, 1024),
        const(T_MERGE), const(T_CMERGE), const(T_BLOCK.T), const(T_MERGE.T), const(T_CBLOCK.T), const(T_CMERGE.T),
        const(COLUMNS_64), const(COLUMNS_16),
        const(same_block(256, 64, 256, 64)), const(same_block(256, 32, 256, 32)), const(same_block(256, 64, 128, 32)),
    )
    tokens = lambda width, kind=BF16: pltpu.VMEM((256, width), kind)
    results = pl.pallas_call(
        block_kernel,
        out_shape=outputs,
        in_specs=[pl.BlockSpec(memory_space=pl.ANY)] * 27,
        out_specs=(vmem,) * 5,
        scratch_shapes=[
            tokens(768), tokens(768), tokens(512), tokens(512), tokens(256),
            pltpu.VMEM((4, 4, 2, 16, 1536), BF16),
            pltpu.VMEM((4, 4, 2, 16, 512), BF16),
            pltpu.VMEM((4, 4, 2, 64, 1024), BF16),
            tokens(512),
            pltpu.VMEM((64, 1024), BF16),
            tokens(1536), tokens(512), tokens(512), tokens(512, F32), tokens(512, F32),
            pltpu.VMEM((4, 4, 64, 256), F32),
            pltpu.VMEM((4, 64, 256), F32),
            pltpu.VMEM((64, 16, 64), F32),
            pltpu.VMEM((16, 256), F32),
            pltpu.VMEM((2, 64, 256), F32),
            tokens(512), tokens(512), tokens(512, F32), tokens(512, F32), tokens(1536),
            tokens(512, F32), tokens(1, F32), tokens(512), tokens(512), tokens(512),
            tokens(512), tokens(512),
            pltpu.VMEM((1, 512), F32),
            tokens(512), tokens(256), tokens(512), tokens(256), tokens(512), tokens(256),
            pltpu.VMEM((64, 1024), BF16),
            pltpu.VMEM((64, 1024), BF16),
            tokens(512), tokens(1536),
            pltpu.VMEM((2, 4, 4, 32, 1024), BF16),
            pltpu.VMEM((2, 4, 4, 16, 1024), BF16),
            tokens(256),
            *[pltpu.VMEM(load.shape, load.dtype) for load in loads],
            *reduce_scratch(32, 64),
            *reduce_scratch(16, 32),
            sems((COPIES,)),
            sems((COPIES,)),
            sems((32,)),
        ],
        compiler_params=pltpu.CompilerParams(
            collective_id=0, has_side_effects=True, vmem_limit_bytes=60 * 1024 * 1024
        ),
        name="block_forward_backward",
    )(w_qkv, w_out, w_reduce, *loads)
    return pl.pallas_call(
        hand_on,
        out_shape=outputs,
        in_specs=[vmem] * 5,
        out_specs=(vmem,) * 5,
        name="hand_on",
    )(*results)


def solution(mesh):
    tile = P("wide", "narrow", None)
    rows = P("wide", None)
    both = P("wide", "narrow")
    return jax.shard_map(
        on_device,
        mesh=mesh,
        in_specs=(tile, both, rows, rows, rows, P(), P(), P(), P(), P(), tile),
        out_specs=(tile, tile, both, both, both),
        check_vma=False,
    )
```

```python
import jax
import jax.numpy as jnp
import numpy as np
from jax import lax
from jax.experimental import pallas as pl
from jax.experimental.pallas import tpu as pltpu
from jax.sharding import PartitionSpec as P

MESH = pl.DeviceIdType.MESH
F32 = jnp.float32
BF16 = jnp.bfloat16
NT = (((1,), (1,)), ((), ()))
TN = (((0,), (0,)), ((), ()))


def one_hot(sources):
    sources = np.asarray(sources).reshape(-1)
    table = np.zeros((len(sources), len(sources)), np.float32)
    table[np.arange(len(sources)), sources] = 1.0
    return table


def token_tables():
    i, j, r, c = np.meshgrid(*map(np.arange, (2, 8, 4, 4)), indexing="ij")
    block_from_natural = one_hot((4 * i + r) * 32 + 4 * j + c)
    k, win, mr, mc = np.meshgrid(*map(np.arange, (4, 4, 4, 4)), indexing="ij")
    i, r = mr // 2, 2 * (mr % 2) + k % 2
    j, c = 2 * win + mc // 2, 2 * (mc % 2) + k // 2
    merge_from_block = one_hot((i * 8 + j) * 16 + r * 4 + c)
    i, j, q, m = np.meshgrid(*map(np.arange, (2, 8, 4, 4)), indexing="ij")
    cot_block_from_natural = one_hot(q * 64 + (2 * i + m // 2) * 16 + 2 * j + m % 2)
    q, win, mr, mc = np.meshgrid(*map(np.arange, (4, 4, 4, 4)), indexing="ij")
    i, j, m = mr // 2, 2 * win + mc // 2, (mr % 2) * 2 + mc % 2
    cot_merge_from_block = one_hot((i * 8 + j) * 16 + q * 4 + m)
    return (
        block_from_natural,
        merge_from_block,
        cot_block_from_natural,
        cot_merge_from_block,
    )


def window_tables():
    k, mr, mc = np.meshgrid(*map(np.arange, (4, 4, 4)), indexing="ij")
    row, col = (2 * mr + k % 2).reshape(-1), (2 * mc + k // 2).reshape(-1)
    order = one_hot(row * 8 + col)
    row_cut = (row[:, None] >= 4) != (row[None, :] >= 4)
    col_cut = (col[:, None] >= 4) != (col[None, :] >= 4)
    tiled = lambda cut: np.tile(cut.astype(np.float32), (1, 4))
    return order, tiled(row_cut), tiled(col_cut)


def same_block(rows, row_size, cols, col_size):
    return (
        (np.arange(rows) // row_size)[:, None] == (np.arange(cols) // col_size)[None]
    ).astype(np.float32)


T_BLOCK, T_MERGE, T_CBLOCK, T_CMERGE = token_tables()
COLUMNS_64 = one_hot(np.arange(512).reshape(4, 2, 64).transpose(1, 0, 2)).T
COLUMNS_16 = one_hot(np.arange(512).reshape(16, 2, 16).transpose(1, 0, 2)).T
WIN_ORDER, ROW_CUT, COL_CUT = window_tables()


def const(table, dtype=BF16):
    return jnp.asarray(table, dtype)


class Place:
    def __init__(self):
        wide, narrow = lax.axis_index("wide"), lax.axis_index("narrow")
        self.wide, self.narrow = wide, narrow
        self.core = lax.rem(wide, 2)
        self.zh = lax.rem(lax.div(wide, 2), 4)
        self.x = lax.div(wide, 8)
        self.y = lax.div(narrow, 2)
        self.zl = lax.rem(narrow, 2)
        self.z = 2 * self.zh + self.zl
        self.sibling = (wide + 1 - 2 * self.core, narrow)

    def at_x(self, step):
        return ((lax.rem(self.x + step + 4, 4) * 4 + self.zh) * 2 + self.core, self.narrow)

    def at_y(self, step):
        return (self.wide, lax.rem(self.y + step + 4, 4) * 2 + self.zl)

    def at_z(self, step):
        z = lax.rem(self.z + step + 8, 8)
        return ((self.x * 4 + lax.div(z, 2)) * 2 + self.core, self.y * 2 + lax.rem(z, 2))

    def at_tile(self, rows, cols):
        return (lax.rem(self.wide + rows + 32, 32), lax.rem(self.narrow + cols + 8, 8))


class Sender:
    def __init__(self, send_sem, recv_sem, local_sem):
        self.send_sem, self.recv_sem, self.local_sem = send_sem, recv_sem, local_sem
        self.started, self.count, self.local_count, self.drained = [], 0, 0, 0

    def remote(self, src, dst, device):
        copy = pltpu.make_async_remote_copy(
            src_ref=src,
            dst_ref=dst,
            send_sem=self.send_sem.at[self.count],
            recv_sem=self.recv_sem.at[self.count],
            device_id=device,
            device_id_type=MESH,
        )
        self.count += 1
        copy.start()
        self.started.append(copy)
        return copy

    def local(self, src, dst):
        copy = pltpu.make_async_copy(src, dst, self.local_sem.at[self.local_count])
        self.local_count += 1
        copy.start()
        return copy

    def drain(self, until=None):
        until = self.count if until is None else until
        for copy in self.started[self.drained : until]:
            copy.wait_send()
        self.drained = until


def greet(devices):
    barrier = pltpu.get_barrier_semaphore()
    for device in devices:
        pl.semaphore_signal(barrier, inc=1, device_id=device, device_id_type=MESH)


def wait_for(devices):
    pl.semaphore_wait(pltpu.get_barrier_semaphore(), len(devices))


def lanes(start, size):
    return pl.ds(pl.multiple_of(start, 128), size)


def mm(a, b):
    return jnp.dot(a, b, preferred_element_type=F32)


def dg(a, b, dims):
    return lax.dot_general(a, b, dims, preferred_element_type=F32)


def add(*parts):
    total = parts[0].astype(F32)
    for one in parts[1:]:
        total = total + one.astype(F32)
    return total


def split_mm(values, table):
    high = values.astype(BF16)
    low = (values - high.astype(F32)).astype(BF16)
    both = mm(jnp.concatenate([high, low], 0), table)
    return both[: len(values)] + both[len(values) :]


def norm_parts(values):
    centred = values - jnp.mean(values, -1, keepdims=True)
    scale = lax.rsqrt(jnp.mean(centred * centred, -1, keepdims=True) + 1e-05)
    return centred * scale, scale


def norm_back(cot, normed, scale, gain):
    cot = cot * gain
    shared = jnp.mean(cot, -1, keepdims=True) + normed * jnp.mean(cot * normed, -1, keepdims=True)
    return scale * (cot - shared)


EVERY = pl.ds(0, 4)


class Gather:
    def __init__(self, at, go, shard, whole, cut, quarters=False, direct=False):
        self.at, self.go, self.shard, self.whole, self.cut = at, go, shard, whole, cut
        self.quarters, self.direct = quarters, direct
        self.x_left, self.x_right, self.x_far = (lax.rem(at.x + step, 4) for step in (3, 1, 2))
        self.y_left, self.y_right, self.y_far = (lax.rem(at.y + step, 4) for step in (3, 1, 2))
        self.shared = []

    def part(self, xs, zs, y=None):
        y = self.at.y if y is None else y
        return self.whole.at[(xs, zs, self.at.core) + self.cut(y)]

    def move(self, xs, zs, device, y=None):
        ref = self.part(xs, zs, y)
        return self.go.remote(ref, ref, device)

    def share(self, xs, zs, y=None):
        self.shared.append(self.move(xs, zs, self.at.sibling, y))

    def start(self):
        at = self.at
        own, there = self.shard.at[self.cut(at.y)], self.part(at.x, at.zh)
        way = 2 * at.zl - 1
        self.z = [self.go.remote(own, there, at.at_z(way * step)) for step in (1, 2, 3)]
        self.mine = self.go.local(own, there)

    def x1(self):
        at = self.at
        self.mine.wait()
        for copy in self.z:
            copy.wait_recv()
        steps = (1, 2, -1) if self.direct else (1, -1)
        self.x = [self.move(at.x, EVERY, at.at_x(step)) for step in steps]
        if not self.quarters:
            self.share(at.x, EVERY)

    def x2(self):
        at = self.at
        self.x[0].wait_recv()
        far = [self.move(self.x_left, pl.ds(0, 2), at.at_x(1))]
        self.x[1].wait_recv()
        far.append(self.move(self.x_right, pl.ds(2, 2), at.at_x(-1)))
        self.x = far
        if not self.quarters:
            self.share(self.x_left, EVERY)
            self.share(self.x_right, EVERY)

    def x3(self):
        if self.direct and not self.quarters:
            for copy, x in zip(self.x, (self.x_left, self.x_far, self.x_right)):
                copy.wait_recv()
                self.share(x, EVERY)
            return
        for copy in self.x:
            copy.wait_recv()
        if not self.quarters:
            self.share(self.x_far, EVERY)

    def y1(self):
        at = self.at
        self.x3()
        self.y = [self.move(EVERY, EVERY, at.at_y(step)) for step in (1, -1)]
        self.share(EVERY, EVERY)

    def y2(self):
        at = self.at
        self.y[0].wait_recv()
        far = [self.move(pl.ds(0, 2), EVERY, at.at_y(1), self.y_left)]
        self.y[1].wait_recv()
        far.append(self.move(pl.ds(2, 2), EVERY, at.at_y(-1), self.y_right))
        self.y = far
        self.share(EVERY, EVERY, self.y_left)
        self.share(EVERY, EVERY, self.y_right)

    def y3(self):
        for copy in self.y:
            copy.wait_recv()
        self.share(EVERY, EVERY, self.y_far)

    def done(self):
        for copy in self.shared:
            copy.wait_recv()


def y_cut(j):
    return lanes(j * 256, 256)


class Reduce:
    def __init__(self, at, go, m, bx1, bx2, by1, by2, cx, cy, dx, dy, zsend, zland):
        self.at, self.go, self.m = at, go, m
        self.bx1, self.bx2, self.by1, self.by2 = bx1, bx2, by1, by2
        self.cx, self.cy = cx, cy
        self.dx, self.dy = dx, dy
        self.zsend, self.zland = zsend, zland
        self.xs = [lax.rem(at.x + step, 4) for step in (2, 1, 3, 0)]
        self.ys = [lax.rem(at.y + step, 4) for step in (2, 1, 3, 0)]
        self.d = []
        self.x_left, self.x_right = at.at_x(-1), at.at_x(1)
        self.y_left, self.y_right = at.at_y(-1), at.at_y(1)

    def both(self, src, dst, right, left, step):
        if step == 1:
            pairs = ((src(0, pl.ds(0, 2)), right), (src(0, pl.ds(2, 2)), left))
        else:
            pairs = ((src(1, EVERY), right), (src(2, EVERY), left))
        return [self.go.remote(ref, dst.at[n], device) for n, (ref, device) in enumerate(pairs)]

    def x_src(self, n, part):
        return self.m.at[0, self.xs[n], part]

    def y_src(self, n, part):
        return self.m.at[1, part, :, :, y_cut(self.ys[n])]

    def first_x(self):
        self.b_x = self.both(self.x_src, self.bx1, self.x_right, self.x_left, 1)

    def first_y(self):
        self.b_y = self.both(self.y_src, self.by1, self.y_right, self.y_left, 1)

    def second_x(self):
        m, xs = self.m, self.xs
        for copy in self.b_x:
            copy.wait_recv()
        for s in range(2):
            m[0, xs[1], s] = add(m[0, xs[1], s], self.bx1[0, s]).astype(BF16)
            m[0, xs[2], 2 + s] = add(m[0, xs[2], 2 + s], self.bx1[1, s]).astype(BF16)
        self.b_x = self.both(self.x_src, self.bx2, self.x_right, self.x_left, 2)

    def second_y(self):
        m, ys = self.m, self.ys
        for copy in self.b_y:
            copy.wait_recv()
        for s in range(2):
            cut = y_cut(ys[1])
            m[1, s, :, :, cut] = add(m[1, s, :, :, cut], self.by1[0, s]).astype(BF16)
            cut = y_cut(ys[2])
            m[1, 2 + s, :, :, cut] = add(m[1, 2 + s, :, :, cut], self.by1[1, s]).astype(BF16)
        self.b_y = self.both(self.y_src, self.by2, self.y_right, self.y_left, 2)

    def third_x(self):
        at = self.at
        for copy in self.b_x:
            copy.wait_recv()
        for s in range(4):
            self.cx[s] = add(self.m[0, at.x, s], self.bx2[0, s], self.bx2[1, s]).astype(BF16)
        for n, step in ((0, 2), (1, 1), (2, 3)):
            src = self.cx.at[:, :, y_cut(self.ys[n])]
            self.d.append(self.go.remote(src, self.dx.at[n], at.at_y(step)))

    def third_y(self):
        at = self.at
        for copy in self.b_y:
            copy.wait_recv()
        for s in range(4):
            self.cy[s] = add(self.m[1, s, :, :, y_cut(at.y)], self.by2[0, s], self.by2[1, s]).astype(BF16)
        for n, step in ((0, 2), (1, 1), (2, 3)):
            self.d.append(self.go.remote(self.cy.at[self.xs[n]], self.dy.at[n], at.at_x(step)))

    def fourth(self, pack):
        for copy in self.d:
            copy.wait_recv()
        for h in range(4):
            a = add(self.cx[h, :, y_cut(self.at.y)], *[self.dx[n, h] for n in range(3)])
            b = add(self.cy[self.at.x, h], *[self.dy[n, h] for n in range(3)])
            for low in range(2):
                self.zsend[h, low] = pack(a, b, low).astype(BF16)
        self.last = []
        for step in range(1, 8):
            z = lax.rem(self.at.z + step, 8)
            src = self.zsend.at[lax.div(z, 2), lax.rem(z, 2)]
            self.last.append(self.go.remote(src, self.zland.at[step - 1], self.at.at_z(step)))

    def fifth(self):
        total = self.zsend[self.at.zh, self.at.zl].astype(F32)
        for step in range(7):
            self.last[step].wait_recv()
            total = total + self.zland[step].astype(F32)
        return total


def pack_reduce(a, b, low):
    cut = slice(128 * low, 128 * low + 128)
    return jnp.concatenate([a[:, cut], b[:, cut]], 0)


def pack_qkv_out(a, b, low):
    if low == 0:
        rows = a[:, 0:128], jnp.concatenate([a[:, 128:192], b[:, 128:192]], 1)
    else:
        rows = (
            jnp.concatenate([a[:, 192:256], b[:, 0:64]], 1),
            jnp.concatenate([b[:, 64:128], b[:, 192:256]], 1),
        )
    return jnp.concatenate(rows, 0)


def reduce_scratch(rows, z_rows):
    return [
        pltpu.VMEM((2, 2, rows, 1024), BF16),
        pltpu.VMEM((2, 4, rows, 1024), BF16),
        pltpu.VMEM((2, 2, 4, rows, 256), BF16),
        pltpu.VMEM((2, 4, 4, rows, 256), BF16),
        pltpu.VMEM((4, rows, 1024), BF16),
        pltpu.VMEM((4, 4, rows, 256), BF16),
        pltpu.VMEM((3, 4, rows, 256), BF16),
        pltpu.VMEM((3, 4, rows, 256), BF16),
        pltpu.VMEM((4, 2, z_rows, 128), BF16),
        pltpu.VMEM((7, z_rows, 128), BF16),
    ]


COPIES = 12 + 18 + 3 * 11 + 15 + 8 + 2 * (8 + 6 + 7) + 16


def block_kernel(
    wq_ref, wo_ref, wr_ref, *rest,
):
    loads, rest = rest[:24], rest[24:]
    (
    merged_ref, gin_ref, gq_ref, go_ref, gr_ref,
    blk, land, back, oland, ocland, wq, wo, wr,
    x_tok, cot_tok, qkv, qs, kh, rq, rk, probs, bias, bias_rows, table, mask, att, d_att, dqs, dkh, dqkv,
    xhat, xscale, ro, dproj, dtok, xt, at_t, ls_row, ro_cols, ro_theirs, x_cols, x_theirs, at_cols, at_theirs,
    dred, dred_theirs, dproj_theirs, dqkv_theirs, fa, fb, mb,
    *rest,
    ) = rest
    held, rest = rest[:24], rest[24:]
    (
        stash_ref, exp_ref, t_block_ref, cot_ref, t_cblock_ref,
        table_ref, rel_ref, order_ref, row_cut_ref, col_cut_ref, ls_ref,
        ng_ref, mg_ref, t_merge_ref, t_cmerge_ref, t_unblock_ref, t_unmerge_ref, t_cunblock_ref, t_cunmerge_ref,
        columns_ref, columns_16_ref, bd64_ref, bd32_ref, heads_ref,
    ) = held
    a_bufs, b_bufs, (send_sem, recv_sem, local_sem) = rest[0:10], rest[10:20], rest[20:]
    go = Sender(send_sem, recv_sem, local_sem)
    at = Place()
    c = at.core
    partners = (
        [at.sibling]
        + [at.at_x(step) for step in (1, 2, 3)]
        + [at.at_y(step) for step in (1, 2, 3)]
        + [at.at_z(step) for step in range(1, 8)]
        + [at.at_tile(*step) for step in ((-1, 0), (0, -1), (-1, -1), (1, 0), (0, 1), (1, 1))]
    )
    greet(partners)
    arrivals = [go.local(src, dst) for src, dst in zip(loads, held)]

    def loaded(first, last):
        for copy in arrivals[first:last]:
            copy.wait()

    wait_for(partners)
    all_rows = pl.ds(0, 16)
    q_y = Gather(at, go, wq_ref, wq, lambda y: (all_rows, lanes(512 + 256 * y, 256)), True, True)
    q_x = Gather(at, go, wq_ref, wq, lambda y: (all_rows, pl.ds(0, 512)))
    o_x = Gather(at, go, wo_ref, wo, lambda y: (all_rows, pl.ds(0, 512)))
    r_x = Gather(at, go, wr_ref, wr, lambda y: (pl.ds(0, 64), pl.ds(0, 512)))
    r_y = Gather(at, go, wr_ref, wr, lambda y: (pl.ds(pl.multiple_of(16 * y, 16), 16), pl.ds(512, 512)), True, True)

    q_y.start()
    r_y.start()

    loaded(0, 11)
    table[...] = jnp.zeros((16, 256), F32)
    table[:, 0:225] = 16.0 * jax.nn.sigmoid(table_ref[...])
    by_head = table[...]
    high = by_head.astype(BF16)
    low = (by_head - high.astype(F32)).astype(BF16)
    both = jnp.concatenate([high, low], 0)
    rel = mm(order_ref[...], rel_ref[...].astype(F32).astype(BF16)).astype(BF16)
    rel = dg(rel, order_ref[...], NT).astype(jnp.int32)
    rel = jnp.concatenate([rel[16 * j : 16 * j + 16] for j in range(4)], 1)
    entry = lax.broadcasted_iota(jnp.int32, (256, 256), 0)

    def bias_of(rows):
        for a in rows:
            chosen = jnp.where(entry == rel[a : a + 1], 1.0, 0.0).astype(BF16)
            got = mm(both, chosen)
            got = got[0:16] + got[16:32]
            for j in range(4):
                bias_rows[16 * j + a] = got[:, 64 * j : 64 * j + 64]

    bias_of(range(0, 5))
    o_x.start()

    factor_of = exp_ref[...]
    factor_of = jnp.where(factor_of == -8, 2.0**-8, jnp.where(factor_of == -7, 2.0**-7, 2.0**-6))
    in_window = lax.broadcasted_iota(jnp.int32, (32, 512), 0) // 8
    factor = jnp.zeros((32, 512), F32)
    for w in range(4):
        factor = jnp.where(in_window == w, factor_of[:, w : w + 1], factor)
    inputs = stash_ref[...].astype(F32) * factor[None]
    blk[:, 0:512] = mm(t_block_ref[...], inputs.reshape(256, 512).astype(BF16)).astype(BF16)
    q_x.start()
    q_y.x1()
    cot = cot_ref[...].astype(F32).reshape(64, 1024).astype(BF16)
    cot = jnp.concatenate([cot[:, 256 * q : 256 * q + 256] for q in range(4)], 0)
    blk[:, 512:768] = mm(t_cblock_ref[...], cot).astype(BF16)
    r_y.x1()
    r_x.start()
    q_x.x1()
    q_y.y1()
    o_x.x1()
    halo = [
        go.remote(blk.at[pl.ds(16, 112)], land.at[pl.ds(128, 112)], at.at_tile(-1, 0)),
        go.remote(blk.at[pl.ds(128, 16)], land.at[pl.ds(112, 16)], at.at_tile(0, -1)),
        go.remote(blk.at[pl.ds(0, 16)], land.at[pl.ds(240, 16)], at.at_tile(-1, -1)),
    ]
    bias_of(range(5, 10))
    r_y.y1()
    q_x.x2()
    r_x.x1()
    bias_of(range(10, 16))
    q_y.y2()
    q_x.x3()
    o_x.x2()
    for g in range(4):
        bias[g] = jnp.concatenate([bias_rows[:, 4 * g + h, :] for h in range(4)], 1)
    last_rows = (at.wide == 31).astype(F32)
    last_cols = (at.narrow == 7).astype(F32)
    mask[0] = row_cut_ref[...] * last_rows * -100.0
    mask[1] = jnp.maximum(row_cut_ref[...] * last_rows, col_cut_ref[...] * last_cols) * -100.0
    lane = lax.broadcasted_iota(jnp.int32, (1, 512), 1) // 32
    scales = jnp.zeros((1, 512), F32)
    for h in range(16):
        scales = jnp.where(lane == h, ls_ref[:, h : h + 1], scales)
    ls_row[...] = scales


    for copy in halo:
        copy.wait_recv()
    r_y.y2()
    q_y.y3()
    r_x.x2()
    o_x.x3()
    loaded(11, 24)
    land[pl.ds(0, 112)] = blk[pl.ds(144, 112)]
    x_tok[...] = mm(t_merge_ref[...], land[:, 0:512]).astype(BF16)
    cot = mm(t_cmerge_ref[...], land[:, 512:768]).astype(BF16)
    cot_tok[...] = jnp.concatenate([cot[64 * q : 64 * q + 64] for q in range(4)], 1)
    x_cols[...] = mm(x_tok[...], columns_16_ref[...]).astype(BF16)
    not_mine = lanes(256 * (1 - c), 256)
    mine = lanes(256 * c, 256)
    x_swap = go.remote(x_cols.at[:, not_mine], x_theirs, at.sibling)

    q_x.done()
    q_y.done()

    qkv[...] = mm(x_tok[...], wq[...].reshape(512, 1536)).astype(BF16)
    r_y.y3()
    o_x.done()
    r_x.x3()
    for start, inverse, unit in ((0, rq, qs), (512, rk, kh)):
        for n in range(2):
            cut = slice(256 * n, 256 * n + 256)
            for row in range(0, 256, 128):
                rows = slice(row, row + 128)
                raw = qkv[rows, start + 256 * n : start + 256 * n + 256].astype(F32)
                inv = lax.rsqrt(jnp.maximum(split_mm(raw * raw, bd32_ref[...]), 1e-24))
                inverse[rows, cut] = inv
                raw = raw * inv
                if start == 0:
                    raw = raw * ls_row[:, cut]
                unit[rows, cut] = raw.astype(BF16)
    x_swap.wait_recv()
    xt[:, 0:256] = x_cols[:, mine].T
    xt[:, 256:512] = x_theirs[...].T

    def window(ref, win, cut):
        return jnp.concatenate([ref[pl.ds(64 * k + 16 * win, 16), cut] for k in range(4)], 0)

    def put_window(ref, win, cut, values):
        for k in range(4):
            ref[pl.ds(64 * k + 16 * win, 16), cut] = values[16 * k : 16 * k + 16]

    def spread(rows):
        return jnp.concatenate([rows] * 4, 0) * heads_ref[...]

    def fold(values):
        values = values * heads_ref[...].astype(F32)
        return (values[0:64] + values[64:128]) + (values[128:192] + values[192:256])

    def forward(g):
        cut = slice(g * 128, g * 128 + 128)
        v_cut = slice(g * 128 + 1024, g * 128 + 1152)
        weights = []
        for win in range(4):
            scores = dg(window(qs, win, cut), spread(window(kh, win, cut)), NT)
            weights.append(jnp.exp(scores + bias[g] + mask[1 if win == 3 else 0]))
        totals = split_mm(jnp.concatenate(weights, 0), bd64_ref[...])
        for win in range(4):
            p = weights[win] / totals[64 * win : 64 * win + 64]
            probs[g, win] = p
            values = spread(window(qkv, win, v_cut))
            put_window(att, win, cut, mm(p.astype(BF16), values).astype(BF16))

    for g in range(4):
        forward(g)
    at_cols[...] = mm(att[...], columns_16_ref[...]).astype(BF16)
    at_swap = go.remote(at_cols.at[:, not_mine], at_theirs, at.sibling)
    r_y.done()
    xhat[...] = mm(att[...], wo[...].reshape(512, 512))
    for row in range(0, 256, 64):
        rows = slice(row, row + 64)
        normed, scale = norm_parts(xhat[rows])
        xhat[rows] = normed
        xscale[rows] = scale
        ro[rows] = (x_tok[rows].astype(F32) + normed * ng_ref[...]).astype(BF16)
    ro_cols[...] = mm(ro[...], columns_ref[...]).astype(BF16)
    swap = [go.remote(ro_cols.at[:, not_mine], ro_theirs, at.sibling)]
    r_x.done()

    reduced = jnp.zeros((64, 1024), F32)
    for k in range(4):
        reduced += mm(ro[64 * k : 64 * k + 64], wr[k].reshape(512, 1024))
    normed, scale = norm_parts(reduced)
    dred[...] = norm_back(cot_tok[...].astype(F32), normed, scale, mg_ref[...]).astype(BF16)
    swap.append(go.remote(dred, dred_theirs, at.sibling))
    merged = (normed * mg_ref[...]).astype(BF16)
    merged = jnp.concatenate([merged[:, 256 * q : 256 * q + 256] for q in range(4)], 0)
    mb[...] = mm(t_cunmerge_ref[...], merged).astype(BF16)

    def send_back(tile, landing):
        return [
            go.remote(tile.at[pl.ds(128, 112)], landing.at[pl.ds(16, 112)], at.at_tile(1, 0)),
            go.remote(tile.at[pl.ds(112, 16)], landing.at[pl.ds(128, 16)], at.at_tile(0, 1)),
            go.remote(tile.at[pl.ds(240, 16)], landing.at[pl.ds(0, 16)], at.at_tile(1, 1)),
        ]

    for k in range(4):
        dtok[64 * k : 64 * k + 64] = dg(dred[...], wr[k].reshape(512, 1024), NT).astype(BF16)

    for row in range(0, 256, 64):
        rows = slice(row, row + 64)
        got = norm_back(dtok[rows].astype(F32), xhat[rows], xscale[rows], ng_ref[...])
        dproj[rows] = got.astype(BF16)
    dproj_swap = go.remote(dproj, dproj_theirs, at.sibling)
    d_att[...] = dg(dproj[...], wo[...].reshape(512, 512), NT).astype(BF16)

    for copy in swap:
        copy.wait_recv()
    before_a = go.count
    a_sum = Reduce(at, go, fa, *a_bufs)
    grads = jnp.concatenate([dred[...], dred_theirs[...]], 0)
    for n in range(4):
        k = a_sum.xs[n]
        rows = pl.ds(pl.multiple_of(64 * k, 64), 64)
        tokens = jnp.concatenate([ro_cols[rows, mine], ro_theirs[rows]], 0).T
        for cut in (slice(0, 512), slice(512, 1024)):
            got = mm(tokens, grads[:, cut]).astype(BF16).reshape(4, 64, 512)
            fa[0, k, :, :, cut] = got[:, 0:32]
            fa[1, k, :, :, cut] = got[:, 32:64]
        if n == 0:
            a_sum.first_x()
    a_sum.first_y()

    def backward(g):
        cut = slice(g * 128, g * 128 + 128)
        v_cut = slice(g * 128 + 1024, g * 128 + 1152)
        dps = []
        for win in range(4):
            dp = dg(window(d_att, win, cut), spread(window(qkv, win, v_cut)), NT)
            dps.append(dp.astype(BF16).astype(F32))
        alike = split_mm(jnp.concatenate([probs[g, win] * dps[win] for win in range(4)], 0), bd64_ref[...])
        for win in range(4):
            p = probs[g, win]
            ds = (p * (dps[win] - alike[64 * win : 64 * win + 64])).astype(BF16)
            put_window(dqs, win, cut, mm(ds, spread(window(kh, win, cut))))
            put_window(dkh, win, cut, fold(dg(ds, window(qs, win, cut), TN)))
            put_window(dqkv, win, v_cut, fold(dg(p.astype(BF16), window(d_att, win, cut), TN)).astype(BF16))

    for g in range(4):
        backward(g)

    def swap_dqkv(start):
        cut = pl.ds(start, 512)
        return go.remote(dqkv.at[:, cut], dqkv_theirs.at[:, cut], at.sibling)

    dqkv_swap = [swap_dqkv(1024)]
    a_sum.second_x()
    a_sum.second_y()
    for start, inverse, grad in ((0, rq, dqs), (512, rk, dkh)):
        for n in range(2):
            cut = slice(256 * n, 256 * n + 256)
            both_cut = slice(start + 256 * n, start + 256 * n + 256)
            for row in range(0, 256, 128):
                rows = slice(row, row + 128)
                inv = inverse[rows, cut]
                unit = qkv[rows, both_cut].astype(F32) * inv
                d_unit = grad[rows, cut]
                if start == 0:
                    d_unit = d_unit * ls_row[:, cut]
                along = split_mm(unit * d_unit, bd32_ref[...])
                along = jnp.where(inv < 1e12, along, 0.0)
                dqkv[rows, both_cut] = (inv * (d_unit - unit * along)).astype(BF16)
        dqkv_swap.append(swap_dqkv(start))
    at_swap.wait_recv()
    at_t[:, 0:256] = at_cols[:, mine].T
    at_t[:, 256:512] = at_theirs[...].T
    dproj_swap.wait_recv()
    d_out = jnp.concatenate([dproj[...], dproj_theirs[...]], 0)
    out = mm(at_t[...], d_out).astype(BF16)
    for y in range(4):
        fb[1, :, :, :, 256 * y + 128 : 256 * y + 256] = out[:, 128 * y : 128 * y + 128].reshape(4, 4, 16, 128)

    merged_back = send_back(mb, ocland)
    d_in = dtok[...].astype(F32) + dg(dqkv[...], wq[...].reshape(512, 1536), NT)
    back[...] = mm(t_unmerge_ref[...], d_in.astype(BF16)).astype(BF16)
    grad_back = send_back(back, oland)

    for copy in dqkv_swap:
        copy.wait_recv()
    before_b = go.count
    b_sum = Reduce(at, go, fb, *b_bufs)
    for n in range(4):
        y = b_sum.ys[n]
        cut = lanes(384 * y, 384)
        grads = jnp.concatenate([dqkv[:, cut], dqkv_theirs[:, cut]], 0)
        got = mm(xt[...], grads).astype(BF16)
        fb[0, :, :, :, y_cut(y)] = got[:, 0:256].reshape(4, 4, 16, 256)
        fb[1, :, :, :, lanes(256 * y, 128)] = got[:, 256:384].reshape(4, 4, 16, 128)
    b_sum.first_x()
    b_sum.first_y()
    go.drain(before_a // 2)
    a_sum.third_x()
    a_sum.third_y()
    b_sum.second_y()
    b_sum.second_x()
    go.drain(before_b)
    before_c = go.count
    a_sum.fourth(pack_reduce)
    b_sum.third_y()
    b_sum.third_x()
    b_sum.fourth(pack_qkv_out)
    go.drain(before_c)
    for copy in merged_back + grad_back:
        copy.wait_recv()
    oland[pl.ds(144, 112)] = back[pl.ds(0, 112)]
    ocland[pl.ds(144, 112)] = mb[pl.ds(0, 112)]
    gin_ref[...] = mm(t_unblock_ref[...], oland[...]).astype(BF16).reshape(8, 32, 512)
    got = mm(t_cunblock_ref[...], ocland[...]).astype(BF16)
    for q in range(4):
        merged_ref[:, :, 256 * q : 256 * q + 256] = got[64 * q : 64 * q + 64].reshape(4, 16, 256)
    factor = 1.0 / 256.0
    gr_ref[...] = a_sum.fifth() * factor
    go.drain()
    total = b_sum.fifth() * factor
    gq_ref[:, 0:128] = total[0:16]
    gq_ref[:, 128:192] = total[16:32, 0:64]
    go_ref[...] = total[16:32, 64:128]


def hand_on(*refs):
    for src, dst in zip(refs[:5], refs[5:]):
        dst[...] = src[...]


def on_device(
    stash_values, scale_exp, w_qkv, w_out, w_reduce, logit_scale, bias_table, rel_index, norm_gain, merge_gain, cotangent
):
    vmem = pl.BlockSpec(memory_space=pltpu.VMEM)
    sems = pltpu.SemaphoreType.DMA
    outputs = (
        jax.ShapeDtypeStruct((4, 16, 1024), BF16),
        jax.ShapeDtypeStruct((8, 32, 512), BF16),
        jax.ShapeDtypeStruct((16, 192), F32),
        jax.ShapeDtypeStruct((16, 64), F32),
        jax.ShapeDtypeStruct((64, 128), F32),
    )
    loads = (
        stash_values, scale_exp, const(T_BLOCK), cotangent, const(T_CBLOCK),
        bias_table.T, rel_index, const(WIN_ORDER), const(ROW_CUT, F32), const(COL_CUT, F32), logit_scale.reshape(1, 16),
        norm_gain.reshape(1, 512), merge_gain.reshape(1, 1024),
        const(T_MERGE), const(T_CMERGE), const(T_BLOCK.T), const(T_MERGE.T), const(T_CBLOCK.T), const(T_CMERGE.T),
        const(COLUMNS_64), const(COLUMNS_16),
        const(same_block(256, 64, 256, 64)), const(same_block(256, 32, 256, 32)), const(same_block(256, 64, 128, 32)),
    )
    tokens = lambda width, kind=BF16: pltpu.VMEM((256, width), kind)
    results = pl.pallas_call(
        block_kernel,
        out_shape=outputs,
        in_specs=[pl.BlockSpec(memory_space=pl.ANY)] * 27,
        out_specs=(vmem,) * 5,
        scratch_shapes=[
            tokens(768), tokens(768), tokens(512), tokens(512), tokens(256),
            pltpu.VMEM((4, 4, 2, 16, 1536), BF16),
            pltpu.VMEM((4, 4, 2, 16, 512), BF16),
            pltpu.VMEM((4, 4, 2, 64, 1024), BF16),
            tokens(512),
            pltpu.VMEM((64, 1024), BF16),
            tokens(1536), tokens(512), tokens(512), tokens(512, F32), tokens(512, F32),
            pltpu.VMEM((4, 4, 64, 256), F32),
            pltpu.VMEM((4, 64, 256), F32),
            pltpu.VMEM((64, 16, 64), F32),
            pltpu.VMEM((16, 256), F32),
            pltpu.VMEM((2, 64, 256), F32),
            tokens(512), tokens(512), tokens(512, F32), tokens(512, F32), tokens(1536),
            tokens(512, F32), tokens(1, F32), tokens(512), tokens(512), tokens(512),
            tokens(512), tokens(512),
            pltpu.VMEM((1, 512), F32),
            tokens(512), tokens(256), tokens(512), tokens(256), tokens(512), tokens(256),
            pltpu.VMEM((64, 1024), BF16),
            pltpu.VMEM((64, 1024), BF16),
            tokens(512), tokens(1536),
            pltpu.VMEM((2, 4, 4, 32, 1024), BF16),
            pltpu.VMEM((2, 4, 4, 16, 1024), BF16),
            tokens(256),
            *[pltpu.VMEM(load.shape, load.dtype) for load in loads],
            *reduce_scratch(32, 64),
            *reduce_scratch(16, 32),
            sems((COPIES,)),
            sems((COPIES,)),
            sems((32,)),
        ],
        compiler_params=pltpu.CompilerParams(
            collective_id=0, has_side_effects=True, vmem_limit_bytes=60 * 1024 * 1024
        ),
        name="block_forward_backward",
    )(w_qkv, w_out, w_reduce, *loads)
    return pl.pallas_call(
        hand_on,
        out_shape=outputs,
        in_specs=[vmem] * 5,
        out_specs=(vmem,) * 5,
        name="hand_on",
    )(*results)


def solution(mesh):
    tile = P("wide", "narrow", None)
    rows = P("wide", None)
    both = P("wide", "narrow")
    return jax.shard_map(
        on_device,
        mesh=mesh,
        in_specs=(tile, both, rows, rows, rows, P(), P(), P(), P(), P(), tile),
        out_specs=(tile, tile, both, both, both),
        check_vma=False,
    )
```

```python
import jax
import jax.numpy as jnp
import numpy as np
from jax import lax
from jax.experimental import pallas as pl
from jax.experimental.pallas import tpu as pltpu
from jax.sharding import PartitionSpec as P

MESH = pl.DeviceIdType.MESH
F32 = jnp.float32
BF16 = jnp.bfloat16
NT = (((1,), (1,)), ((), ()))
TN = (((0,), (0,)), ((), ()))


def one_hot(sources):
    sources = np.asarray(sources).reshape(-1)
    table = np.zeros((len(sources), len(sources)), np.float32)
    table[np.arange(len(sources)), sources] = 1.0
    return table


def token_tables():
    i, j, r, c = np.meshgrid(*map(np.arange, (2, 8, 4, 4)), indexing="ij")
    block_from_natural = one_hot((4 * i + r) * 32 + 4 * j + c)
    k, win, mr, mc = np.meshgrid(*map(np.arange, (4, 4, 4, 4)), indexing="ij")
    i, r = mr // 2, 2 * (mr % 2) + k % 2
    j, c = 2 * win + mc // 2, 2 * (mc % 2) + k // 2
    merge_from_block = one_hot((i * 8 + j) * 16 + r * 4 + c)
    i, j, q, m = np.meshgrid(*map(np.arange, (2, 8, 4, 4)), indexing="ij")
    cot_block_from_natural = one_hot(q * 64 + (2 * i + m // 2) * 16 + 2 * j + m % 2)
    q, win, mr, mc = np.meshgrid(*map(np.arange, (4, 4, 4, 4)), indexing="ij")
    i, j, m = mr // 2, 2 * win + mc // 2, (mr % 2) * 2 + mc % 2
    cot_merge_from_block = one_hot((i * 8 + j) * 16 + q * 4 + m)
    return (
        block_from_natural,
        merge_from_block,
        cot_block_from_natural,
        cot_merge_from_block,
    )


def window_tables():
    k, mr, mc = np.meshgrid(*map(np.arange, (4, 4, 4)), indexing="ij")
    row, col = (2 * mr + k % 2).reshape(-1), (2 * mc + k // 2).reshape(-1)
    order = one_hot(row * 8 + col)
    row_cut = (row[:, None] >= 4) != (row[None, :] >= 4)
    col_cut = (col[:, None] >= 4) != (col[None, :] >= 4)
    tiled = lambda cut: np.tile(cut.astype(np.float32), (1, 4))
    return order, tiled(row_cut), tiled(col_cut)


def same_block(rows, row_size, cols, col_size):
    return (
        (np.arange(rows) // row_size)[:, None] == (np.arange(cols) // col_size)[None]
    ).astype(np.float32)


T_BLOCK, T_MERGE, T_CBLOCK, T_CMERGE = token_tables()
COLUMNS_64 = one_hot(np.arange(512).reshape(4, 2, 64).transpose(1, 0, 2)).T
COLUMNS_16 = one_hot(np.arange(512).reshape(16, 2, 16).transpose(1, 0, 2)).T
WIN_ORDER, ROW_CUT, COL_CUT = window_tables()


def const(table, dtype=BF16):
    return jnp.asarray(table, dtype)


class Place:
    def __init__(self):
        wide, narrow = lax.axis_index("wide"), lax.axis_index("narrow")
        self.wide, self.narrow = wide, narrow
        self.core = lax.rem(wide, 2)
        self.zh = lax.rem(lax.div(wide, 2), 4)
        self.x = lax.div(wide, 8)
        self.y = lax.div(narrow, 2)
        self.zl = lax.rem(narrow, 2)
        self.z = 2 * self.zh + self.zl
        self.sibling = (wide + 1 - 2 * self.core, narrow)

    def at_x(self, step):
        return ((lax.rem(self.x + step + 4, 4) * 4 + self.zh) * 2 + self.core, self.narrow)

    def at_y(self, step):
        return (self.wide, lax.rem(self.y + step + 4, 4) * 2 + self.zl)

    def at_z(self, step):
        z = lax.rem(self.z + step + 8, 8)
        return ((self.x * 4 + lax.div(z, 2)) * 2 + self.core, self.y * 2 + lax.rem(z, 2))

    def at_tile(self, rows, cols):
        return (lax.rem(self.wide + rows + 32, 32), lax.rem(self.narrow + cols + 8, 8))


class Sender:
    def __init__(self, send_sem, recv_sem, local_sem):
        self.send_sem, self.recv_sem, self.local_sem = send_sem, recv_sem, local_sem
        self.started, self.count, self.local_count, self.drained = [], 0, 0, 0

    def remote(self, src, dst, device):
        copy = pltpu.make_async_remote_copy(
            src_ref=src,
            dst_ref=dst,
            send_sem=self.send_sem.at[self.count],
            recv_sem=self.recv_sem.at[self.count],
            device_id=device,
            device_id_type=MESH,
        )
        self.count += 1
        copy.start()
        self.started.append(copy)
        return copy

    def local(self, src, dst):
        copy = pltpu.make_async_copy(src, dst, self.local_sem.at[self.local_count])
        self.local_count += 1
        copy.start()
        return copy

    def drain(self, until=None):
        until = self.count if until is None else until
        for copy in self.started[self.drained : until]:
            copy.wait_send()
        self.drained = until


def greet(devices):
    barrier = pltpu.get_barrier_semaphore()
    for device in devices:
        pl.semaphore_signal(barrier, inc=1, device_id=device, device_id_type=MESH)


def wait_for(devices):
    pl.semaphore_wait(pltpu.get_barrier_semaphore(), len(devices))


def lanes(start, size):
    return pl.ds(pl.multiple_of(start, 128), size)


def mm(a, b):
    return jnp.dot(a, b, preferred_element_type=F32)


def dg(a, b, dims):
    return lax.dot_general(a, b, dims, preferred_element_type=F32)


def add(*parts):
    total = parts[0].astype(F32)
    for one in parts[1:]:
        total = total + one.astype(F32)
    return total


def split_mm(values, table):
    high = values.astype(BF16)
    low = (values - high.astype(F32)).astype(BF16)
    both = mm(jnp.concatenate([high, low], 0), table)
    return both[: len(values)] + both[len(values) :]


def norm_parts(values):
    centred = values - jnp.mean(values, -1, keepdims=True)
    scale = lax.rsqrt(jnp.mean(centred * centred, -1, keepdims=True) + 1e-05)
    return centred * scale, scale


def norm_back(cot, normed, scale, gain):
    cot = cot * gain
    shared = jnp.mean(cot, -1, keepdims=True) + normed * jnp.mean(cot * normed, -1, keepdims=True)
    return scale * (cot - shared)


EVERY = pl.ds(0, 4)


class Gather:
    def __init__(self, at, go, shard, whole, cut, quarters=False, direct=False):
        self.at, self.go, self.shard, self.whole, self.cut = at, go, shard, whole, cut
        self.quarters, self.direct = quarters, direct
        self.x_left, self.x_right, self.x_far = (lax.rem(at.x + step, 4) for step in (3, 1, 2))
        self.y_left, self.y_right, self.y_far = (lax.rem(at.y + step, 4) for step in (3, 1, 2))
        self.shared = []

    def part(self, xs, zs, y=None):
        y = self.at.y if y is None else y
        return self.whole.at[(xs, zs, self.at.core) + self.cut(y)]

    def move(self, xs, zs, device, y=None):
        ref = self.part(xs, zs, y)
        return self.go.remote(ref, ref, device)

    def share(self, xs, zs, y=None):
        self.shared.append(self.move(xs, zs, self.at.sibling, y))

    def start(self):
        at = self.at
        own, there = self.shard.at[self.cut(at.y)], self.part(at.x, at.zh)
        way = 2 * at.zl - 1
        self.z = [self.go.remote(own, there, at.at_z(way * step)) for step in (1, 2, 3)]
        self.mine = self.go.local(own, there)

    def x1(self):
        at = self.at
        self.mine.wait()
        for copy in self.z:
            copy.wait_recv()
        steps = (1, 2, -1) if self.direct else (1, -1)
        self.x = [self.move(at.x, EVERY, at.at_x(step)) for step in steps]
        if not self.quarters:
            self.share(at.x, EVERY)

    def x2(self):
        at = self.at
        self.x[0].wait_recv()
        far = [self.move(self.x_left, pl.ds(0, 2), at.at_x(1))]
        self.x[1].wait_recv()
        far.append(self.move(self.x_right, pl.ds(2, 2), at.at_x(-1)))
        self.x = far
        if not self.quarters:
            self.share(self.x_left, EVERY)
            self.share(self.x_right, EVERY)

    def x3(self):
        if self.direct and not self.quarters:
            for copy, x in zip(self.x, (self.x_left, self.x_far, self.x_right)):
                copy.wait_recv()
                self.share(x, EVERY)
            return
        for copy in self.x:
            copy.wait_recv()
        if not self.quarters:
            self.share(self.x_far, EVERY)

    def y1(self):
        at = self.at
        self.x3()
        self.y = [self.move(EVERY, EVERY, at.at_y(step)) for step in (1, -1)]
        self.share(EVERY, EVERY)

    def y2(self):
        at = self.at
        self.y[0].wait_recv()
        far = [self.move(pl.ds(0, 2), EVERY, at.at_y(1), self.y_left)]
        self.y[1].wait_recv()
        far.append(self.move(pl.ds(2, 2), EVERY, at.at_y(-1), self.y_right))
        self.y = far
        self.share(EVERY, EVERY, self.y_left)
        self.share(EVERY, EVERY, self.y_right)

    def y3(self):
        for copy in self.y:
            copy.wait_recv()
        self.share(EVERY, EVERY, self.y_far)

    def done(self):
        for copy in self.shared:
            copy.wait_recv()


def y_cut(j):
    return lanes(j * 256, 256)


class Reduce:
    def __init__(self, at, go, m, bx1, bx2, by1, by2, cx, cy, dx, dy, zsend, zland):
        self.at, self.go, self.m = at, go, m
        self.bx1, self.bx2, self.by1, self.by2 = bx1, bx2, by1, by2
        self.cx, self.cy = cx, cy
        self.dx, self.dy = dx, dy
        self.zsend, self.zland = zsend, zland
        self.xs = [lax.rem(at.x + step, 4) for step in (2, 1, 3, 0)]
        self.ys = [lax.rem(at.y + step, 4) for step in (2, 1, 3, 0)]
        self.d = []
        self.x_left, self.x_right = at.at_x(-1), at.at_x(1)
        self.y_left, self.y_right = at.at_y(-1), at.at_y(1)

    def both(self, src, dst, right, left, step):
        if step == 1:
            pairs = ((src(0, pl.ds(0, 2)), right), (src(0, pl.ds(2, 2)), left))
        else:
            pairs = ((src(1, EVERY), right), (src(2, EVERY), left))
        return [self.go.remote(ref, dst.at[n], device) for n, (ref, device) in enumerate(pairs)]

    def x_src(self, n, part):
        return self.m.at[0, self.xs[n], part]

    def y_src(self, n, part):
        return self.m.at[1, part, :, :, y_cut(self.ys[n])]

    def first_x(self):
        self.b_x = self.both(self.x_src, self.bx1, self.x_right, self.x_left, 1)

    def first_y(self):
        self.b_y = self.both(self.y_src, self.by1, self.y_right, self.y_left, 1)

    def second_x(self):
        m, xs = self.m, self.xs
        for copy in self.b_x:
            copy.wait_recv()
        for s in range(2):
            m[0, xs[1], s] = add(m[0, xs[1], s], self.bx1[0, s]).astype(BF16)
            m[0, xs[2], 2 + s] = add(m[0, xs[2], 2 + s], self.bx1[1, s]).astype(BF16)
        self.b_x = self.both(self.x_src, self.bx2, self.x_right, self.x_left, 2)

    def second_y(self):
        m, ys = self.m, self.ys
        for copy in self.b_y:
            copy.wait_recv()
        for s in range(2):
            cut = y_cut(ys[1])
            m[1, s, :, :, cut] = add(m[1, s, :, :, cut], self.by1[0, s]).astype(BF16)
            cut = y_cut(ys[2])
            m[1, 2 + s, :, :, cut] = add(m[1, 2 + s, :, :, cut], self.by1[1, s]).astype(BF16)
        self.b_y = self.both(self.y_src, self.by2, self.y_right, self.y_left, 2)

    def third_x(self):
        at = self.at
        for copy in self.b_x:
            copy.wait_recv()
        for s in range(4):
            self.cx[s] = add(self.m[0, at.x, s], self.bx2[0, s], self.bx2[1, s]).astype(BF16)
        for n, step in ((0, 2), (1, 1), (2, 3)):
            src = self.cx.at[:, :, y_cut(self.ys[n])]
            self.d.append(self.go.remote(src, self.dx.at[n], at.at_y(step)))

    def third_y(self):
        at = self.at
        for copy in self.b_y:
            copy.wait_recv()
        for s in range(4):
            self.cy[s] = add(self.m[1, s, :, :, y_cut(at.y)], self.by2[0, s], self.by2[1, s]).astype(BF16)
        for n, step in ((0, 2), (1, 1), (2, 3)):
            self.d.append(self.go.remote(self.cy.at[self.xs[n]], self.dy.at[n], at.at_x(step)))

    def fourth(self, pack):
        for copy in self.d:
            copy.wait_recv()
        for h in range(4):
            a = add(self.cx[h, :, y_cut(self.at.y)], *[self.dx[n, h] for n in range(3)])
            b = add(self.cy[self.at.x, h], *[self.dy[n, h] for n in range(3)])
            for low in range(2):
                self.zsend[h, low] = pack(a, b, low).astype(BF16)
        self.last = []
        for step in range(1, 8):
            z = lax.rem(self.at.z + step, 8)
            src = self.zsend.at[lax.div(z, 2), lax.rem(z, 2)]
            self.last.append(self.go.remote(src, self.zland.at[step - 1], self.at.at_z(step)))

    def fifth(self):
        total = self.zsend[self.at.zh, self.at.zl].astype(F32)
        for step in range(7):
            self.last[step].wait_recv()
            total = total + self.zland[step].astype(F32)
        return total


class ReduceZ:
    def __init__(self, at, go, m, r1, r2, r3, r4, ex, dx, ey, dy):
        self.at, self.go, self.m = at, go, m
        self.r1, self.rings = r1, (r2, r3, r4)
        self.ex, self.dx, self.ey, self.dy = ex, dx, ey, dy

    def slot(self, step):
        z = lax.rem(self.at.z + step, 8)
        return lax.div(z, 2), lax.rem(z, 2)

    def first(self):
        far = self.m.at[self.slot(4)]
        self.sent = [
            self.go.remote(far.at[pl.ds(0, 2)], self.r1.at[0], self.at.at_z(1)),
            self.go.remote(far.at[pl.ds(2, 2)], self.r1.at[1], self.at.at_z(-1)),
        ]

    def step(self, n):
        up, down = self.slot(4 - n), self.slot(4 + n)
        for copy in self.sent:
            copy.wait_recv()
        for k in range(2 if n == 1 else 4):
            if n == 1:
                got, ups, downs = self.r1, up + (k,), down + (2 + k,)
            else:
                got, ups, downs = self.rings[n - 2], up + (k,), down + (k,)
            self.m[ups] = add(self.m[ups], got[0, k]).astype(BF16)
            self.m[downs] = add(self.m[downs], got[1, k]).astype(BF16)
        self.sent = [
            self.go.remote(self.m.at[up], self.rings[n - 1].at[0], self.at.at_z(1)),
            self.go.remote(self.m.at[down], self.rings[n - 1].at[1], self.at.at_z(-1)),
        ]

    def fifth(self):
        for copy in self.sent:
            copy.wait_recv()
        mine, last = self.slot(0), self.rings[2]
        for k in range(4):
            self.ex[k] = add(self.m[mine + (k,)], last[0, k], last[1, k]).astype(BF16)
        self.sent = []
        for n, step in enumerate((2, 1, 3)):
            src = self.ex.at[lax.rem(self.at.x + step, 4)]
            self.sent.append(self.go.remote(src, self.dx.at[n], self.at.at_x(step)))

    def sixth(self):
        for copy in self.sent:
            copy.wait_recv()
        self.ey[...] = add(self.ex[self.at.x], *[self.dx[n] for n in range(3)]).astype(BF16)
        self.sent = []
        for n, step in enumerate((2, 1, 3)):
            src = self.ey.at[:, lanes(lax.rem(self.at.y + step, 4) * 128, 128)]
            self.sent.append(self.go.remote(src, self.dy.at[n], self.at.at_y(step)))

    def last(self):
        for copy in self.sent:
            copy.wait_recv()
        return add(self.ey[:, lanes(self.at.y * 128, 128)], *[self.dy[n] for n in range(3)])


Z_SCRATCH = (
    pltpu.VMEM((2, 2, 32, 512), BF16),
    pltpu.VMEM((2, 4, 32, 512), BF16),
    pltpu.VMEM((2, 4, 32, 512), BF16),
    pltpu.VMEM((2, 4, 32, 512), BF16),
    pltpu.VMEM((4, 32, 512), BF16),
    pltpu.VMEM((3, 32, 512), BF16),
    pltpu.VMEM((32, 512), BF16),
    pltpu.VMEM((3, 32, 128), BF16),
)


def pack_reduce(a, b, low):
    cut = slice(128 * low, 128 * low + 128)
    return jnp.concatenate([a[:, cut], b[:, cut]], 0)


def pack_qkv_out(a, b, low):
    if low == 0:
        rows = a[:, 0:128], jnp.concatenate([a[:, 128:192], b[:, 128:192]], 1)
    else:
        rows = (
            jnp.concatenate([a[:, 192:256], b[:, 0:64]], 1),
            jnp.concatenate([b[:, 64:128], b[:, 192:256]], 1),
        )
    return jnp.concatenate(rows, 0)


def reduce_scratch(rows, z_rows):
    return [
        pltpu.VMEM((2, 2, rows, 1024), BF16),
        pltpu.VMEM((2, 4, rows, 1024), BF16),
        pltpu.VMEM((2, 2, 4, rows, 256), BF16),
        pltpu.VMEM((2, 4, 4, rows, 256), BF16),
        pltpu.VMEM((4, rows, 1024), BF16),
        pltpu.VMEM((4, 4, rows, 256), BF16),
        pltpu.VMEM((3, 4, rows, 256), BF16),
        pltpu.VMEM((3, 4, rows, 256), BF16),
        pltpu.VMEM((4, 2, z_rows, 128), BF16),
        pltpu.VMEM((7, z_rows, 128), BF16),
    ]


COPIES = 12 + 18 + 3 * 11 + 15 + 8 + 2 * (8 + 6 + 7) + 14 + 16


def block_kernel(
    wq_ref, wo_ref, wr_ref, *rest,
):
    loads, rest = rest[:24], rest[24:]
    (
    merged_ref, gin_ref, gq_ref, go_ref, gr_ref,
    blk, land, back, oland, ocland, wq, wo, wr,
    x_tok, cot_tok, qkv, qs, kh, rq, rk, probs, bias, bias_rows, table, mask, att, d_att, dqs, dkh, dqkv,
    xhat, xscale, ro, dproj, dtok, xt, at_t, ls_row, ro_cols, ro_theirs, x_cols, x_theirs, at_cols, at_theirs,
    dred, dred_theirs, dproj_theirs, dqkv_theirs, fa, fz, fb, mb,
    *rest,
    ) = rest
    held, rest = rest[:24], rest[24:]
    (
        stash_ref, exp_ref, t_block_ref, cot_ref, t_cblock_ref,
        table_ref, rel_ref, order_ref, row_cut_ref, col_cut_ref, ls_ref,
        ng_ref, mg_ref, t_merge_ref, t_cmerge_ref, t_unblock_ref, t_unmerge_ref, t_cunblock_ref, t_cunmerge_ref,
        columns_ref, columns_16_ref, bd64_ref, bd32_ref, heads_ref,
    ) = held
    a_bufs, b_bufs, z_bufs, (send_sem, recv_sem, local_sem) = rest[0:10], rest[10:20], rest[20:28], rest[28:]
    go = Sender(send_sem, recv_sem, local_sem)
    at = Place()
    c = at.core
    partners = (
        [at.sibling]
        + [at.at_x(step) for step in (1, 2, 3)]
        + [at.at_y(step) for step in (1, 2, 3)]
        + [at.at_z(step) for step in range(1, 8)]
        + [at.at_tile(*step) for step in ((-1, 0), (0, -1), (-1, -1), (1, 0), (0, 1), (1, 1))]
    )
    greet(partners)
    arrivals = [go.local(src, dst) for src, dst in zip(loads, held)]

    def loaded(first, last):
        for copy in arrivals[first:last]:
            copy.wait()

    wait_for(partners)
    all_rows = pl.ds(0, 16)
    q_y = Gather(at, go, wq_ref, wq, lambda y: (all_rows, lanes(512 + 256 * y, 256)), True, True)
    q_x = Gather(at, go, wq_ref, wq, lambda y: (all_rows, pl.ds(0, 512)))
    o_x = Gather(at, go, wo_ref, wo, lambda y: (all_rows, pl.ds(0, 512)))
    r_x = Gather(at, go, wr_ref, wr, lambda y: (pl.ds(0, 64), pl.ds(0, 512)))
    r_y = Gather(at, go, wr_ref, wr, lambda y: (pl.ds(pl.multiple_of(16 * y, 16), 16), pl.ds(512, 512)), True, True)

    q_y.start()
    r_y.start()

    loaded(0, 11)
    table[...] = jnp.zeros((16, 256), F32)
    table[:, 0:225] = 16.0 * jax.nn.sigmoid(table_ref[...])
    by_head = table[...]
    high = by_head.astype(BF16)
    low = (by_head - high.astype(F32)).astype(BF16)
    both = jnp.concatenate([high, low], 0)
    rel = mm(order_ref[...], rel_ref[...].astype(F32).astype(BF16)).astype(BF16)
    rel = dg(rel, order_ref[...], NT).astype(jnp.int32)
    rel = jnp.concatenate([rel[16 * j : 16 * j + 16] for j in range(4)], 1)
    entry = lax.broadcasted_iota(jnp.int32, (256, 256), 0)

    def bias_of(rows):
        for a in rows:
            chosen = jnp.where(entry == rel[a : a + 1], 1.0, 0.0).astype(BF16)
            got = mm(both, chosen)
            got = got[0:16] + got[16:32]
            for j in range(4):
                bias_rows[16 * j + a] = got[:, 64 * j : 64 * j + 64]

    bias_of(range(0, 5))
    o_x.start()

    factor_of = exp_ref[...]
    factor_of = jnp.where(factor_of == -8, 2.0**-8, jnp.where(factor_of == -7, 2.0**-7, 2.0**-6))
    in_window = lax.broadcasted_iota(jnp.int32, (32, 512), 0) // 8
    factor = jnp.zeros((32, 512), F32)
    for w in range(4):
        factor = jnp.where(in_window == w, factor_of[:, w : w + 1], factor)
    inputs = stash_ref[...].astype(F32) * factor[None]
    blk[:, 0:512] = mm(t_block_ref[...], inputs.reshape(256, 512).astype(BF16)).astype(BF16)
    q_x.start()
    q_y.x1()
    cot = cot_ref[...].astype(F32).reshape(64, 1024).astype(BF16)
    cot = jnp.concatenate([cot[:, 256 * q : 256 * q + 256] for q in range(4)], 0)
    blk[:, 512:768] = mm(t_cblock_ref[...], cot).astype(BF16)
    r_y.x1()
    r_x.start()
    q_x.x1()
    q_y.y1()
    o_x.x1()
    halo = [
        go.remote(blk.at[pl.ds(16, 112)], land.at[pl.ds(128, 112)], at.at_tile(-1, 0)),
        go.remote(blk.at[pl.ds(128, 16)], land.at[pl.ds(112, 16)], at.at_tile(0, -1)),
        go.remote(blk.at[pl.ds(0, 16)], land.at[pl.ds(240, 16)], at.at_tile(-1, -1)),
    ]
    bias_of(range(5, 10))
    r_y.y1()
    q_x.x2()
    r_x.x1()
    bias_of(range(10, 16))
    q_y.y2()
    q_x.x3()
    o_x.x2()
    for g in range(4):
        bias[g] = jnp.concatenate([bias_rows[:, 4 * g + h, :] for h in range(4)], 1)
    last_rows = (at.wide == 31).astype(F32)
    last_cols = (at.narrow == 7).astype(F32)
    mask[0] = row_cut_ref[...] * last_rows * -100.0
    mask[1] = jnp.maximum(row_cut_ref[...] * last_rows, col_cut_ref[...] * last_cols) * -100.0
    lane = lax.broadcasted_iota(jnp.int32, (1, 512), 1) // 32
    scales = jnp.zeros((1, 512), F32)
    for h in range(16):
        scales = jnp.where(lane == h, ls_ref[:, h : h + 1], scales)
    ls_row[...] = scales


    for copy in halo:
        copy.wait_recv()
    r_y.y2()
    q_y.y3()
    r_x.x2()
    o_x.x3()
    loaded(11, 24)
    land[pl.ds(0, 112)] = blk[pl.ds(144, 112)]
    x_tok[...] = mm(t_merge_ref[...], land[:, 0:512]).astype(BF16)
    cot = mm(t_cmerge_ref[...], land[:, 512:768]).astype(BF16)
    cot_tok[...] = jnp.concatenate([cot[64 * q : 64 * q + 64] for q in range(4)], 1)
    x_cols[...] = mm(x_tok[...], columns_16_ref[...]).astype(BF16)
    not_mine = lanes(256 * (1 - c), 256)
    mine = lanes(256 * c, 256)
    x_swap = go.remote(x_cols.at[:, not_mine], x_theirs, at.sibling)

    q_x.done()
    q_y.done()

    qkv[...] = mm(x_tok[...], wq[...].reshape(512, 1536)).astype(BF16)
    r_y.y3()
    o_x.done()
    r_x.x3()
    for start, inverse, unit in ((0, rq, qs), (512, rk, kh)):
        for n in range(2):
            cut = slice(256 * n, 256 * n + 256)
            for row in range(0, 256, 128):
                rows = slice(row, row + 128)
                raw = qkv[rows, start + 256 * n : start + 256 * n + 256].astype(F32)
                inv = lax.rsqrt(jnp.maximum(split_mm(raw * raw, bd32_ref[...]), 1e-24))
                inverse[rows, cut] = inv
                raw = raw * inv
                if start == 0:
                    raw = raw * ls_row[:, cut]
                unit[rows, cut] = raw.astype(BF16)
    x_swap.wait_recv()
    xt[:, 0:256] = x_cols[:, mine].T
    xt[:, 256:512] = x_theirs[...].T

    def window(ref, win, cut):
        return jnp.concatenate([ref[pl.ds(64 * k + 16 * win, 16), cut] for k in range(4)], 0)

    def put_window(ref, win, cut, values):
        for k in range(4):
            ref[pl.ds(64 * k + 16 * win, 16), cut] = values[16 * k : 16 * k + 16]

    def spread(rows):
        return jnp.concatenate([rows] * 4, 0) * heads_ref[...]

    def fold(values):
        values = values * heads_ref[...].astype(F32)
        return (values[0:64] + values[64:128]) + (values[128:192] + values[192:256])

    def forward(g):
        cut = slice(g * 128, g * 128 + 128)
        v_cut = slice(g * 128 + 1024, g * 128 + 1152)
        weights = []
        for win in range(4):
            scores = dg(window(qs, win, cut), spread(window(kh, win, cut)), NT)
            weights.append(jnp.exp(scores + bias[g] + mask[1 if win == 3 else 0]))
        totals = split_mm(jnp.concatenate(weights, 0), bd64_ref[...])
        for win in range(4):
            p = weights[win] / totals[64 * win : 64 * win + 64]
            probs[g, win] = p
            values = spread(window(qkv, win, v_cut))
            put_window(att, win, cut, mm(p.astype(BF16), values).astype(BF16))

    for g in range(4):
        forward(g)
    at_cols[...] = mm(att[...], columns_16_ref[...]).astype(BF16)
    at_swap = go.remote(at_cols.at[:, not_mine], at_theirs, at.sibling)
    r_y.done()
    xhat[...] = mm(att[...], wo[...].reshape(512, 512))
    for row in range(0, 256, 64):
        rows = slice(row, row + 64)
        normed, scale = norm_parts(xhat[rows])
        xhat[rows] = normed
        xscale[rows] = scale
        ro[rows] = (x_tok[rows].astype(F32) + normed * ng_ref[...]).astype(BF16)
    ro_cols[...] = mm(ro[...], columns_ref[...]).astype(BF16)
    swap = [go.remote(ro_cols.at[:, not_mine], ro_theirs, at.sibling)]
    r_x.done()

    reduced = jnp.zeros((64, 1024), F32)
    for k in range(4):
        reduced += mm(ro[64 * k : 64 * k + 64], wr[k].reshape(512, 1024))
    normed, scale = norm_parts(reduced)
    dred[...] = norm_back(cot_tok[...].astype(F32), normed, scale, mg_ref[...]).astype(BF16)
    swap.append(go.remote(dred, dred_theirs, at.sibling))
    merged = (normed * mg_ref[...]).astype(BF16)
    merged = jnp.concatenate([merged[:, 256 * q : 256 * q + 256] for q in range(4)], 0)
    mb[...] = mm(t_cunmerge_ref[...], merged).astype(BF16)

    def send_back(tile, landing):
        return [
            go.remote(tile.at[pl.ds(128, 112)], landing.at[pl.ds(16, 112)], at.at_tile(1, 0)),
            go.remote(tile.at[pl.ds(112, 16)], landing.at[pl.ds(128, 16)], at.at_tile(0, 1)),
            go.remote(tile.at[pl.ds(240, 16)], landing.at[pl.ds(0, 16)], at.at_tile(1, 1)),
        ]

    for k in range(4):
        dtok[64 * k : 64 * k + 64] = dg(dred[...], wr[k].reshape(512, 1024), NT).astype(BF16)

    for row in range(0, 256, 64):
        rows = slice(row, row + 64)
        got = norm_back(dtok[rows].astype(F32), xhat[rows], xscale[rows], ng_ref[...])
        dproj[rows] = got.astype(BF16)
    dproj_swap = go.remote(dproj, dproj_theirs, at.sibling)
    d_att[...] = dg(dproj[...], wo[...].reshape(512, 512), NT).astype(BF16)

    for copy in swap:
        copy.wait_recv()
    before_a = go.count
    a_sum = Reduce(at, go, fa, *a_bufs)
    z_sum = ReduceZ(at, go, fz, *z_bufs)
    grads = jnp.concatenate([dred[...], dred_theirs[...]], 0)
    for n in range(4):
        k = a_sum.xs[n]
        rows = pl.ds(pl.multiple_of(64 * k, 64), 64)
        tokens = jnp.concatenate([ro_cols[rows, mine], ro_theirs[rows]], 0).T
        for h in range(2):
            cut = slice(512 * h, 512 * h + 512)
            got = mm(tokens, grads[:, cut]).astype(BF16).reshape(4, 64, 512)
            fa[0, k, :, :, cut] = got[:, 0:16]
            fa[1, k, :, :, cut] = got[:, 16:32]
            for low in range(2):
                for y in range(2):
                    start = 256 * y + 128 * low
                    to = slice(256 * h + 128 * y, 256 * h + 128 * y + 128)
                    fz[:, low, k, :, to] = got[:, 32:64, start : start + 128]
        if n == 0:
            a_sum.first_x()
    z_sum.first()
    a_sum.first_y()

    def backward(g):
        cut = slice(g * 128, g * 128 + 128)
        v_cut = slice(g * 128 + 1024, g * 128 + 1152)
        dps = []
        for win in range(4):
            dp = dg(window(d_att, win, cut), spread(window(qkv, win, v_cut)), NT)
            dps.append(dp.astype(BF16).astype(F32))
        alike = split_mm(jnp.concatenate([probs[g, win] * dps[win] for win in range(4)], 0), bd64_ref[...])
        for win in range(4):
            p = probs[g, win]
            ds = (p * (dps[win] - alike[64 * win : 64 * win + 64])).astype(BF16)
            put_window(dqs, win, cut, mm(ds, spread(window(kh, win, cut))))
            put_window(dkh, win, cut, fold(dg(ds, window(qs, win, cut), TN)))
            put_window(dqkv, win, v_cut, fold(dg(p.astype(BF16), window(d_att, win, cut), TN)).astype(BF16))

    for g in range(4):
        backward(g)

    def swap_dqkv(start):
        cut = pl.ds(start, 512)
        return go.remote(dqkv.at[:, cut], dqkv_theirs.at[:, cut], at.sibling)

    dqkv_swap = [swap_dqkv(1024)]
    a_sum.second_x()
    a_sum.second_y()
    z_sum.step(1)
    for start, inverse, grad in ((0, rq, dqs), (512, rk, dkh)):
        for n in range(2):
            cut = slice(256 * n, 256 * n + 256)
            both_cut = slice(start + 256 * n, start + 256 * n + 256)
            for row in range(0, 256, 128):
                rows = slice(row, row + 128)
                inv = inverse[rows, cut]
                unit = qkv[rows, both_cut].astype(F32) * inv
                d_unit = grad[rows, cut]
                if start == 0:
                    d_unit = d_unit * ls_row[:, cut]
                along = split_mm(unit * d_unit, bd32_ref[...])
                along = jnp.where(inv < 1e12, along, 0.0)
                dqkv[rows, both_cut] = (inv * (d_unit - unit * along)).astype(BF16)
        dqkv_swap.append(swap_dqkv(start))
    at_swap.wait_recv()
    at_t[:, 0:256] = at_cols[:, mine].T
    at_t[:, 256:512] = at_theirs[...].T
    dproj_swap.wait_recv()
    d_out = jnp.concatenate([dproj[...], dproj_theirs[...]], 0)
    out = mm(at_t[...], d_out).astype(BF16)
    for y in range(4):
        fb[1, :, :, :, 256 * y + 128 : 256 * y + 256] = out[:, 128 * y : 128 * y + 128].reshape(4, 4, 16, 128)

    merged_back = send_back(mb, ocland)
    d_in = dtok[...].astype(F32) + dg(dqkv[...], wq[...].reshape(512, 1536), NT)
    back[...] = mm(t_unmerge_ref[...], d_in.astype(BF16)).astype(BF16)
    grad_back = send_back(back, oland)

    z_sum.step(2)
    for copy in dqkv_swap:
        copy.wait_recv()
    before_b = go.count
    b_sum = Reduce(at, go, fb, *b_bufs)
    for n in range(4):
        y = b_sum.ys[n]
        cut = lanes(384 * y, 384)
        grads = jnp.concatenate([dqkv[:, cut], dqkv_theirs[:, cut]], 0)
        got = mm(xt[...], grads).astype(BF16)
        fb[0, :, :, :, y_cut(y)] = got[:, 0:256].reshape(4, 4, 16, 256)
        fb[1, :, :, :, lanes(256 * y, 128)] = got[:, 256:384].reshape(4, 4, 16, 128)
    b_sum.first_x()
    b_sum.first_y()
    go.drain(before_a // 2)
    a_sum.third_x()
    a_sum.third_y()
    z_sum.step(3)
    b_sum.second_y()
    b_sum.second_x()
    go.drain(before_b)
    before_c = go.count
    a_sum.fourth(pack_reduce)
    z_sum.fifth()
    b_sum.third_y()
    b_sum.third_x()
    z_sum.sixth()
    b_sum.fourth(pack_qkv_out)
    go.drain(before_c)
    for copy in merged_back + grad_back:
        copy.wait_recv()
    oland[pl.ds(144, 112)] = back[pl.ds(0, 112)]
    ocland[pl.ds(144, 112)] = mb[pl.ds(0, 112)]
    gin_ref[...] = mm(t_unblock_ref[...], oland[...]).astype(BF16).reshape(8, 32, 512)
    got = mm(t_cunblock_ref[...], ocland[...]).astype(BF16)
    for q in range(4):
        merged_ref[:, :, 256 * q : 256 * q + 256] = got[64 * q : 64 * q + 64].reshape(4, 16, 256)
    factor = 1.0 / 256.0
    gr_ref[0:32] = a_sum.fifth() * factor
    gr_ref[32:64] = z_sum.last() * factor
    go.drain()
    total = b_sum.fifth() * factor
    gq_ref[:, 0:128] = total[0:16]
    gq_ref[:, 128:192] = total[16:32, 0:64]
    go_ref[...] = total[16:32, 64:128]


def hand_on(*refs):
    for src, dst in zip(refs[:5], refs[5:]):
        dst[...] = src[...]


def on_device(
    stash_values, scale_exp, w_qkv, w_out, w_reduce, logit_scale, bias_table, rel_index, norm_gain, merge_gain, cotangent
):
    vmem = pl.BlockSpec(memory_space=pltpu.VMEM)
    sems = pltpu.SemaphoreType.DMA
    outputs = (
        jax.ShapeDtypeStruct((4, 16, 1024), BF16),
        jax.ShapeDtypeStruct((8, 32, 512), BF16),
        jax.ShapeDtypeStruct((16, 192), F32),
        jax.ShapeDtypeStruct((16, 64), F32),
        jax.ShapeDtypeStruct((64, 128), F32),
    )
    loads = (
        stash_values, scale_exp, const(T_BLOCK), cotangent, const(T_CBLOCK),
        bias_table.T, rel_index, const(WIN_ORDER), const(ROW_CUT, F32), const(COL_CUT, F32), logit_scale.reshape(1, 16),
        norm_gain.reshape(1, 512), merge_gain.reshape(1, 1024),
        const(T_MERGE), const(T_CMERGE), const(T_BLOCK.T), const(T_MERGE.T), const(T_CBLOCK.T), const(T_CMERGE.T),
        const(COLUMNS_64), const(COLUMNS_16),
        const(same_block(256, 64, 256, 64)), const(same_block(256, 32, 256, 32)), const(same_block(256, 64, 128, 32)),
    )
    tokens = lambda width, kind=BF16: pltpu.VMEM((256, width), kind)
    results = pl.pallas_call(
        block_kernel,
        out_shape=outputs,
        in_specs=[pl.BlockSpec(memory_space=pl.ANY)] * 27,
        out_specs=(vmem,) * 5,
        scratch_shapes=[
            tokens(768), tokens(768), tokens(512), tokens(512), tokens(256),
            pltpu.VMEM((4, 4, 2, 16, 1536), BF16),
            pltpu.VMEM((4, 4, 2, 16, 512), BF16),
            pltpu.VMEM((4, 4, 2, 64, 1024), BF16),
            tokens(512),
            pltpu.VMEM((64, 1024), BF16),
            tokens(1536), tokens(512), tokens(512), tokens(512, F32), tokens(512, F32),
            pltpu.VMEM((4, 4, 64, 256), F32),
            pltpu.VMEM((4, 64, 256), F32),
            pltpu.VMEM((64, 16, 64), F32),
            pltpu.VMEM((16, 256), F32),
            pltpu.VMEM((2, 64, 256), F32),
            tokens(512), tokens(512), tokens(512, F32), tokens(512, F32), tokens(1536),
            tokens(512, F32), tokens(1, F32), tokens(512), tokens(512), tokens(512),
            tokens(512), tokens(512),
            pltpu.VMEM((1, 512), F32),
            tokens(512), tokens(256), tokens(512), tokens(256), tokens(512), tokens(256),
            pltpu.VMEM((64, 1024), BF16),
            pltpu.VMEM((64, 1024), BF16),
            tokens(512), tokens(1536),
            pltpu.VMEM((2, 4, 4, 16, 1024), BF16),
            pltpu.VMEM((4, 2, 4, 32, 512), BF16),
            pltpu.VMEM((2, 4, 4, 16, 1024), BF16),
            tokens(256),
            *[pltpu.VMEM(load.shape, load.dtype) for load in loads],
            *reduce_scratch(16, 32),
            *reduce_scratch(16, 32),
            *Z_SCRATCH,
            sems((COPIES,)),
            sems((COPIES,)),
            sems((32,)),
        ],
        compiler_params=pltpu.CompilerParams(
            collective_id=0, has_side_effects=True, vmem_limit_bytes=60 * 1024 * 1024
        ),
        name="block_forward_backward",
    )(w_qkv, w_out, w_reduce, *loads)
    return pl.pallas_call(
        hand_on,
        out_shape=outputs,
        in_specs=[vmem] * 5,
        out_specs=(vmem,) * 5,
        name="hand_on",
    )(*results)


def solution(mesh):
    tile = P("wide", "narrow", None)
    rows = P("wide", None)
    both = P("wide", "narrow")
    return jax.shard_map(
        on_device,
        mesh=mesh,
        in_specs=(tile, both, rows, rows, rows, P(), P(), P(), P(), P(), tile),
        out_specs=(tile, tile, both, both, both),
        check_vma=False,
    )
```

```python
import jax
import jax.numpy as jnp
import numpy as np
from jax import lax
from jax.experimental import pallas as pl
from jax.experimental.pallas import tpu as pltpu
from jax.sharding import PartitionSpec as P

MESH = pl.DeviceIdType.MESH
F32 = jnp.float32
BF16 = jnp.bfloat16
NT = (((1,), (1,)), ((), ()))
TN = (((0,), (0,)), ((), ()))


def one_hot(sources):
    sources = np.asarray(sources).reshape(-1)
    table = np.zeros((len(sources), len(sources)), np.float32)
    table[np.arange(len(sources)), sources] = 1.0
    return table


def token_tables():
    i, j, r, c = np.meshgrid(*map(np.arange, (2, 8, 4, 4)), indexing="ij")
    block_from_natural = one_hot((4 * i + r) * 32 + 4 * j + c)
    k, win, mr, mc = np.meshgrid(*map(np.arange, (4, 4, 4, 4)), indexing="ij")
    i, r = mr // 2, 2 * (mr % 2) + k % 2
    j, c = 2 * win + mc // 2, 2 * (mc % 2) + k // 2
    merge_from_block = one_hot((i * 8 + j) * 16 + r * 4 + c)
    i, j, q, m = np.meshgrid(*map(np.arange, (2, 8, 4, 4)), indexing="ij")
    cot_block_from_natural = one_hot(q * 64 + (2 * i + m // 2) * 16 + 2 * j + m % 2)
    q, win, mr, mc = np.meshgrid(*map(np.arange, (4, 4, 4, 4)), indexing="ij")
    i, j, m = mr // 2, 2 * win + mc // 2, (mr % 2) * 2 + mc % 2
    cot_merge_from_block = one_hot((i * 8 + j) * 16 + q * 4 + m)
    return (
        block_from_natural,
        merge_from_block,
        cot_block_from_natural,
        cot_merge_from_block,
    )


def window_tables():
    k, mr, mc = np.meshgrid(*map(np.arange, (4, 4, 4)), indexing="ij")
    row, col = (2 * mr + k % 2).reshape(-1), (2 * mc + k // 2).reshape(-1)
    order = one_hot(row * 8 + col)
    row_cut = (row[:, None] >= 4) != (row[None, :] >= 4)
    col_cut = (col[:, None] >= 4) != (col[None, :] >= 4)
    tiled = lambda cut: np.tile(cut.astype(np.float32), (1, 4))
    return order, tiled(row_cut), tiled(col_cut)


def same_block(rows, row_size, cols, col_size):
    return (
        (np.arange(rows) // row_size)[:, None] == (np.arange(cols) // col_size)[None]
    ).astype(np.float32)


T_BLOCK, T_MERGE, T_CBLOCK, T_CMERGE = token_tables()
COLUMNS_64 = one_hot(np.arange(512).reshape(4, 2, 64).transpose(1, 0, 2)).T
COLUMNS_16 = one_hot(np.arange(512).reshape(16, 2, 16).transpose(1, 0, 2)).T
WIN_ORDER, ROW_CUT, COL_CUT = window_tables()


def const(table, dtype=BF16):
    return jnp.asarray(table, dtype)


class Place:
    def __init__(self):
        wide, narrow = lax.axis_index("wide"), lax.axis_index("narrow")
        self.wide, self.narrow = wide, narrow
        self.core = lax.rem(wide, 2)
        self.zh = lax.rem(lax.div(wide, 2), 4)
        self.x = lax.div(wide, 8)
        self.y = lax.div(narrow, 2)
        self.zl = lax.rem(narrow, 2)
        self.z = 2 * self.zh + self.zl
        self.sibling = (wide + 1 - 2 * self.core, narrow)

    def at_x(self, step):
        return ((lax.rem(self.x + step + 4, 4) * 4 + self.zh) * 2 + self.core, self.narrow)

    def at_y(self, step):
        return (self.wide, lax.rem(self.y + step + 4, 4) * 2 + self.zl)

    def at_z(self, step):
        z = lax.rem(self.z + step + 8, 8)
        return ((self.x * 4 + lax.div(z, 2)) * 2 + self.core, self.y * 2 + lax.rem(z, 2))

    def at_tile(self, rows, cols):
        return (lax.rem(self.wide + rows + 32, 32), lax.rem(self.narrow + cols + 8, 8))


class Sender:
    def __init__(self, send_sem, recv_sem, local_sem):
        self.send_sem, self.recv_sem, self.local_sem = send_sem, recv_sem, local_sem
        self.started, self.count, self.local_count, self.drained = [], 0, 0, 0

    def remote(self, src, dst, device):
        copy = pltpu.make_async_remote_copy(
            src_ref=src,
            dst_ref=dst,
            send_sem=self.send_sem.at[self.count],
            recv_sem=self.recv_sem.at[self.count],
            device_id=device,
            device_id_type=MESH,
        )
        self.count += 1
        copy.start()
        self.started.append(copy)
        return copy

    def local(self, src, dst):
        copy = pltpu.make_async_copy(src, dst, self.local_sem.at[self.local_count])
        self.local_count += 1
        copy.start()
        return copy

    def drain(self, until=None):
        until = self.count if until is None else until
        for copy in self.started[self.drained : until]:
            copy.wait_send()
        self.drained = until


def greet(devices):
    barrier = pltpu.get_barrier_semaphore()
    for device in devices:
        pl.semaphore_signal(barrier, inc=1, device_id=device, device_id_type=MESH)


def wait_for(devices):
    pl.semaphore_wait(pltpu.get_barrier_semaphore(), len(devices))


def lanes(start, size):
    return pl.ds(pl.multiple_of(start, 128), size)


def mm(a, b):
    return jnp.dot(a, b, preferred_element_type=F32)


def dg(a, b, dims):
    return lax.dot_general(a, b, dims, preferred_element_type=F32)


def add(*parts):
    total = parts[0].astype(F32)
    for one in parts[1:]:
        total = total + one.astype(F32)
    return total


def split_mm(values, table):
    high = values.astype(BF16)
    low = (values - high.astype(F32)).astype(BF16)
    both = mm(jnp.concatenate([high, low], 0), table)
    return both[: len(values)] + both[len(values) :]


def norm_parts(values):
    centred = values - jnp.mean(values, -1, keepdims=True)
    scale = lax.rsqrt(jnp.mean(centred * centred, -1, keepdims=True) + 1e-05)
    return centred * scale, scale


def norm_back(cot, normed, scale, gain):
    cot = cot * gain
    shared = jnp.mean(cot, -1, keepdims=True) + normed * jnp.mean(cot * normed, -1, keepdims=True)
    return scale * (cot - shared)


EVERY = pl.ds(0, 4)


class Gather:
    def __init__(self, at, go, shard, whole, cut, quarters=False, direct=False):
        self.at, self.go, self.shard, self.whole, self.cut = at, go, shard, whole, cut
        self.quarters, self.direct = quarters, direct
        self.x_left, self.x_right, self.x_far = (lax.rem(at.x + step, 4) for step in (3, 1, 2))
        self.y_left, self.y_right, self.y_far = (lax.rem(at.y + step, 4) for step in (3, 1, 2))
        self.shared = []

    def part(self, xs, zs, y=None):
        y = self.at.y if y is None else y
        return self.whole.at[(xs, zs, self.at.core) + self.cut(y)]

    def move(self, xs, zs, device, y=None):
        ref = self.part(xs, zs, y)
        return self.go.remote(ref, ref, device)

    def share(self, xs, zs, y=None):
        self.shared.append(self.move(xs, zs, self.at.sibling, y))

    def start(self):
        at = self.at
        own, there = self.shard.at[self.cut(at.y)], self.part(at.x, at.zh)
        way = 2 * at.zl - 1
        self.z = [self.go.remote(own, there, at.at_z(way * step)) for step in (1, 2, 3)]
        self.mine = self.go.local(own, there)

    def x1(self):
        at = self.at
        self.mine.wait()
        for copy in self.z:
            copy.wait_recv()
        steps = (1, 2, -1) if self.direct else (1, -1)
        self.x = [self.move(at.x, EVERY, at.at_x(step)) for step in steps]
        if not self.quarters:
            self.share(at.x, EVERY)

    def x2(self):
        at = self.at
        self.x[0].wait_recv()
        far = [self.move(self.x_left, pl.ds(0, 2), at.at_x(1))]
        self.x[1].wait_recv()
        far.append(self.move(self.x_right, pl.ds(2, 2), at.at_x(-1)))
        self.x = far
        if not self.quarters:
            self.share(self.x_left, EVERY)
            self.share(self.x_right, EVERY)

    def x3(self):
        if self.direct and not self.quarters:
            for copy, x in zip(self.x, (self.x_left, self.x_far, self.x_right)):
                copy.wait_recv()
                self.share(x, EVERY)
            return
        for copy in self.x:
            copy.wait_recv()
        if not self.quarters:
            self.share(self.x_far, EVERY)

    def y1(self):
        at = self.at
        self.x3()
        self.y = [self.move(EVERY, EVERY, at.at_y(step)) for step in (1, -1)]
        self.share(EVERY, EVERY)

    def y2(self):
        at = self.at
        self.y[0].wait_recv()
        far = [self.move(pl.ds(0, 2), EVERY, at.at_y(1), self.y_left)]
        self.y[1].wait_recv()
        far.append(self.move(pl.ds(2, 2), EVERY, at.at_y(-1), self.y_right))
        self.y = far
        self.share(EVERY, EVERY, self.y_left)
        self.share(EVERY, EVERY, self.y_right)

    def y3(self):
        for copy in self.y:
            copy.wait_recv()
        self.share(EVERY, EVERY, self.y_far)

    def done(self):
        for copy in self.shared:
            copy.wait_recv()


def y_cut(j):
    return lanes(j * 256, 256)


class Reduce:
    def __init__(self, at, go, m, bx1, bx2, by1, by2, cx, cy, dx, dy, zsend, zland, direct=False):
        self.at, self.go, self.m = at, go, m
        self.bx1, self.bx2, self.by1, self.by2 = bx1, bx2, by1, by2
        self.cx, self.cy = cx, cy
        self.dx, self.dy = dx, dy
        self.zsend, self.zland = zsend, zland
        self.xs = [lax.rem(at.x + step, 4) for step in (2, 1, 3, 0)]
        self.ys = [lax.rem(at.y + step, 4) for step in (2, 1, 3, 0)]
        self.direct, self.parts = direct, 3 if direct else 2
        self.d, self.d_y = [], []
        self.x_left, self.x_right = at.at_x(-1), at.at_x(1)
        self.y_left, self.y_right = at.at_y(-1), at.at_y(1)

    def both(self, src, dst, right, left, step):
        if step == 1:
            pairs = ((src(0, pl.ds(0, 2)), right), (src(0, pl.ds(2, 2)), left))
        else:
            pairs = ((src(1, EVERY), right), (src(2, EVERY), left))
        return [self.go.remote(ref, dst.at[n], device) for n, (ref, device) in enumerate(pairs)]

    def x_src(self, n, part):
        return self.m.at[0, self.xs[n], part]

    def y_src(self, n, part):
        return self.m.at[1, part, :, :, y_cut(self.ys[n])]

    def direct_y(self, n):
        self.d_y = self.d_y + [self.go.remote(self.y_src(n, EVERY), self.by2.at[n], self.at.at_y((2, 1, 3)[n]))]

    def direct_x(self):
        self.d_x = [
            self.go.remote(self.x_src(n, EVERY), self.bx2.at[n], self.at.at_x(step)) for n, step in ((0, 2), (1, 1), (2, 3))
        ]

    def first_x(self):
        self.b_x = self.both(self.x_src, self.bx1, self.x_right, self.x_left, 1)

    def first_y(self):
        self.b_y = self.both(self.y_src, self.by1, self.y_right, self.y_left, 1)

    def second_x(self):
        m, xs = self.m, self.xs
        for copy in self.b_x:
            copy.wait_recv()
        for s in range(2):
            m[0, xs[1], s] = add(m[0, xs[1], s], self.bx1[0, s]).astype(BF16)
            m[0, xs[2], 2 + s] = add(m[0, xs[2], 2 + s], self.bx1[1, s]).astype(BF16)
        self.b_x = self.both(self.x_src, self.bx2, self.x_right, self.x_left, 2)

    def second_y(self):
        m, ys = self.m, self.ys
        for copy in self.b_y:
            copy.wait_recv()
        for s in range(2):
            cut = y_cut(ys[1])
            m[1, s, :, :, cut] = add(m[1, s, :, :, cut], self.by1[0, s]).astype(BF16)
            cut = y_cut(ys[2])
            m[1, 2 + s, :, :, cut] = add(m[1, 2 + s, :, :, cut], self.by1[1, s]).astype(BF16)
        self.b_y = self.both(self.y_src, self.by2, self.y_right, self.y_left, 2)

    def third_x(self):
        at = self.at
        for copy in self.d_x if self.direct else self.b_x:
            copy.wait_recv()
        for s in range(4):
            self.cx[s] = add(self.m[0, at.x, s], *[self.bx2[n, s] for n in range(self.parts)]).astype(BF16)
        for n, step in ((0, 2), (1, 1), (2, 3)):
            src = self.cx.at[:, :, y_cut(self.ys[n])]
            self.d.append(self.go.remote(src, self.dx.at[n], at.at_y(step)))

    def third_y(self):
        at = self.at
        for copy in self.d_y if self.direct else self.b_y:
            copy.wait_recv()
        for s in range(4):
            own = self.m[1, s, :, :, y_cut(at.y)]
            self.cy[s] = add(own, *[self.by2[n, s] for n in range(self.parts)]).astype(BF16)
        for n, step in ((0, 2), (1, 1), (2, 3)):
            self.d.append(self.go.remote(self.cy.at[self.xs[n]], self.dy.at[n], at.at_x(step)))

    def fourth(self, pack):
        for copy in self.d:
            copy.wait_recv()
        for h in range(4):
            a = add(self.cx[h, :, y_cut(self.at.y)], *[self.dx[n, h] for n in range(3)])
            b = add(self.cy[self.at.x, h], *[self.dy[n, h] for n in range(3)])
            for low in range(2):
                self.zsend[h, low] = pack(a, b, low).astype(BF16)
        self.last = []
        for step in range(1, 8):
            z = lax.rem(self.at.z + step, 8)
            src = self.zsend.at[lax.div(z, 2), lax.rem(z, 2)]
            self.last.append(self.go.remote(src, self.zland.at[step - 1], self.at.at_z(step)))

    def fifth(self):
        total = self.zsend[self.at.zh, self.at.zl].astype(F32)
        for step in range(7):
            self.last[step].wait_recv()
            total = total + self.zland[step].astype(F32)
        return total


def pack_reduce(a, b, low):
    cut = slice(128 * low, 128 * low + 128)
    return jnp.concatenate([a[:, cut], b[:, cut]], 0)


def pack_qkv_out(a, b, low):
    if low == 0:
        rows = a[:, 0:128], jnp.concatenate([a[:, 128:192], b[:, 128:192]], 1)
    else:
        rows = (
            jnp.concatenate([a[:, 192:256], b[:, 0:64]], 1),
            jnp.concatenate([b[:, 64:128], b[:, 192:256]], 1),
        )
    return jnp.concatenate(rows, 0)


def reduce_scratch(rows, z_rows, parts):
    return [
        pltpu.VMEM((2, 2, rows, 1024), BF16),
        pltpu.VMEM((parts, 4, rows, 1024), BF16),
        pltpu.VMEM((2, 2, 4, rows, 256), BF16),
        pltpu.VMEM((parts, 4, 4, rows, 256), BF16),
        pltpu.VMEM((4, rows, 1024), BF16),
        pltpu.VMEM((4, 4, rows, 256), BF16),
        pltpu.VMEM((3, 4, rows, 256), BF16),
        pltpu.VMEM((3, 4, rows, 256), BF16),
        pltpu.VMEM((4, 2, z_rows, 128), BF16),
        pltpu.VMEM((7, z_rows, 128), BF16),
    ]


COPIES = 12 + 18 + 3 * 11 + 15 + 8 + 2 * (8 + 6 + 7) + 16


def block_kernel(
    wq_ref, wo_ref, wr_ref, *rest,
):
    loads, rest = rest[:24], rest[24:]
    (
    merged_ref, gin_ref, gq_ref, go_ref, gr_ref,
    blk, land, back, oland, ocland, wq, wo, wr,
    x_tok, cot_tok, qkv, qs, kh, rq, rk, probs, bias, bias_rows, table, mask, att, d_att, dqs, dkh, dqkv,
    xhat, xscale, ro, dproj, dtok, xt, at_t, ls_row, ro_cols, ro_theirs, x_cols, x_theirs, at_cols, at_theirs,
    dred, dred_theirs, dproj_theirs, dqkv_theirs, fa, fb, mb,
    *rest,
    ) = rest
    held, rest = rest[:24], rest[24:]
    (
        stash_ref, exp_ref, t_block_ref, cot_ref, t_cblock_ref,
        table_ref, rel_ref, order_ref, row_cut_ref, col_cut_ref, ls_ref,
        ng_ref, mg_ref, t_merge_ref, t_cmerge_ref, t_unblock_ref, t_unmerge_ref, t_cunblock_ref, t_cunmerge_ref,
        columns_ref, columns_16_ref, bd64_ref, bd32_ref, heads_ref,
    ) = held
    a_bufs, b_bufs, (send_sem, recv_sem, local_sem) = rest[0:10], rest[10:20], rest[20:]
    go = Sender(send_sem, recv_sem, local_sem)
    at = Place()
    c = at.core
    partners = (
        [at.sibling]
        + [at.at_x(step) for step in (1, 2, 3)]
        + [at.at_y(step) for step in (1, 2, 3)]
        + [at.at_z(step) for step in range(1, 8)]
        + [at.at_tile(*step) for step in ((-1, 0), (0, -1), (-1, -1), (1, 0), (0, 1), (1, 1))]
    )
    greet(partners)
    arrivals = [go.local(src, dst) for src, dst in zip(loads, held)]

    def loaded(first, last):
        for copy in arrivals[first:last]:
            copy.wait()

    wait_for(partners)
    all_rows = pl.ds(0, 16)
    q_y = Gather(at, go, wq_ref, wq, lambda y: (all_rows, lanes(512 + 256 * y, 256)), True, True)
    q_x = Gather(at, go, wq_ref, wq, lambda y: (all_rows, pl.ds(0, 512)))
    o_x = Gather(at, go, wo_ref, wo, lambda y: (all_rows, pl.ds(0, 512)))
    r_x = Gather(at, go, wr_ref, wr, lambda y: (pl.ds(0, 64), pl.ds(0, 512)))
    r_y = Gather(at, go, wr_ref, wr, lambda y: (pl.ds(pl.multiple_of(16 * y, 16), 16), pl.ds(512, 512)), True, True)

    q_y.start()
    r_y.start()

    loaded(0, 11)
    table[...] = jnp.zeros((16, 256), F32)
    table[:, 0:225] = 16.0 * jax.nn.sigmoid(table_ref[...])
    by_head = table[...]
    high = by_head.astype(BF16)
    low = (by_head - high.astype(F32)).astype(BF16)
    both = jnp.concatenate([high, low], 0)
    rel = mm(order_ref[...], rel_ref[...].astype(F32).astype(BF16)).astype(BF16)
    rel = dg(rel, order_ref[...], NT).astype(jnp.int32)
    rel = jnp.concatenate([rel[16 * j : 16 * j + 16] for j in range(4)], 1)
    entry = lax.broadcasted_iota(jnp.int32, (256, 256), 0)

    def bias_of(rows):
        for a in rows:
            chosen = jnp.where(entry == rel[a : a + 1], 1.0, 0.0).astype(BF16)
            got = mm(both, chosen)
            got = got[0:16] + got[16:32]
            for j in range(4):
                bias_rows[16 * j + a] = got[:, 64 * j : 64 * j + 64]

    bias_of(range(0, 5))
    o_x.start()

    factor_of = exp_ref[...]
    factor_of = jnp.where(factor_of == -8, 2.0**-8, jnp.where(factor_of == -7, 2.0**-7, 2.0**-6))
    in_window = lax.broadcasted_iota(jnp.int32, (32, 512), 0) // 8
    factor = jnp.zeros((32, 512), F32)
    for w in range(4):
        factor = jnp.where(in_window == w, factor_of[:, w : w + 1], factor)
    inputs = stash_ref[...].astype(F32) * factor[None]
    blk[:, 0:512] = mm(t_block_ref[...], inputs.reshape(256, 512).astype(BF16)).astype(BF16)
    q_x.start()
    q_y.x1()
    cot = cot_ref[...].astype(F32).reshape(64, 1024).astype(BF16)
    cot = jnp.concatenate([cot[:, 256 * q : 256 * q + 256] for q in range(4)], 0)
    blk[:, 512:768] = mm(t_cblock_ref[...], cot).astype(BF16)
    r_y.x1()
    r_x.start()
    q_x.x1()
    q_y.y1()
    o_x.x1()
    halo = [
        go.remote(blk.at[pl.ds(16, 112)], land.at[pl.ds(128, 112)], at.at_tile(-1, 0)),
        go.remote(blk.at[pl.ds(128, 16)], land.at[pl.ds(112, 16)], at.at_tile(0, -1)),
        go.remote(blk.at[pl.ds(0, 16)], land.at[pl.ds(240, 16)], at.at_tile(-1, -1)),
    ]
    bias_of(range(5, 10))
    r_y.y1()
    q_x.x2()
    r_x.x1()
    bias_of(range(10, 16))
    q_y.y2()
    q_x.x3()
    o_x.x2()
    for g in range(4):
        bias[g] = jnp.concatenate([bias_rows[:, 4 * g + h, :] for h in range(4)], 1)
    last_rows = (at.wide == 31).astype(F32)
    last_cols = (at.narrow == 7).astype(F32)
    mask[0] = row_cut_ref[...] * last_rows * -100.0
    mask[1] = jnp.maximum(row_cut_ref[...] * last_rows, col_cut_ref[...] * last_cols) * -100.0
    lane = lax.broadcasted_iota(jnp.int32, (1, 512), 1) // 32
    scales = jnp.zeros((1, 512), F32)
    for h in range(16):
        scales = jnp.where(lane == h, ls_ref[:, h : h + 1], scales)
    ls_row[...] = scales


    for copy in halo:
        copy.wait_recv()
    r_y.y2()
    q_y.y3()
    r_x.x2()
    o_x.x3()
    loaded(11, 24)
    land[pl.ds(0, 112)] = blk[pl.ds(144, 112)]
    x_tok[...] = mm(t_merge_ref[...], land[:, 0:512]).astype(BF16)
    cot = mm(t_cmerge_ref[...], land[:, 512:768]).astype(BF16)
    cot_tok[...] = jnp.concatenate([cot[64 * q : 64 * q + 64] for q in range(4)], 1)
    x_cols[...] = mm(x_tok[...], columns_16_ref[...]).astype(BF16)
    not_mine = lanes(256 * (1 - c), 256)
    mine = lanes(256 * c, 256)
    x_swap = go.remote(x_cols.at[:, not_mine], x_theirs, at.sibling)

    q_x.done()
    q_y.done()

    qkv[...] = mm(x_tok[...], wq[...].reshape(512, 1536)).astype(BF16)
    r_y.y3()
    o_x.done()
    r_x.x3()
    for start, inverse, unit in ((0, rq, qs), (512, rk, kh)):
        for n in range(2):
            cut = slice(256 * n, 256 * n + 256)
            for row in range(0, 256, 128):
                rows = slice(row, row + 128)
                raw = qkv[rows, start + 256 * n : start + 256 * n + 256].astype(F32)
                inv = lax.rsqrt(jnp.maximum(split_mm(raw * raw, bd32_ref[...]), 1e-24))
                inverse[rows, cut] = inv
                raw = raw * inv
                if start == 0:
                    raw = raw * ls_row[:, cut]
                unit[rows, cut] = raw.astype(BF16)
    x_swap.wait_recv()
    xt[:, 0:256] = x_cols[:, mine].T
    xt[:, 256:512] = x_theirs[...].T

    def window(ref, win, cut):
        return jnp.concatenate([ref[pl.ds(64 * k + 16 * win, 16), cut] for k in range(4)], 0)

    def put_window(ref, win, cut, values):
        for k in range(4):
            ref[pl.ds(64 * k + 16 * win, 16), cut] = values[16 * k : 16 * k + 16]

    def spread(rows):
        return jnp.concatenate([rows] * 4, 0) * heads_ref[...]

    def fold(values):
        values = values * heads_ref[...].astype(F32)
        return (values[0:64] + values[64:128]) + (values[128:192] + values[192:256])

    def forward(g):
        cut = slice(g * 128, g * 128 + 128)
        v_cut = slice(g * 128 + 1024, g * 128 + 1152)
        weights = []
        for win in range(4):
            scores = dg(window(qs, win, cut), spread(window(kh, win, cut)), NT)
            weights.append(jnp.exp(scores + bias[g] + mask[1 if win == 3 else 0]))
        totals = split_mm(jnp.concatenate(weights, 0), bd64_ref[...])
        for win in range(4):
            p = weights[win] / totals[64 * win : 64 * win + 64]
            probs[g, win] = p
            values = spread(window(qkv, win, v_cut))
            put_window(att, win, cut, mm(p.astype(BF16), values).astype(BF16))

    for g in range(4):
        forward(g)
    at_cols[...] = mm(att[...], columns_16_ref[...]).astype(BF16)
    at_swap = go.remote(at_cols.at[:, not_mine], at_theirs, at.sibling)
    r_y.done()
    xhat[...] = mm(att[...], wo[...].reshape(512, 512))
    for row in range(0, 256, 64):
        rows = slice(row, row + 64)
        normed, scale = norm_parts(xhat[rows])
        xhat[rows] = normed
        xscale[rows] = scale
        ro[rows] = (x_tok[rows].astype(F32) + normed * ng_ref[...]).astype(BF16)
    ro_cols[...] = mm(ro[...], columns_ref[...]).astype(BF16)
    swap = [go.remote(ro_cols.at[:, not_mine], ro_theirs, at.sibling)]
    r_x.done()

    reduced = jnp.zeros((64, 1024), F32)
    for k in range(4):
        reduced += mm(ro[64 * k : 64 * k + 64], wr[k].reshape(512, 1024))
    normed, scale = norm_parts(reduced)
    dred[...] = norm_back(cot_tok[...].astype(F32), normed, scale, mg_ref[...]).astype(BF16)
    swap.append(go.remote(dred, dred_theirs, at.sibling))
    merged = (normed * mg_ref[...]).astype(BF16)
    merged = jnp.concatenate([merged[:, 256 * q : 256 * q + 256] for q in range(4)], 0)
    mb[...] = mm(t_cunmerge_ref[...], merged).astype(BF16)

    def send_back(tile, landing):
        return [
            go.remote(tile.at[pl.ds(128, 112)], landing.at[pl.ds(16, 112)], at.at_tile(1, 0)),
            go.remote(tile.at[pl.ds(112, 16)], landing.at[pl.ds(128, 16)], at.at_tile(0, 1)),
            go.remote(tile.at[pl.ds(240, 16)], landing.at[pl.ds(0, 16)], at.at_tile(1, 1)),
        ]

    for k in range(4):
        dtok[64 * k : 64 * k + 64] = dg(dred[...], wr[k].reshape(512, 1024), NT).astype(BF16)

    for row in range(0, 256, 64):
        rows = slice(row, row + 64)
        got = norm_back(dtok[rows].astype(F32), xhat[rows], xscale[rows], ng_ref[...])
        dproj[rows] = got.astype(BF16)
    dproj_swap = go.remote(dproj, dproj_theirs, at.sibling)
    d_att[...] = dg(dproj[...], wo[...].reshape(512, 512), NT).astype(BF16)

    for copy in swap:
        copy.wait_recv()
    before_a = go.count
    a_sum = Reduce(at, go, fa, *a_bufs)
    grads = jnp.concatenate([dred[...], dred_theirs[...]], 0)
    for n in range(4):
        k = a_sum.xs[n]
        rows = pl.ds(pl.multiple_of(64 * k, 64), 64)
        tokens = jnp.concatenate([ro_cols[rows, mine], ro_theirs[rows]], 0).T
        for cut in (slice(0, 512), slice(512, 1024)):
            got = mm(tokens, grads[:, cut]).astype(BF16).reshape(4, 64, 512)
            fa[0, k, :, :, cut] = got[:, 0:32]
            fa[1, k, :, :, cut] = got[:, 32:64]
        if n == 0:
            a_sum.first_x()
    a_sum.first_y()

    def backward(g):
        cut = slice(g * 128, g * 128 + 128)
        v_cut = slice(g * 128 + 1024, g * 128 + 1152)
        dps = []
        for win in range(4):
            dp = dg(window(d_att, win, cut), spread(window(qkv, win, v_cut)), NT)
            dps.append(dp.astype(BF16).astype(F32))
        alike = split_mm(jnp.concatenate([probs[g, win] * dps[win] for win in range(4)], 0), bd64_ref[...])
        for win in range(4):
            p = probs[g, win]
            ds = (p * (dps[win] - alike[64 * win : 64 * win + 64])).astype(BF16)
            put_window(dqs, win, cut, mm(ds, spread(window(kh, win, cut))))
            put_window(dkh, win, cut, fold(dg(ds, window(qs, win, cut), TN)))
            put_window(dqkv, win, v_cut, fold(dg(p.astype(BF16), window(d_att, win, cut), TN)).astype(BF16))

    for g in range(4):
        backward(g)

    def swap_dqkv(start):
        cut = pl.ds(start, 512)
        return go.remote(dqkv.at[:, cut], dqkv_theirs.at[:, cut], at.sibling)

    dqkv_swap = [swap_dqkv(1024)]
    a_sum.second_x()
    a_sum.second_y()
    for start, inverse, grad in ((0, rq, dqs), (512, rk, dkh)):
        for n in range(2):
            cut = slice(256 * n, 256 * n + 256)
            both_cut = slice(start + 256 * n, start + 256 * n + 256)
            for row in range(0, 256, 128):
                rows = slice(row, row + 128)
                inv = inverse[rows, cut]
                unit = qkv[rows, both_cut].astype(F32) * inv
                d_unit = grad[rows, cut]
                if start == 0:
                    d_unit = d_unit * ls_row[:, cut]
                along = split_mm(unit * d_unit, bd32_ref[...])
                along = jnp.where(inv < 1e12, along, 0.0)
                dqkv[rows, both_cut] = (inv * (d_unit - unit * along)).astype(BF16)
        dqkv_swap.append(swap_dqkv(start))
    at_swap.wait_recv()
    at_t[:, 0:256] = at_cols[:, mine].T
    at_t[:, 256:512] = at_theirs[...].T
    dproj_swap.wait_recv()
    d_out = jnp.concatenate([dproj[...], dproj_theirs[...]], 0)
    out = mm(at_t[...], d_out).astype(BF16)
    for y in range(4):
        fb[1, :, :, :, 256 * y + 128 : 256 * y + 256] = out[:, 128 * y : 128 * y + 128].reshape(4, 4, 16, 128)

    merged_back = send_back(mb, ocland)
    d_in = dtok[...].astype(F32) + dg(dqkv[...], wq[...].reshape(512, 1536), NT)
    back[...] = mm(t_unmerge_ref[...], d_in.astype(BF16)).astype(BF16)
    grad_back = send_back(back, oland)

    for copy in dqkv_swap:
        copy.wait_recv()
    before_b = go.count
    b_sum = Reduce(at, go, fb, *b_bufs, direct=True)
    for n in range(4):
        y = b_sum.ys[n]
        cut = lanes(384 * y, 384)
        grads = jnp.concatenate([dqkv[:, cut], dqkv_theirs[:, cut]], 0)
        got = mm(xt[...], grads).astype(BF16)
        fb[0, :, :, :, y_cut(y)] = got[:, 0:256].reshape(4, 4, 16, 256)
        fb[1, :, :, :, lanes(256 * y, 128)] = got[:, 256:384].reshape(4, 4, 16, 128)
        if n < 3:
            b_sum.direct_y(n)
    b_sum.direct_x()
    go.drain(before_a // 2)
    a_sum.third_x()
    a_sum.third_y()
    go.drain(before_b)
    before_c = go.count
    b_sum.third_y()
    b_sum.third_x()
    a_sum.fourth(pack_reduce)
    b_sum.fourth(pack_qkv_out)
    go.drain(before_c)
    for copy in merged_back + grad_back:
        copy.wait_recv()
    oland[pl.ds(144, 112)] = back[pl.ds(0, 112)]
    ocland[pl.ds(144, 112)] = mb[pl.ds(0, 112)]
    gin_ref[...] = mm(t_unblock_ref[...], oland[...]).astype(BF16).reshape(8, 32, 512)
    got = mm(t_cunblock_ref[...], ocland[...]).astype(BF16)
    for q in range(4):
        merged_ref[:, :, 256 * q : 256 * q + 256] = got[64 * q : 64 * q + 64].reshape(4, 16, 256)
    factor = 1.0 / 256.0
    gr_ref[...] = a_sum.fifth() * factor
    go.drain()
    total = b_sum.fifth() * factor
    gq_ref[:, 0:128] = total[0:16]
    gq_ref[:, 128:192] = total[16:32, 0:64]
    go_ref[...] = total[16:32, 64:128]


def hand_on(*refs):
    for src, dst in zip(refs[:5], refs[5:]):
        dst[...] = src[...]


def on_device(
    stash_values, scale_exp, w_qkv, w_out, w_reduce, logit_scale, bias_table, rel_index, norm_gain, merge_gain, cotangent
):
    vmem = pl.BlockSpec(memory_space=pltpu.VMEM)
    sems = pltpu.SemaphoreType.DMA
    outputs = (
        jax.ShapeDtypeStruct((4, 16, 1024), BF16),
        jax.ShapeDtypeStruct((8, 32, 512), BF16),
        jax.ShapeDtypeStruct((16, 192), F32),
        jax.ShapeDtypeStruct((16, 64), F32),
        jax.ShapeDtypeStruct((64, 128), F32),
    )
    loads = (
        stash_values, scale_exp, const(T_BLOCK), cotangent, const(T_CBLOCK),
        bias_table.T, rel_index, const(WIN_ORDER), const(ROW_CUT, F32), const(COL_CUT, F32), logit_scale.reshape(1, 16),
        norm_gain.reshape(1, 512), merge_gain.reshape(1, 1024),
        const(T_MERGE), const(T_CMERGE), const(T_BLOCK.T), const(T_MERGE.T), const(T_CBLOCK.T), const(T_CMERGE.T),
        const(COLUMNS_64), const(COLUMNS_16),
        const(same_block(256, 64, 256, 64)), const(same_block(256, 32, 256, 32)), const(same_block(256, 64, 128, 32)),
    )
    tokens = lambda width, kind=BF16: pltpu.VMEM((256, width), kind)
    results = pl.pallas_call(
        block_kernel,
        out_shape=outputs,
        in_specs=[pl.BlockSpec(memory_space=pl.ANY)] * 27,
        out_specs=(vmem,) * 5,
        scratch_shapes=[
            tokens(768), tokens(768), tokens(512), tokens(512), tokens(256),
            pltpu.VMEM((4, 4, 2, 16, 1536), BF16),
            pltpu.VMEM((4, 4, 2, 16, 512), BF16),
            pltpu.VMEM((4, 4, 2, 64, 1024), BF16),
            tokens(512),
            pltpu.VMEM((64, 1024), BF16),
            tokens(1536), tokens(512), tokens(512), tokens(512, F32), tokens(512, F32),
            pltpu.VMEM((4, 4, 64, 256), F32),
            pltpu.VMEM((4, 64, 256), F32),
            pltpu.VMEM((64, 16, 64), F32),
            pltpu.VMEM((16, 256), F32),
            pltpu.VMEM((2, 64, 256), F32),
            tokens(512), tokens(512), tokens(512, F32), tokens(512, F32), tokens(1536),
            tokens(512, F32), tokens(1, F32), tokens(512), tokens(512), tokens(512),
            tokens(512), tokens(512),
            pltpu.VMEM((1, 512), F32),
            tokens(512), tokens(256), tokens(512), tokens(256), tokens(512), tokens(256),
            pltpu.VMEM((64, 1024), BF16),
            pltpu.VMEM((64, 1024), BF16),
            tokens(512), tokens(1536),
            pltpu.VMEM((2, 4, 4, 32, 1024), BF16),
            pltpu.VMEM((2, 4, 4, 16, 1024), BF16),
            tokens(256),
            *[pltpu.VMEM(load.shape, load.dtype) for load in loads],
            *reduce_scratch(32, 64, 2),
            *reduce_scratch(16, 32, 3),
            sems((COPIES,)),
            sems((COPIES,)),
            sems((32,)),
        ],
        compiler_params=pltpu.CompilerParams(
            collective_id=0, has_side_effects=True, vmem_limit_bytes=60 * 1024 * 1024
        ),
        name="block_forward_backward",
    )(w_qkv, w_out, w_reduce, *loads)
    return pl.pallas_call(
        hand_on,
        out_shape=outputs,
        in_specs=[vmem] * 5,
        out_specs=(vmem,) * 5,
        name="hand_on",
    )(*results)


def solution(mesh):
    tile = P("wide", "narrow", None)
    rows = P("wide", None)
    both = P("wide", "narrow")
    return jax.shard_map(
        on_device,
        mesh=mesh,
        in_specs=(tile, both, rows, rows, rows, P(), P(), P(), P(), P(), tile),
        out_specs=(tile, tile, both, both, both),
        check_vma=False,
    )
```

```python
import jax
import jax.numpy as jnp
import numpy as np
from jax import lax
from jax.experimental import pallas as pl
from jax.experimental.pallas import tpu as pltpu
from jax.sharding import PartitionSpec as P

MESH = pl.DeviceIdType.MESH
F32 = jnp.float32
BF16 = jnp.bfloat16
NT = (((1,), (1,)), ((), ()))
TN = (((0,), (0,)), ((), ()))


def one_hot(sources):
    sources = np.asarray(sources).reshape(-1)
    table = np.zeros((len(sources), len(sources)), np.float32)
    table[np.arange(len(sources)), sources] = 1.0
    return table


def token_tables():
    i, j, r, c = np.meshgrid(*map(np.arange, (2, 8, 4, 4)), indexing="ij")
    block_from_natural = one_hot((4 * i + r) * 32 + 4 * j + c)
    k, win, mr, mc = np.meshgrid(*map(np.arange, (4, 4, 4, 4)), indexing="ij")
    i, r = mr // 2, 2 * (mr % 2) + k % 2
    j, c = 2 * win + mc // 2, 2 * (mc % 2) + k // 2
    merge_from_block = one_hot((i * 8 + j) * 16 + r * 4 + c)
    i, j, q, m = np.meshgrid(*map(np.arange, (2, 8, 4, 4)), indexing="ij")
    cot_block_from_natural = one_hot(q * 64 + (2 * i + m // 2) * 16 + 2 * j + m % 2)
    q, win, mr, mc = np.meshgrid(*map(np.arange, (4, 4, 4, 4)), indexing="ij")
    i, j, m = mr // 2, 2 * win + mc // 2, (mr % 2) * 2 + mc % 2
    cot_merge_from_block = one_hot((i * 8 + j) * 16 + q * 4 + m)
    return (
        block_from_natural,
        merge_from_block,
        cot_block_from_natural,
        cot_merge_from_block,
    )


def window_tables():
    k, mr, mc = np.meshgrid(*map(np.arange, (4, 4, 4)), indexing="ij")
    row, col = (2 * mr + k % 2).reshape(-1), (2 * mc + k // 2).reshape(-1)
    order = one_hot(row * 8 + col)
    row_cut = (row[:, None] >= 4) != (row[None, :] >= 4)
    col_cut = (col[:, None] >= 4) != (col[None, :] >= 4)
    tiled = lambda cut: np.tile(cut.astype(np.float32), (1, 4))
    return order, tiled(row_cut), tiled(col_cut)


def same_block(rows, row_size, cols, col_size):
    return (
        (np.arange(rows) // row_size)[:, None] == (np.arange(cols) // col_size)[None]
    ).astype(np.float32)


T_BLOCK, T_MERGE, T_CBLOCK, T_CMERGE = token_tables()
COLUMNS_64 = one_hot(np.arange(512).reshape(4, 2, 64).transpose(1, 0, 2)).T
COLUMNS_16 = one_hot(np.arange(512).reshape(16, 2, 16).transpose(1, 0, 2)).T
WIN_ORDER, ROW_CUT, COL_CUT = window_tables()


def const(table, dtype=BF16):
    return jnp.asarray(table, dtype)


class Place:
    def __init__(self):
        wide, narrow = lax.axis_index("wide"), lax.axis_index("narrow")
        self.wide, self.narrow = wide, narrow
        self.core = lax.rem(wide, 2)
        self.zh = lax.rem(lax.div(wide, 2), 4)
        self.x = lax.div(wide, 8)
        self.y = lax.div(narrow, 2)
        self.zl = lax.rem(narrow, 2)
        self.z = 2 * self.zh + self.zl
        self.sibling = (wide + 1 - 2 * self.core, narrow)

    def at_x(self, step):
        return ((lax.rem(self.x + step + 4, 4) * 4 + self.zh) * 2 + self.core, self.narrow)

    def at_y(self, step):
        return (self.wide, lax.rem(self.y + step + 4, 4) * 2 + self.zl)

    def at_z(self, step):
        z = lax.rem(self.z + step + 8, 8)
        return ((self.x * 4 + lax.div(z, 2)) * 2 + self.core, self.y * 2 + lax.rem(z, 2))

    def at_tile(self, rows, cols):
        return (lax.rem(self.wide + rows + 32, 32), lax.rem(self.narrow + cols + 8, 8))


class Sender:
    def __init__(self, send_sem, recv_sem, local_sem):
        self.send_sem, self.recv_sem, self.local_sem = send_sem, recv_sem, local_sem
        self.started, self.count, self.local_count, self.drained = [], 0, 0, 0

    def remote(self, src, dst, device):
        copy = pltpu.make_async_remote_copy(
            src_ref=src,
            dst_ref=dst,
            send_sem=self.send_sem.at[self.count],
            recv_sem=self.recv_sem.at[self.count],
            device_id=device,
            device_id_type=MESH,
        )
        self.count += 1
        copy.start()
        self.started.append(copy)
        return copy

    def local(self, src, dst):
        copy = pltpu.make_async_copy(src, dst, self.local_sem.at[self.local_count])
        self.local_count += 1
        copy.start()
        return copy

    def drain(self, until=None):
        until = self.count if until is None else until
        for copy in self.started[self.drained : until]:
            copy.wait_send()
        self.drained = until


def greet(devices):
    barrier = pltpu.get_barrier_semaphore()
    for device in devices:
        pl.semaphore_signal(barrier, inc=1, device_id=device, device_id_type=MESH)


def wait_for(devices):
    pl.semaphore_wait(pltpu.get_barrier_semaphore(), len(devices))


def lanes(start, size):
    return pl.ds(pl.multiple_of(start, 128), size)


def mm(a, b):
    return jnp.dot(a, b, preferred_element_type=F32)


def dg(a, b, dims):
    return lax.dot_general(a, b, dims, preferred_element_type=F32)


def add(*parts):
    total = parts[0].astype(F32)
    for one in parts[1:]:
        total = total + one.astype(F32)
    return total


def sums(values, table):
    return mm(values.astype(BF16), table)


def norm_parts(values):
    centred = values - jnp.mean(values, -1, keepdims=True)
    scale = lax.rsqrt(jnp.mean(centred * centred, -1, keepdims=True) + 1e-05)
    return centred * scale, scale


def norm_back(cot, normed, scale, gain):
    cot = cot * gain
    shared = jnp.mean(cot, -1, keepdims=True) + normed * jnp.mean(cot * normed, -1, keepdims=True)
    return scale * (cot - shared)


EVERY = pl.ds(0, 4)


class Gather:
    def __init__(self, at, go, shard, whole, cut, quarters=False, direct=False):
        self.at, self.go, self.shard, self.whole, self.cut = at, go, shard, whole, cut
        self.quarters, self.direct = quarters, direct
        self.x_left, self.x_right, self.x_far = (lax.rem(at.x + step, 4) for step in (3, 1, 2))
        self.y_left, self.y_right, self.y_far = (lax.rem(at.y + step, 4) for step in (3, 1, 2))
        self.shared = []

    def part(self, xs, zs, y=None):
        y = self.at.y if y is None else y
        return self.whole.at[(xs, zs, self.at.core) + self.cut(y)]

    def move(self, xs, zs, device, y=None):
        ref = self.part(xs, zs, y)
        return self.go.remote(ref, ref, device)

    def share(self, xs, zs, y=None):
        self.shared.append(self.move(xs, zs, self.at.sibling, y))

    def start(self):
        at = self.at
        own, there = self.shard.at[self.cut(at.y)], self.part(at.x, at.zh)
        way = 2 * at.zl - 1
        self.z = [self.go.remote(own, there, at.at_z(way * step)) for step in (1, 2, 3)]
        self.mine = self.go.local(own, there)

    def x1(self):
        at = self.at
        self.mine.wait()
        for copy in self.z:
            copy.wait_recv()
        steps = (1, 2, -1) if self.direct else (1, -1)
        self.x = [self.move(at.x, EVERY, at.at_x(step)) for step in steps]
        if not self.quarters:
            self.share(at.x, EVERY)

    def x2(self):
        at = self.at
        self.x[0].wait_recv()
        far = [self.move(self.x_left, pl.ds(0, 2), at.at_x(1))]
        self.x[1].wait_recv()
        far.append(self.move(self.x_right, pl.ds(2, 2), at.at_x(-1)))
        self.x = far
        if not self.quarters:
            self.share(self.x_left, EVERY)
            self.share(self.x_right, EVERY)

    def x3(self):
        if self.direct and not self.quarters:
            for copy, x in zip(self.x, (self.x_left, self.x_far, self.x_right)):
                copy.wait_recv()
                self.share(x, EVERY)
            return
        for copy in self.x:
            copy.wait_recv()
        if not self.quarters:
            self.share(self.x_far, EVERY)

    def y1(self):
        at = self.at
        self.x3()
        self.y = [self.move(EVERY, EVERY, at.at_y(step)) for step in (1, -1)]
        self.share(EVERY, EVERY)

    def y2(self):
        at = self.at
        self.y[0].wait_recv()
        far = [self.move(pl.ds(0, 2), EVERY, at.at_y(1), self.y_left)]
        self.y[1].wait_recv()
        far.append(self.move(pl.ds(2, 2), EVERY, at.at_y(-1), self.y_right))
        self.y = far
        self.share(EVERY, EVERY, self.y_left)
        self.share(EVERY, EVERY, self.y_right)

    def y3(self):
        for copy in self.y:
            copy.wait_recv()
        self.share(EVERY, EVERY, self.y_far)

    def done(self):
        for copy in self.shared:
            copy.wait_recv()


def y_cut(j):
    return lanes(j * 256, 256)


class Reduce:
    def __init__(self, at, go, m, bx2, by2, cx, cy, dx, dy, zsend, zland):
        self.at, self.go, self.m = at, go, m
        self.bx2, self.by2 = bx2, by2
        self.cx, self.cy = cx, cy
        self.dx, self.dy = dx, dy
        self.zsend, self.zland = zsend, zland
        self.xs = [lax.rem(at.x + step, 4) for step in (2, 1, 3, 0)]
        self.ys = [lax.rem(at.y + step, 4) for step in (2, 1, 3, 0)]
        self.d, self.d_x, self.d_y = [], [], []

    def x_src(self, n, part):
        return self.m.at[0, self.xs[n], part]

    def y_src(self, n, part):
        return self.m.at[1, part, :, :, y_cut(self.ys[n])]

    def direct_y(self, n):
        self.d_y = self.d_y + [self.go.remote(self.y_src(n, EVERY), self.by2.at[n], self.at.at_y((2, 1, 3)[n]))]

    def direct_x(self, n):
        self.d_x = self.d_x + [self.go.remote(self.x_src(n, EVERY), self.bx2.at[n], self.at.at_x((2, 1, 3)[n]))]

    def third_x(self):
        at = self.at
        for copy in self.d_x:
            copy.wait_recv()
        for s in range(4):
            self.cx[s] = add(self.m[0, at.x, s], *[self.bx2[n, s] for n in range(3)]).astype(BF16)
        for n, step in ((0, 2), (1, 1), (2, 3)):
            src = self.cx.at[:, :, y_cut(self.ys[n])]
            self.d.append(self.go.remote(src, self.dx.at[n], at.at_y(step)))

    def third_y(self):
        at = self.at
        for copy in self.d_y:
            copy.wait_recv()
        for s in range(4):
            own = self.m[1, s, :, :, y_cut(at.y)]
            self.cy[s] = add(own, *[self.by2[n, s] for n in range(3)]).astype(BF16)
        for n, step in ((0, 2), (1, 1), (2, 3)):
            self.d.append(self.go.remote(self.cy.at[self.xs[n]], self.dy.at[n], at.at_x(step)))

    def fourth(self, pack):
        for copy in self.d:
            copy.wait_recv()
        for h in range(4):
            a = add(self.cx[h, :, y_cut(self.at.y)], *[self.dx[n, h] for n in range(3)])
            b = add(self.cy[self.at.x, h], *[self.dy[n, h] for n in range(3)])
            for low in range(2):
                self.zsend[h, low] = pack(a, b, low).astype(BF16)
        self.last = []
        for step in range(1, 8):
            z = lax.rem(self.at.z + step, 8)
            src = self.zsend.at[lax.div(z, 2), lax.rem(z, 2)]
            self.last.append(self.go.remote(src, self.zland.at[step - 1], self.at.at_z(step)))

    def fifth(self):
        total = self.zsend[self.at.zh, self.at.zl].astype(F32)
        for step in range(7):
            self.last[step].wait_recv()
            total = total + self.zland[step].astype(F32)
        return total


def pack_reduce(a, b, low):
    cut = slice(128 * low, 128 * low + 128)
    return jnp.concatenate([a[:, cut], b[:, cut]], 0)


def pack_qkv_out(a, b, low):
    if low == 0:
        rows = a[:, 0:128], jnp.concatenate([a[:, 128:192], b[:, 128:192]], 1)
    else:
        rows = (
            jnp.concatenate([a[:, 192:256], b[:, 0:64]], 1),
            jnp.concatenate([b[:, 64:128], b[:, 192:256]], 1),
        )
    return jnp.concatenate(rows, 0)


def reduce_scratch(rows, z_rows):
    return [
        pltpu.VMEM((3, 4, rows, 1024), BF16),
        pltpu.VMEM((3, 4, 4, rows, 256), BF16),
        pltpu.VMEM((4, rows, 1024), BF16),
        pltpu.VMEM((4, 4, rows, 256), BF16),
        pltpu.VMEM((3, 4, rows, 256), BF16),
        pltpu.VMEM((3, 4, rows, 256), BF16),
        pltpu.VMEM((4, 2, z_rows, 128), BF16),
        pltpu.VMEM((7, z_rows, 128), BF16),
    ]


COPIES = 12 + 18 + 3 * 11 + 15 + 8 + 2 * (8 + 6 + 7) + 16


def block_kernel(
    wq_ref, wo_ref, wr_ref, *rest,
):
    loads, rest = rest[:24], rest[24:]
    (
    merged_ref, gin_ref, gq_ref, go_ref, gr_ref,
    blk, land, back, oland, ocland, wq, wo, wr,
    x_tok, cot_tok, qkv, qs, kh, rq, rk, probs, masked, bias_rows, table, att, d_att, dqs, dkh, dqkv,
    xhat, xscale, ro, dproj, dtok, xt, at_t, ls_row, ro_cols, ro_theirs, x_cols, x_theirs, at_cols, at_theirs,
    dred, dred_theirs, dproj_theirs, dqkv_theirs, fa, fb, mb,
    *rest,
    ) = rest
    held, rest = rest[:24], rest[24:]
    (
        stash_ref, exp_ref, t_block_ref, cot_ref, t_cblock_ref,
        table_ref, rel_ref, order_ref, row_cut_ref, col_cut_ref, ls_ref,
        ng_ref, mg_ref, t_merge_ref, t_cmerge_ref, t_unblock_ref, t_unmerge_ref, t_cunblock_ref, t_cunmerge_ref,
        columns_ref, columns_16_ref, bd64_ref, bd32_ref, heads_ref,
    ) = held
    a_bufs, b_bufs, (send_sem, recv_sem, local_sem) = rest[0:8], rest[8:16], rest[16:]
    go = Sender(send_sem, recv_sem, local_sem)
    at = Place()
    c = at.core
    partners = (
        [at.sibling]
        + [at.at_x(step) for step in (1, 2, 3)]
        + [at.at_y(step) for step in (1, 2, 3)]
        + [at.at_z(step) for step in range(1, 8)]
        + [at.at_tile(*step) for step in ((-1, 0), (0, -1), (-1, -1), (1, 0), (0, 1), (1, 1))]
    )
    greet(partners)
    arrivals = [go.local(src, dst) for src, dst in zip(loads, held)]

    def loaded(first, last):
        for copy in arrivals[first:last]:
            copy.wait()

    wait_for(partners)
    all_rows = pl.ds(0, 16)
    q_y = Gather(at, go, wq_ref, wq, lambda y: (all_rows, lanes(512 + 256 * y, 256)), True, True)
    q_x = Gather(at, go, wq_ref, wq, lambda y: (all_rows, pl.ds(0, 512)))
    o_x = Gather(at, go, wo_ref, wo, lambda y: (all_rows, pl.ds(0, 512)))
    r_x = Gather(at, go, wr_ref, wr, lambda y: (pl.ds(0, 64), pl.ds(0, 512)))
    r_y = Gather(at, go, wr_ref, wr, lambda y: (pl.ds(pl.multiple_of(16 * y, 16), 16), pl.ds(512, 512)), True, True)

    q_y.start()
    r_y.start()

    loaded(0, 11)
    table[...] = jnp.zeros((16, 256), F32)
    table[:, 0:225] = 16.0 * jax.nn.sigmoid(table_ref[...])
    by_head = table[...]
    high = by_head.astype(BF16)
    low = (by_head - high.astype(F32)).astype(BF16)
    both = jnp.concatenate([high, low], 0)
    rel = mm(order_ref[...], rel_ref[...].astype(F32).astype(BF16)).astype(BF16)
    rel = dg(rel, order_ref[...], NT).astype(jnp.int32)
    rel = jnp.concatenate([rel[16 * j : 16 * j + 16] for j in range(4)], 1)
    entry = lax.broadcasted_iota(jnp.int32, (256, 256), 0)

    def bias_of(rows):
        for a in rows:
            chosen = jnp.where(entry == rel[a : a + 1], 1.0, 0.0).astype(BF16)
            got = mm(both, chosen)
            got = got[0:16] + got[16:32]
            for j in range(4):
                bias_rows[16 * j + a] = got[:, 64 * j : 64 * j + 64]

    bias_of(range(0, 5))
    o_x.start()

    factor_of = exp_ref[...]
    factor_of = jnp.where(factor_of == -8, 2.0**-8, jnp.where(factor_of == -7, 2.0**-7, 2.0**-6))
    in_window = lax.broadcasted_iota(jnp.int32, (32, 512), 0) // 8
    factor = jnp.zeros((32, 512), F32)
    for w in range(4):
        factor = jnp.where(in_window == w, factor_of[:, w : w + 1], factor)
    inputs = stash_ref[...].astype(F32) * factor[None]
    blk[:, 0:512] = mm(t_block_ref[...], inputs.reshape(256, 512).astype(BF16)).astype(BF16)
    q_x.start()
    q_y.x1()
    cot = cot_ref[...].astype(F32).reshape(64, 1024).astype(BF16)
    cot = jnp.concatenate([cot[:, 256 * q : 256 * q + 256] for q in range(4)], 0)
    blk[:, 512:768] = mm(t_cblock_ref[...], cot).astype(BF16)
    r_y.x1()
    r_x.start()
    q_x.x1()
    q_y.y1()
    o_x.x1()
    halo = [
        go.remote(blk.at[pl.ds(16, 112)], land.at[pl.ds(128, 112)], at.at_tile(-1, 0)),
        go.remote(blk.at[pl.ds(128, 16)], land.at[pl.ds(112, 16)], at.at_tile(0, -1)),
        go.remote(blk.at[pl.ds(0, 16)], land.at[pl.ds(240, 16)], at.at_tile(-1, -1)),
    ]
    bias_of(range(5, 10))
    r_y.y1()
    q_x.x2()
    r_x.x1()
    bias_of(range(10, 16))
    q_y.y2()
    q_x.x3()
    o_x.x2()
    last_rows = (at.wide == 31).astype(F32)
    last_cols = (at.narrow == 7).astype(F32)
    mask = row_cut_ref[...] * last_rows * -100.0
    mask_end = jnp.maximum(row_cut_ref[...] * last_rows, col_cut_ref[...] * last_cols) * -100.0
    for g in range(4):
        bias = jnp.concatenate([bias_rows[:, 4 * g + h, :] for h in range(4)], 1)
        masked[0, g] = bias + mask
        masked[1, g] = bias + mask_end
    lane = lax.broadcasted_iota(jnp.int32, (1, 512), 1) // 32
    scales = jnp.zeros((1, 512), F32)
    for h in range(16):
        scales = jnp.where(lane == h, ls_ref[:, h : h + 1], scales)
    ls_row[...] = scales


    for copy in halo:
        copy.wait_recv()
    r_y.y2()
    q_y.y3()
    r_x.x2()
    o_x.x3()
    loaded(11, 24)
    land[pl.ds(0, 112)] = blk[pl.ds(144, 112)]
    x_tok[...] = mm(t_merge_ref[...], land[:, 0:512]).astype(BF16)
    cot = mm(t_cmerge_ref[...], land[:, 512:768]).astype(BF16)
    cot_tok[...] = jnp.concatenate([cot[64 * q : 64 * q + 64] for q in range(4)], 1)
    x_cols[...] = mm(x_tok[...], columns_16_ref[...]).astype(BF16)
    not_mine = lanes(256 * (1 - c), 256)
    mine = lanes(256 * c, 256)
    x_swap = go.remote(x_cols.at[:, not_mine], x_theirs, at.sibling)

    q_x.done()
    q_y.done()

    qkv[...] = mm(x_tok[...], wq[...].reshape(512, 1536)).astype(BF16)
    r_y.y3()
    o_x.done()
    r_x.x3()
    for start, inverse, unit in ((0, rq, qs), (512, rk, kh)):
        for n in range(2):
            cut = slice(256 * n, 256 * n + 256)
            for row in range(0, 256, 128):
                rows = slice(row, row + 128)
                raw = qkv[rows, start + 256 * n : start + 256 * n + 256].astype(F32)
                inv = lax.rsqrt(jnp.maximum(sums(raw * raw, bd32_ref[...]), 1e-24))
                inverse[rows, cut] = inv
                raw = raw * inv
                if start == 0:
                    raw = raw * ls_row[:, cut]
                unit[rows, cut] = raw.astype(BF16)
    x_swap.wait_recv()
    xt[:, 0:256] = x_cols[:, mine].T
    xt[:, 256:512] = x_theirs[...].T

    def window(ref, win, cut):
        return jnp.concatenate([ref[pl.ds(64 * k + 16 * win, 16), cut] for k in range(4)], 0)

    def put_window(ref, win, cut, values):
        for k in range(4):
            ref[pl.ds(64 * k + 16 * win, 16), cut] = values[16 * k : 16 * k + 16]

    def spread(rows):
        return jnp.concatenate([rows] * 4, 0) * heads_ref[...]

    def fold(values):
        values = values * heads_ref[...].astype(F32)
        return (values[0:64] + values[64:128]) + (values[128:192] + values[192:256])

    def forward(g):
        cut = slice(g * 128, g * 128 + 128)
        v_cut = slice(g * 128 + 1024, g * 128 + 1152)
        weights = []
        for win in range(4):
            scores = dg(window(qs, win, cut), spread(window(kh, win, cut)), NT)
            weights.append(jnp.exp(scores + masked[1 if win == 3 else 0, g]))
        totals = sums(jnp.concatenate(weights, 0), bd64_ref[...])
        for win in range(4):
            p = weights[win] / totals[64 * win : 64 * win + 64]
            probs[g, win] = p
            values = spread(window(qkv, win, v_cut))
            put_window(att, win, cut, mm(p.astype(BF16), values).astype(BF16))

    for g in range(4):
        forward(g)
    at_cols[...] = mm(att[...], columns_16_ref[...]).astype(BF16)
    at_swap = go.remote(at_cols.at[:, not_mine], at_theirs, at.sibling)
    r_y.done()
    xhat[...] = mm(att[...], wo[...].reshape(512, 512))
    for row in range(0, 256, 64):
        rows = slice(row, row + 64)
        normed, scale = norm_parts(xhat[rows])
        xhat[rows] = normed
        xscale[rows] = scale
        ro[rows] = (x_tok[rows].astype(F32) + normed * ng_ref[...]).astype(BF16)
    ro_cols[...] = mm(ro[...], columns_ref[...]).astype(BF16)
    swap = [go.remote(ro_cols.at[:, not_mine], ro_theirs, at.sibling)]
    r_x.done()

    reduced = jnp.zeros((64, 1024), F32)
    for k in range(4):
        reduced += mm(ro[64 * k : 64 * k + 64], wr[k].reshape(512, 1024))
    normed, scale = norm_parts(reduced)
    dred[...] = norm_back(cot_tok[...].astype(F32), normed, scale, mg_ref[...]).astype(BF16)
    swap.append(go.remote(dred, dred_theirs, at.sibling))
    merged = (normed * mg_ref[...]).astype(BF16)
    merged = jnp.concatenate([merged[:, 256 * q : 256 * q + 256] for q in range(4)], 0)
    mb[...] = mm(t_cunmerge_ref[...], merged).astype(BF16)

    def send_back(tile, landing):
        return [
            go.remote(tile.at[pl.ds(128, 112)], landing.at[pl.ds(16, 112)], at.at_tile(1, 0)),
            go.remote(tile.at[pl.ds(112, 16)], landing.at[pl.ds(128, 16)], at.at_tile(0, 1)),
            go.remote(tile.at[pl.ds(240, 16)], landing.at[pl.ds(0, 16)], at.at_tile(1, 1)),
        ]

    for k in range(4):
        dtok[64 * k : 64 * k + 64] = dg(dred[...], wr[k].reshape(512, 1024), NT).astype(BF16)

    for row in range(0, 256, 64):
        rows = slice(row, row + 64)
        got = norm_back(dtok[rows].astype(F32), xhat[rows], xscale[rows], ng_ref[...])
        dproj[rows] = got.astype(BF16)
    dproj_swap = go.remote(dproj, dproj_theirs, at.sibling)
    d_att[...] = dg(dproj[...], wo[...].reshape(512, 512), NT).astype(BF16)

    for copy in swap:
        copy.wait_recv()
    before_a = go.count
    a_sum = Reduce(at, go, fa, *a_bufs)
    grads = jnp.concatenate([dred[...], dred_theirs[...]], 0)
    for n in range(4):
        k = a_sum.xs[n]
        rows = pl.ds(pl.multiple_of(64 * k, 64), 64)
        tokens = jnp.concatenate([ro_cols[rows, mine], ro_theirs[rows]], 0).T
        for cut in (slice(0, 512), slice(512, 1024)):
            got = mm(tokens, grads[:, cut]).astype(BF16).reshape(4, 64, 512)
            fa[0, k, :, :, cut] = got[:, 0:32]
            fa[1, k, :, :, cut] = got[:, 32:64]
        if n < 3:
            a_sum.direct_x(n)
    for n in range(3):
        a_sum.direct_y(n)

    def backward(g):
        cut = slice(g * 128, g * 128 + 128)
        v_cut = slice(g * 128 + 1024, g * 128 + 1152)
        dps = []
        for win in range(4):
            dp = dg(window(d_att, win, cut), spread(window(qkv, win, v_cut)), NT)
            dps.append(dp.astype(BF16).astype(F32))
        alike = sums(jnp.concatenate([probs[g, win] * dps[win] for win in range(4)], 0), bd64_ref[...])
        for win in range(4):
            p = probs[g, win]
            ds = (p * (dps[win] - alike[64 * win : 64 * win + 64])).astype(BF16)
            put_window(dqs, win, cut, mm(ds, spread(window(kh, win, cut))))
            put_window(dkh, win, cut, fold(dg(ds, window(qs, win, cut), TN)))
            put_window(dqkv, win, v_cut, fold(dg(p.astype(BF16), window(d_att, win, cut), TN)).astype(BF16))

    for g in range(4):
        backward(g)

    def swap_dqkv(start):
        cut = pl.ds(start, 512)
        return go.remote(dqkv.at[:, cut], dqkv_theirs.at[:, cut], at.sibling)

    dqkv_swap = [swap_dqkv(1024)]
    for start, inverse, grad in ((0, rq, dqs), (512, rk, dkh)):
        for n in range(2):
            cut = slice(256 * n, 256 * n + 256)
            both_cut = slice(start + 256 * n, start + 256 * n + 256)
            for row in range(0, 256, 128):
                rows = slice(row, row + 128)
                inv = inverse[rows, cut]
                unit = qkv[rows, both_cut].astype(F32) * inv
                d_unit = grad[rows, cut]
                if start == 0:
                    d_unit = d_unit * ls_row[:, cut]
                along = sums(unit * d_unit, bd32_ref[...])
                along = jnp.where(inv < 1e12, along, 0.0)
                dqkv[rows, both_cut] = (inv * (d_unit - unit * along)).astype(BF16)
        dqkv_swap.append(swap_dqkv(start))
    at_swap.wait_recv()
    at_t[:, 0:256] = at_cols[:, mine].T
    at_t[:, 256:512] = at_theirs[...].T
    dproj_swap.wait_recv()
    d_out = jnp.concatenate([dproj[...], dproj_theirs[...]], 0)
    out = mm(at_t[...], d_out).astype(BF16)
    for y in range(4):
        fb[1, :, :, :, 256 * y + 128 : 256 * y + 256] = out[:, 128 * y : 128 * y + 128].reshape(4, 4, 16, 128)

    merged_back = send_back(mb, ocland)
    d_in = dtok[...].astype(F32) + dg(dqkv[...], wq[...].reshape(512, 1536), NT)
    back[...] = mm(t_unmerge_ref[...], d_in.astype(BF16)).astype(BF16)
    grad_back = send_back(back, oland)

    for copy in dqkv_swap:
        copy.wait_recv()
    before_b = go.count
    b_sum = Reduce(at, go, fb, *b_bufs)
    for n in range(4):
        y = b_sum.ys[n]
        cut = lanes(384 * y, 384)
        grads = jnp.concatenate([dqkv[:, cut], dqkv_theirs[:, cut]], 0)
        got = mm(xt[...], grads).astype(BF16)
        fb[0, :, :, :, y_cut(y)] = got[:, 0:256].reshape(4, 4, 16, 256)
        fb[1, :, :, :, lanes(256 * y, 128)] = got[:, 256:384].reshape(4, 4, 16, 128)
        if n < 3:
            b_sum.direct_y(n)
    for n in range(3):
        b_sum.direct_x(n)
    go.drain(before_a // 2)
    a_sum.third_x()
    a_sum.third_y()
    go.drain(before_b)
    before_c = go.count
    b_sum.third_y()
    b_sum.third_x()
    a_sum.fourth(pack_reduce)
    b_sum.fourth(pack_qkv_out)
    go.drain(before_c)
    for copy in merged_back + grad_back:
        copy.wait_recv()
    oland[pl.ds(144, 112)] = back[pl.ds(0, 112)]
    ocland[pl.ds(144, 112)] = mb[pl.ds(0, 112)]
    gin_ref[...] = mm(t_unblock_ref[...], oland[...]).astype(BF16).reshape(8, 32, 512)
    got = mm(t_cunblock_ref[...], ocland[...]).astype(BF16)
    for q in range(4):
        merged_ref[:, :, 256 * q : 256 * q + 256] = got[64 * q : 64 * q + 64].reshape(4, 16, 256)
    factor = 1.0 / 256.0
    gr_ref[...] = a_sum.fifth() * factor
    go.drain()
    total = b_sum.fifth() * factor
    gq_ref[:, 0:128] = total[0:16]
    gq_ref[:, 128:192] = total[16:32, 0:64]
    go_ref[...] = total[16:32, 64:128]


def hand_on(*refs):
    for src, dst in zip(refs[:5], refs[5:]):
        dst[...] = src[...]


def on_device(
    stash_values, scale_exp, w_qkv, w_out, w_reduce, logit_scale, bias_table, rel_index, norm_gain, merge_gain, cotangent
):
    vmem = pl.BlockSpec(memory_space=pltpu.VMEM)
    sems = pltpu.SemaphoreType.DMA
    outputs = (
        jax.ShapeDtypeStruct((4, 16, 1024), BF16),
        jax.ShapeDtypeStruct((8, 32, 512), BF16),
        jax.ShapeDtypeStruct((16, 192), F32),
        jax.ShapeDtypeStruct((16, 64), F32),
        jax.ShapeDtypeStruct((64, 128), F32),
    )
    loads = (
        stash_values, scale_exp, const(T_BLOCK), cotangent, const(T_CBLOCK),
        bias_table.T, rel_index, const(WIN_ORDER), const(ROW_CUT, F32), const(COL_CUT, F32), logit_scale.reshape(1, 16),
        norm_gain.reshape(1, 512), merge_gain.reshape(1, 1024),
        const(T_MERGE), const(T_CMERGE), const(T_BLOCK.T), const(T_MERGE.T), const(T_CBLOCK.T), const(T_CMERGE.T),
        const(COLUMNS_64), const(COLUMNS_16),
        const(same_block(256, 64, 256, 64)), const(same_block(256, 32, 256, 32)), const(same_block(256, 64, 128, 32)),
    )
    tokens = lambda width, kind=BF16: pltpu.VMEM((256, width), kind)
    results = pl.pallas_call(
        block_kernel,
        out_shape=outputs,
        in_specs=[pl.BlockSpec(memory_space=pl.ANY)] * 27,
        out_specs=(vmem,) * 5,
        scratch_shapes=[
            tokens(768), tokens(768), tokens(512), tokens(512), tokens(256),
            pltpu.VMEM((4, 4, 2, 16, 1536), BF16),
            pltpu.VMEM((4, 4, 2, 16, 512), BF16),
            pltpu.VMEM((4, 4, 2, 64, 1024), BF16),
            tokens(512),
            pltpu.VMEM((64, 1024), BF16),
            tokens(1536), tokens(512), tokens(512), tokens(512, F32), tokens(512, F32),
            pltpu.VMEM((4, 4, 64, 256), F32),
            pltpu.VMEM((2, 4, 64, 256), F32),
            pltpu.VMEM((64, 16, 64), F32),
            pltpu.VMEM((16, 256), F32),
            tokens(512), tokens(512), tokens(512, F32), tokens(512, F32), tokens(1536),
            tokens(512, F32), tokens(1, F32), tokens(512), tokens(512), tokens(512),
            tokens(512), tokens(512),
            pltpu.VMEM((1, 512), F32),
            tokens(512), tokens(256), tokens(512), tokens(256), tokens(512), tokens(256),
            pltpu.VMEM((64, 1024), BF16),
            pltpu.VMEM((64, 1024), BF16),
            tokens(512), tokens(1536),
            pltpu.VMEM((2, 4, 4, 32, 1024), BF16),
            pltpu.VMEM((2, 4, 4, 16, 1024), BF16),
            tokens(256),
            *[pltpu.VMEM(load.shape, load.dtype) for load in loads],
            *reduce_scratch(32, 64),
            *reduce_scratch(16, 32),
            sems((COPIES,)),
            sems((COPIES,)),
            sems((32,)),
        ],
        compiler_params=pltpu.CompilerParams(
            collective_id=0, has_side_effects=True, vmem_limit_bytes=60 * 1024 * 1024
        ),
        name="block_forward_backward",
    )(w_qkv, w_out, w_reduce, *loads)
    return pl.pallas_call(
        hand_on,
        out_shape=outputs,
        in_specs=[vmem] * 5,
        out_specs=(vmem,) * 5,
        name="hand_on",
    )(*results)


def solution(mesh):
    tile = P("wide", "narrow", None)
    rows = P("wide", None)
    both = P("wide", "narrow")
    return jax.shard_map(
        on_device,
        mesh=mesh,
        in_specs=(tile, both, rows, rows, rows, P(), P(), P(), P(), P(), tile),
        out_specs=(tile, tile, both, both, both),
        check_vma=False,
    )
```

```python
import jax
import jax.numpy as jnp
import numpy as np
from jax import lax
from jax.experimental import pallas as pl
from jax.experimental.pallas import tpu as pltpu
from jax.sharding import PartitionSpec as P

MESH = pl.DeviceIdType.MESH
F32 = jnp.float32
BF16 = jnp.bfloat16
NT = (((1,), (1,)), ((), ()))
TN = (((0,), (0,)), ((), ()))


def one_hot(sources):
    sources = np.asarray(sources).reshape(-1)
    table = np.zeros((len(sources), len(sources)), np.float32)
    table[np.arange(len(sources)), sources] = 1.0
    return table


def token_tables():
    i, j, r, c = np.meshgrid(*map(np.arange, (2, 8, 4, 4)), indexing="ij")
    block_from_natural = one_hot((4 * i + r) * 32 + 4 * j + c)
    k, win, mr, mc = np.meshgrid(*map(np.arange, (4, 4, 4, 4)), indexing="ij")
    i, r = mr // 2, 2 * (mr % 2) + k % 2
    j, c = 2 * win + mc // 2, 2 * (mc % 2) + k // 2
    merge_from_block = one_hot((i * 8 + j) * 16 + r * 4 + c)
    i, j, q, m = np.meshgrid(*map(np.arange, (2, 8, 4, 4)), indexing="ij")
    cot_block_from_natural = one_hot(q * 64 + (2 * i + m // 2) * 16 + 2 * j + m % 2)
    q, win, mr, mc = np.meshgrid(*map(np.arange, (4, 4, 4, 4)), indexing="ij")
    i, j, m = mr // 2, 2 * win + mc // 2, (mr % 2) * 2 + mc % 2
    cot_merge_from_block = one_hot((i * 8 + j) * 16 + q * 4 + m)
    return (
        block_from_natural,
        merge_from_block,
        cot_block_from_natural,
        cot_merge_from_block,
    )


def window_tables():
    k, mr, mc = np.meshgrid(*map(np.arange, (4, 4, 4)), indexing="ij")
    row, col = (2 * mr + k % 2).reshape(-1), (2 * mc + k // 2).reshape(-1)
    order = one_hot(row * 8 + col)
    row_cut = (row[:, None] >= 4) != (row[None, :] >= 4)
    col_cut = (col[:, None] >= 4) != (col[None, :] >= 4)
    tiled = lambda cut: np.tile(cut.astype(np.float32), (1, 4))
    return order, tiled(row_cut), tiled(col_cut)


def same_block(rows, row_size, cols, col_size):
    return (
        (np.arange(rows) // row_size)[:, None] == (np.arange(cols) // col_size)[None]
    ).astype(np.float32)


T_BLOCK, T_MERGE, T_CBLOCK, T_CMERGE = token_tables()
COLUMNS_64 = one_hot(np.arange(512).reshape(4, 2, 64).transpose(1, 0, 2)).T
COLUMNS_16 = one_hot(np.arange(512).reshape(16, 2, 16).transpose(1, 0, 2)).T
WIN_ORDER, ROW_CUT, COL_CUT = window_tables()


def const(table, dtype=BF16):
    return jnp.asarray(table, dtype)


class Place:
    def __init__(self):
        wide, narrow = lax.axis_index("wide"), lax.axis_index("narrow")
        self.wide, self.narrow = wide, narrow
        self.core = lax.rem(wide, 2)
        self.zh = lax.rem(lax.div(wide, 2), 4)
        self.x = lax.div(wide, 8)
        self.y = lax.div(narrow, 2)
        self.zl = lax.rem(narrow, 2)
        self.z = 2 * self.zh + self.zl
        self.sibling = (wide + 1 - 2 * self.core, narrow)
        beside = narrow + 1 - 2 * self.zl
        self.others = (self.sibling, (wide, beside), (self.sibling[0], beside))

    def at_x(self, step):
        return ((lax.rem(self.x + step + 4, 4) * 4 + self.zh) * 2 + self.core, self.narrow)

    def at_y(self, step):
        return (self.wide, lax.rem(self.y + step + 4, 4) * 2 + self.zl)

    def at_z(self, step):
        z = lax.rem(self.z + step + 8, 8)
        return ((self.x * 4 + lax.div(z, 2)) * 2 + self.core, self.y * 2 + lax.rem(z, 2))

    def at_tile(self, rows, cols):
        return (lax.rem(self.wide + rows + 32, 32), lax.rem(self.narrow + cols + 8, 8))


class Sender:
    def __init__(self, send_sem, recv_sem, local_sem):
        self.send_sem, self.recv_sem, self.local_sem = send_sem, recv_sem, local_sem
        self.started, self.count, self.local_count, self.drained = [], 0, 0, 0

    def remote(self, src, dst, device):
        copy = pltpu.make_async_remote_copy(
            src_ref=src,
            dst_ref=dst,
            send_sem=self.send_sem.at[self.count],
            recv_sem=self.recv_sem.at[self.count],
            device_id=device,
            device_id_type=MESH,
        )
        self.count += 1
        copy.start()
        self.started.append(copy)
        return copy

    def local(self, src, dst):
        copy = pltpu.make_async_copy(src, dst, self.local_sem.at[self.local_count])
        self.local_count += 1
        copy.start()
        return copy

    def drain(self, until=None):
        until = self.count if until is None else until
        for copy in self.started[self.drained : until]:
            copy.wait_send()
        self.drained = until


def greet(devices):
    barrier = pltpu.get_barrier_semaphore()
    for device in devices:
        pl.semaphore_signal(barrier, inc=1, device_id=device, device_id_type=MESH)


def wait_for(devices):
    pl.semaphore_wait(pltpu.get_barrier_semaphore(), len(devices))


def lanes(start, size):
    return pl.ds(pl.multiple_of(start, 128), size)


def mm(a, b):
    return jnp.dot(a, b, preferred_element_type=F32)


def dg(a, b, dims):
    return lax.dot_general(a, b, dims, preferred_element_type=F32)


def add(*parts):
    total = parts[0].astype(F32)
    for one in parts[1:]:
        total = total + one.astype(F32)
    return total


def sums(values, table):
    return mm(values.astype(BF16), table)


def norm_parts(values):
    centred = values - jnp.mean(values, -1, keepdims=True)
    scale = lax.rsqrt(jnp.mean(centred * centred, -1, keepdims=True) + 1e-05)
    return centred * scale, scale


def norm_back(cot, normed, scale, gain):
    cot = cot * gain
    shared = jnp.mean(cot, -1, keepdims=True) + normed * jnp.mean(cot * normed, -1, keepdims=True)
    return scale * (cot - shared)


EVERY = pl.ds(0, 4)


class Gather:
    def __init__(self, at, go, shard, whole, cut, quarters=False, direct=False):
        self.at, self.go, self.shard, self.whole, self.cut = at, go, shard, whole, cut
        self.quarters, self.direct = quarters, direct
        self.x_left, self.x_right, self.x_far = (lax.rem(at.x + step, 4) for step in (3, 1, 2))
        self.y_left, self.y_right, self.y_far = (lax.rem(at.y + step, 4) for step in (3, 1, 2))
        self.shared = []

    def part(self, xs, zs, y=None):
        y = self.at.y if y is None else y
        return self.whole.at[(xs, zs, self.at.core) + self.cut(y)]

    def move(self, xs, zs, device, y=None):
        ref = self.part(xs, zs, y)
        return self.go.remote(ref, ref, device)

    def share(self, xs, zs, y=None):
        self.shared.append(self.move(xs, zs, self.at.sibling, y))

    def start(self):
        at = self.at
        own, there = self.shard.at[self.cut(at.y)], self.part(at.x, at.zh)
        way = 2 * at.zl - 1
        self.z = [self.go.remote(own, there, at.at_z(way * step)) for step in (1, 2, 3)]
        self.mine = self.go.local(own, there)

    def x1(self):
        at = self.at
        self.mine.wait()
        for copy in self.z:
            copy.wait_recv()
        steps = (1, 2, -1) if self.direct else (1, -1)
        self.x = [self.move(at.x, EVERY, at.at_x(step)) for step in steps]
        if not self.quarters:
            self.share(at.x, EVERY)

    def x2(self):
        at = self.at
        self.x[0].wait_recv()
        far = [self.move(self.x_left, pl.ds(0, 2), at.at_x(1))]
        self.x[1].wait_recv()
        far.append(self.move(self.x_right, pl.ds(2, 2), at.at_x(-1)))
        self.x = far
        if not self.quarters:
            self.share(self.x_left, EVERY)
            self.share(self.x_right, EVERY)

    def x3(self):
        if self.direct and not self.quarters:
            for copy, x in zip(self.x, (self.x_left, self.x_far, self.x_right)):
                copy.wait_recv()
                self.share(x, EVERY)
            return
        for copy in self.x:
            copy.wait_recv()
        if not self.quarters:
            self.share(self.x_far, EVERY)

    def y1(self):
        at = self.at
        self.x3()
        self.y = [self.move(EVERY, EVERY, at.at_y(step)) for step in (1, -1)]
        self.share(EVERY, EVERY)

    def y2(self):
        at = self.at
        self.y[0].wait_recv()
        far = [self.move(pl.ds(0, 2), EVERY, at.at_y(1), self.y_left)]
        self.y[1].wait_recv()
        far.append(self.move(pl.ds(2, 2), EVERY, at.at_y(-1), self.y_right))
        self.y = far
        self.share(EVERY, EVERY, self.y_left)
        self.share(EVERY, EVERY, self.y_right)

    def y3(self):
        for copy in self.y:
            copy.wait_recv()
        self.share(EVERY, EVERY, self.y_far)

    def done(self):
        for copy in self.shared:
            copy.wait_recv()


class Reduce:
    def __init__(self, at, go, m, bx1, bx2, by1, by2, cx, cy, dx, dy, zsend, zland, width, z_steps, direct=False):
        self.at, self.go, self.m = at, go, m
        self.bx1, self.bx2, self.by1, self.by2 = bx1, bx2, by1, by2
        self.cx, self.cy = cx, cy
        self.dx, self.dy = dx, dy
        self.zsend, self.zland = zsend, zland
        self.width, self.z_steps = width, z_steps
        self.xs = [lax.rem(at.x + step, 4) for step in (2, 1, 3, 0)]
        self.ys = [lax.rem(at.y + step, 4) for step in (2, 1, 3, 0)]
        self.direct, self.parts = direct, 3 if direct else 2
        self.d, self.d_y = [], []
        self.x_left, self.x_right = at.at_x(-1), at.at_x(1)
        self.y_left, self.y_right = at.at_y(-1), at.at_y(1)

    def both(self, src, dst, right, left, step):
        if step == 1:
            pairs = ((src(0, pl.ds(0, 2)), right), (src(0, pl.ds(2, 2)), left))
        else:
            pairs = ((src(1, EVERY), right), (src(2, EVERY), left))
        return [self.go.remote(ref, dst.at[n], device) for n, (ref, device) in enumerate(pairs)]

    def y_cut(self, j):
        return lanes(j * self.width, self.width)

    def x_src(self, n, part):
        return self.m.at[0, self.xs[n], part]

    def y_src(self, n, part):
        return self.m.at[1, part, :, :, self.y_cut(self.ys[n])]

    def direct_y(self, n):
        self.d_y = self.d_y + [self.go.remote(self.y_src(n, EVERY), self.by2.at[n], self.at.at_y((2, 1, 3)[n]))]

    def direct_x(self):
        self.d_x = [
            self.go.remote(self.x_src(n, EVERY), self.bx2.at[n], self.at.at_x(step)) for n, step in ((0, 2), (1, 1), (2, 3))
        ]

    def first_x(self):
        self.b_x = self.both(self.x_src, self.bx1, self.x_right, self.x_left, 1)

    def first_y(self):
        self.b_y = self.both(self.y_src, self.by1, self.y_right, self.y_left, 1)

    def second_x(self):
        m, xs = self.m, self.xs
        for copy in self.b_x:
            copy.wait_recv()
        for s in range(2):
            m[0, xs[1], s] = add(m[0, xs[1], s], self.bx1[0, s]).astype(BF16)
            m[0, xs[2], 2 + s] = add(m[0, xs[2], 2 + s], self.bx1[1, s]).astype(BF16)
        self.b_x = self.both(self.x_src, self.bx2, self.x_right, self.x_left, 2)

    def second_y(self):
        m, ys = self.m, self.ys
        for copy in self.b_y:
            copy.wait_recv()
        for s in range(2):
            cut = self.y_cut(ys[1])
            m[1, s, :, :, cut] = add(m[1, s, :, :, cut], self.by1[0, s]).astype(BF16)
            cut = self.y_cut(ys[2])
            m[1, 2 + s, :, :, cut] = add(m[1, 2 + s, :, :, cut], self.by1[1, s]).astype(BF16)
        self.b_y = self.both(self.y_src, self.by2, self.y_right, self.y_left, 2)

    def third_x(self):
        at = self.at
        for copy in self.d_x if self.direct else self.b_x:
            copy.wait_recv()
        for s in range(4):
            self.cx[s] = add(self.m[0, at.x, s], *[self.bx2[n, s] for n in range(self.parts)]).astype(BF16)
        for n, step in ((0, 2), (1, 1), (2, 3)):
            src = self.cx.at[:, :, self.y_cut(self.ys[n])]
            self.d.append(self.go.remote(src, self.dx.at[n], at.at_y(step)))

    def third_y(self):
        at = self.at
        for copy in self.d_y if self.direct else self.b_y:
            copy.wait_recv()
        for s in range(4):
            own = self.m[1, s, :, :, self.y_cut(at.y)]
            self.cy[s] = add(own, *[self.by2[n, s] for n in range(self.parts)]).astype(BF16)
        for n, step in ((0, 2), (1, 1), (2, 3)):
            self.d.append(self.go.remote(self.cy.at[self.xs[n]], self.dy.at[n], at.at_x(step)))

    def z_slot(self, step):
        z = lax.rem(self.at.z + step, 8)
        return lax.div(z, 2), lax.rem(z, 2) if len(self.z_steps) == 7 else 0

    def fourth(self, pack):
        for copy in self.d:
            copy.wait_recv()
        for h in range(4):
            a = add(self.cx[h, :, self.y_cut(self.at.y)], *[self.dx[n, h] for n in range(3)])
            b = add(self.cy[self.at.x, h], *[self.dy[n, h] for n in range(3)])
            for low in range(2):
                if low == 0 or len(self.z_steps) == 7:
                    self.zsend[h, low] = pack(a, b, low).astype(BF16)
        self.last = []
        for n, step in enumerate(self.z_steps):
            self.last.append(self.go.remote(self.zsend.at[self.z_slot(step)], self.zland.at[n], self.at.at_z(step)))

    def fifth(self):
        total = self.zsend[self.z_slot(0)].astype(F32)
        for n, copy in enumerate(self.last):
            copy.wait_recv()
            total = total + self.zland[n].astype(F32)
        return total


def pack_reduce(a, b, low):
    return jnp.concatenate([a, b], 0)


def pack_qkv_out(a, b, low):
    if low == 0:
        rows = a[:, 0:128], jnp.concatenate([a[:, 128:192], b[:, 128:192]], 1)
    else:
        rows = (
            jnp.concatenate([a[:, 192:256], b[:, 0:64]], 1),
            jnp.concatenate([b[:, 64:128], b[:, 192:256]], 1),
        )
    return jnp.concatenate(rows, 0)


def reduce_scratch(rows, z_rows, parts, width):
    return [
        pltpu.VMEM((2, 2, rows, 4 * width), BF16),
        pltpu.VMEM((parts, 4, rows, 4 * width), BF16),
        pltpu.VMEM((2, 2, 4, rows, width), BF16),
        pltpu.VMEM((parts, 4, 4, rows, width), BF16),
        pltpu.VMEM((4, rows, 4 * width), BF16),
        pltpu.VMEM((4, 4, rows, width), BF16),
        pltpu.VMEM((3, 4, rows, width), BF16),
        pltpu.VMEM((3, 4, rows, width), BF16),
        pltpu.VMEM((4, 2, z_rows, 128), BF16),
        pltpu.VMEM((7, z_rows, 128), BF16),
    ]


COPIES = 12 + 18 + 3 * 11 + 15 + 8 + 2 * (8 + 6 + 7) + 16


def block_kernel(
    wq_ref, wo_ref, wr_ref, *rest,
):
    loads, rest = rest[:24], rest[24:]
    (
    merged_ref, gin_ref, gq_ref, go_ref, gr_ref,
    blk, land, back, oland, ocland, wq, wo, wr,
    x_tok, cot_tok, qkv, qs, kh, rq, rk, probs, masked, bias_rows, table, att, d_att, dqs, dkh, dqkv,
    xhat, xscale, ro, dproj, dtok, xt, at_t, ls_row, ro_cols, ro_theirs, x_cols, x_theirs, at_cols, at_theirs,
    dred, dred_cols, dred_theirs, dproj_theirs, dqkv_theirs, fa, fb, mb,
    *rest,
    ) = rest
    held, rest = rest[:24], rest[24:]
    (
        stash_ref, exp_ref, t_block_ref, cot_ref, t_cblock_ref,
        table_ref, rel_ref, order_ref, row_cut_ref, col_cut_ref, ls_ref,
        ng_ref, mg_ref, t_merge_ref, t_cmerge_ref, t_unblock_ref, t_unmerge_ref, t_cunblock_ref, t_cunmerge_ref,
        columns_ref, columns_16_ref, bd64_ref, bd32_ref, heads_ref,
    ) = held
    a_bufs, b_bufs, (send_sem, recv_sem, local_sem) = rest[0:10], rest[10:20], rest[20:]
    go = Sender(send_sem, recv_sem, local_sem)
    at = Place()
    c = at.core
    partners = (
        [at.sibling, at.others[2]]
        + [at.at_x(step) for step in (1, 2, 3)]
        + [at.at_y(step) for step in (1, 2, 3)]
        + [at.at_z(step) for step in range(1, 8)]
        + [at.at_tile(*step) for step in ((-1, 0), (0, -1), (-1, -1), (1, 0), (0, 1), (1, 1))]
    )
    greet(partners)
    arrivals = [go.local(src, dst) for src, dst in zip(loads, held)]

    def loaded(first, last):
        for copy in arrivals[first:last]:
            copy.wait()

    wait_for(partners)
    all_rows = pl.ds(0, 16)
    q_y = Gather(at, go, wq_ref, wq, lambda y: (all_rows, lanes(512 + 256 * y, 256)), True, True)
    q_x = Gather(at, go, wq_ref, wq, lambda y: (all_rows, pl.ds(0, 512)))
    o_x = Gather(at, go, wo_ref, wo, lambda y: (all_rows, pl.ds(0, 512)))
    r_x = Gather(at, go, wr_ref, wr, lambda y: (pl.ds(0, 64), pl.ds(0, 512)))
    r_y = Gather(at, go, wr_ref, wr, lambda y: (pl.ds(pl.multiple_of(16 * y, 16), 16), pl.ds(512, 512)), True, True)

    q_y.start()
    r_y.start()

    loaded(0, 11)
    table[...] = jnp.zeros((16, 256), F32)
    table[:, 0:225] = 16.0 * jax.nn.sigmoid(table_ref[...])
    by_head = table[...]
    high = by_head.astype(BF16)
    low = (by_head - high.astype(F32)).astype(BF16)
    both = jnp.concatenate([high, low], 0)
    rel = mm(order_ref[...], rel_ref[...].astype(F32).astype(BF16)).astype(BF16)
    rel = dg(rel, order_ref[...], NT).astype(jnp.int32)
    rel = jnp.concatenate([rel[16 * j : 16 * j + 16] for j in range(4)], 1)
    entry = lax.broadcasted_iota(jnp.int32, (256, 256), 0)

    def bias_of(rows):
        for a in rows:
            chosen = jnp.where(entry == rel[a : a + 1], 1.0, 0.0).astype(BF16)
            got = mm(both, chosen)
            got = got[0:16] + got[16:32]
            for j in range(4):
                bias_rows[16 * j + a] = got[:, 64 * j : 64 * j + 64]

    bias_of(range(0, 5))
    o_x.start()

    factor_of = exp_ref[...]
    factor_of = jnp.where(factor_of == -8, 2.0**-8, jnp.where(factor_of == -7, 2.0**-7, 2.0**-6))
    in_window = lax.broadcasted_iota(jnp.int32, (32, 512), 0) // 8
    factor = jnp.zeros((32, 512), F32)
    for w in range(4):
        factor = jnp.where(in_window == w, factor_of[:, w : w + 1], factor)
    inputs = stash_ref[...].astype(F32) * factor[None]
    blk[:, 0:512] = mm(t_block_ref[...], inputs.reshape(256, 512).astype(BF16)).astype(BF16)
    q_x.start()
    q_y.x1()
    cot = cot_ref[...].astype(F32).reshape(64, 1024).astype(BF16)
    cot = jnp.concatenate([cot[:, 256 * q : 256 * q + 256] for q in range(4)], 0)
    blk[:, 512:768] = mm(t_cblock_ref[...], cot).astype(BF16)
    r_y.x1()
    r_x.start()
    q_x.x1()
    q_y.y1()
    o_x.x1()
    halo = [
        go.remote(blk.at[pl.ds(16, 112)], land.at[pl.ds(128, 112)], at.at_tile(-1, 0)),
        go.remote(blk.at[pl.ds(128, 16)], land.at[pl.ds(112, 16)], at.at_tile(0, -1)),
        go.remote(blk.at[pl.ds(0, 16)], land.at[pl.ds(240, 16)], at.at_tile(-1, -1)),
    ]
    bias_of(range(5, 10))
    r_y.y1()
    q_x.x2()
    r_x.x1()
    bias_of(range(10, 16))
    q_y.y2()
    q_x.x3()
    o_x.x2()
    last_rows = (at.wide == 31).astype(F32)
    last_cols = (at.narrow == 7).astype(F32)
    mask = row_cut_ref[...] * last_rows * -100.0
    mask_end = jnp.maximum(row_cut_ref[...] * last_rows, col_cut_ref[...] * last_cols) * -100.0
    for g in range(4):
        bias = jnp.concatenate([bias_rows[:, 4 * g + h, :] for h in range(4)], 1)
        masked[0, g] = bias + mask
        masked[1, g] = bias + mask_end
    lane = lax.broadcasted_iota(jnp.int32, (1, 512), 1) // 32
    scales = jnp.zeros((1, 512), F32)
    for h in range(16):
        scales = jnp.where(lane == h, ls_ref[:, h : h + 1], scales)
    ls_row[...] = scales


    for copy in halo:
        copy.wait_recv()
    r_y.y2()
    q_y.y3()
    r_x.x2()
    o_x.x3()
    loaded(11, 24)
    land[pl.ds(0, 112)] = blk[pl.ds(144, 112)]
    x_tok[...] = mm(t_merge_ref[...], land[:, 0:512]).astype(BF16)
    cot = mm(t_cmerge_ref[...], land[:, 512:768]).astype(BF16)
    cot_tok[...] = jnp.concatenate([cot[64 * q : 64 * q + 64] for q in range(4)], 1)
    x_cols[...] = mm(x_tok[...], columns_16_ref[...]).astype(BF16)
    not_mine = lanes(256 * (1 - c), 256)
    mine = lanes(256 * c, 256)
    x_swap = go.remote(x_cols.at[:, not_mine], x_theirs, at.sibling)

    q_x.done()
    q_y.done()

    qkv[...] = mm(x_tok[...], wq[...].reshape(512, 1536)).astype(BF16)
    r_y.y3()
    o_x.done()
    r_x.x3()
    for start, inverse, unit in ((0, rq, qs), (512, rk, kh)):
        for n in range(2):
            cut = slice(256 * n, 256 * n + 256)
            for row in range(0, 256, 128):
                rows = slice(row, row + 128)
                raw = qkv[rows, start + 256 * n : start + 256 * n + 256].astype(F32)
                inv = lax.rsqrt(jnp.maximum(sums(raw * raw, bd32_ref[...]), 1e-24))
                inverse[rows, cut] = inv
                raw = raw * inv
                if start == 0:
                    raw = raw * ls_row[:, cut]
                unit[rows, cut] = raw.astype(BF16)
    x_swap.wait_recv()
    xt[:, 0:256] = x_cols[:, mine].T
    xt[:, 256:512] = x_theirs[...].T

    def window(ref, win, cut):
        return jnp.concatenate([ref[pl.ds(64 * k + 16 * win, 16), cut] for k in range(4)], 0)

    def put_window(ref, win, cut, values):
        for k in range(4):
            ref[pl.ds(64 * k + 16 * win, 16), cut] = values[16 * k : 16 * k + 16]

    def spread(rows):
        return jnp.concatenate([rows] * 4, 0) * heads_ref[...]

    def fold(values):
        values = values * heads_ref[...].astype(F32)
        return (values[0:64] + values[64:128]) + (values[128:192] + values[192:256])

    def forward(g):
        cut = slice(g * 128, g * 128 + 128)
        v_cut = slice(g * 128 + 1024, g * 128 + 1152)
        weights = []
        for win in range(4):
            scores = dg(window(qs, win, cut), spread(window(kh, win, cut)), NT)
            weights.append(jnp.exp(scores + masked[1 if win == 3 else 0, g]))
        totals = sums(jnp.concatenate(weights, 0), bd64_ref[...])
        for win in range(4):
            p = weights[win] / totals[64 * win : 64 * win + 64]
            probs[g, win] = p
            values = spread(window(qkv, win, v_cut))
            put_window(att, win, cut, mm(p.astype(BF16), values).astype(BF16))

    for g in range(4):
        forward(g)
    at_cols[...] = mm(att[...], columns_16_ref[...]).astype(BF16)
    at_swap = go.remote(at_cols.at[:, not_mine], at_theirs, at.sibling)
    r_y.done()
    xhat[...] = mm(att[...], wo[...].reshape(512, 512))
    for row in range(0, 256, 64):
        rows = slice(row, row + 64)
        normed, scale = norm_parts(xhat[rows])
        xhat[rows] = normed
        xscale[rows] = scale
        ro[rows] = (x_tok[rows].astype(F32) + normed * ng_ref[...]).astype(BF16)
    ro_cols[...] = mm(ro[...], columns_ref[...]).astype(BF16)
    swap = [
        go.remote(ro_cols.at[:, cut], ro_theirs.at[n], device)
        for n, (device, cut) in enumerate(zip(at.others, (not_mine, mine, not_mine)))
    ]
    r_x.done()

    reduced = jnp.zeros((64, 1024), F32)
    for k in range(4):
        reduced += mm(ro[64 * k : 64 * k + 64], wr[k].reshape(512, 1024))
    normed, scale = norm_parts(reduced)
    dred[...] = norm_back(cot_tok[...].astype(F32), normed, scale, mg_ref[...]).astype(BF16)
    for low in range(2):
        for y in range(4):
            to, cut = slice(512 * low + 128 * y, 512 * low + 128 * y + 128), slice(256 * y + 128 * low, 256 * y + 128 * low + 128)
            dred_cols[:, to] = dred[:, cut]
    here, there = lanes(512 * at.zl, 512), lanes(512 * (1 - at.zl), 512)
    for n, (device, cut) in enumerate(zip(at.others, (here, there, there))):
        swap.append(go.remote(dred_cols.at[:, cut], dred_theirs.at[n], device))
    merged = (normed * mg_ref[...]).astype(BF16)
    merged = jnp.concatenate([merged[:, 256 * q : 256 * q + 256] for q in range(4)], 0)
    mb[...] = mm(t_cunmerge_ref[...], merged).astype(BF16)

    def send_back(tile, landing):
        return [
            go.remote(tile.at[pl.ds(128, 112)], landing.at[pl.ds(16, 112)], at.at_tile(1, 0)),
            go.remote(tile.at[pl.ds(112, 16)], landing.at[pl.ds(128, 16)], at.at_tile(0, 1)),
            go.remote(tile.at[pl.ds(240, 16)], landing.at[pl.ds(0, 16)], at.at_tile(1, 1)),
        ]

    for k in range(4):
        dtok[64 * k : 64 * k + 64] = dg(dred[...], wr[k].reshape(512, 1024), NT).astype(BF16)

    for row in range(0, 256, 64):
        rows = slice(row, row + 64)
        got = norm_back(dtok[rows].astype(F32), xhat[rows], xscale[rows], ng_ref[...])
        dproj[rows] = got.astype(BF16)
    dproj_swap = go.remote(dproj, dproj_theirs, at.sibling)
    d_att[...] = dg(dproj[...], wo[...].reshape(512, 512), NT).astype(BF16)

    for copy in swap:
        copy.wait_recv()
    before_a = go.count
    a_sum = Reduce(at, go, fa, *a_bufs, 128, (2, 4, 6))
    grads = jnp.concatenate([dred_cols[:, here]] + [dred_theirs[n] for n in range(3)], 0)
    for n in range(4):
        k = a_sum.xs[n]
        rows = pl.ds(pl.multiple_of(64 * k, 64), 64)
        tokens = jnp.concatenate([ro_cols[rows, mine]] + [ro_theirs[m, rows] for m in range(3)], 0).T
        got = mm(tokens, grads).astype(BF16).reshape(4, 64, 512)
        fa[0, k] = got[:, 0:32]
        fa[1, k] = got[:, 32:64]
        if n == 0:
            a_sum.first_x()
    a_sum.first_y()

    def backward(g):
        cut = slice(g * 128, g * 128 + 128)
        v_cut = slice(g * 128 + 1024, g * 128 + 1152)
        dps = []
        for win in range(4):
            dp = dg(window(d_att, win, cut), spread(window(qkv, win, v_cut)), NT)
            dps.append(dp.astype(BF16).astype(F32))
        alike = sums(jnp.concatenate([probs[g, win] * dps[win] for win in range(4)], 0), bd64_ref[...])
        for win in range(4):
            p = probs[g, win]
            ds = (p * (dps[win] - alike[64 * win : 64 * win + 64])).astype(BF16)
            put_window(dqs, win, cut, mm(ds, spread(window(kh, win, cut))))
            put_window(dkh, win, cut, fold(dg(ds, window(qs, win, cut), TN)))
            put_window(dqkv, win, v_cut, fold(dg(p.astype(BF16), window(d_att, win, cut), TN)).astype(BF16))

    for g in range(4):
        backward(g)

    def swap_dqkv(start):
        cut = pl.ds(start, 512)
        return go.remote(dqkv.at[:, cut], dqkv_theirs.at[:, cut], at.sibling)

    dqkv_swap = [swap_dqkv(1024)]
    a_sum.second_x()
    a_sum.second_y()
    for start, inverse, grad in ((0, rq, dqs), (512, rk, dkh)):
        for n in range(2):
            cut = slice(256 * n, 256 * n + 256)
            both_cut = slice(start + 256 * n, start + 256 * n + 256)
            for row in range(0, 256, 128):
                rows = slice(row, row + 128)
                inv = inverse[rows, cut]
                unit = qkv[rows, both_cut].astype(F32) * inv
                d_unit = grad[rows, cut]
                if start == 0:
                    d_unit = d_unit * ls_row[:, cut]
                along = sums(unit * d_unit, bd32_ref[...])
                along = jnp.where(inv < 1e12, along, 0.0)
                dqkv[rows, both_cut] = (inv * (d_unit - unit * along)).astype(BF16)
        dqkv_swap.append(swap_dqkv(start))
    at_swap.wait_recv()
    at_t[:, 0:256] = at_cols[:, mine].T
    at_t[:, 256:512] = at_theirs[...].T
    dproj_swap.wait_recv()
    d_out = jnp.concatenate([dproj[...], dproj_theirs[...]], 0)
    out = mm(at_t[...], d_out).astype(BF16)
    for y in range(4):
        fb[1, :, :, :, 256 * y + 128 : 256 * y + 256] = out[:, 128 * y : 128 * y + 128].reshape(4, 4, 16, 128)

    merged_back = send_back(mb, ocland)
    d_in = dtok[...].astype(F32) + dg(dqkv[...], wq[...].reshape(512, 1536), NT)
    back[...] = mm(t_unmerge_ref[...], d_in.astype(BF16)).astype(BF16)
    grad_back = send_back(back, oland)

    for copy in dqkv_swap:
        copy.wait_recv()
    before_b = go.count
    b_sum = Reduce(at, go, fb, *b_bufs, 256, tuple(range(1, 8)), direct=True)
    for n in range(4):
        y = b_sum.ys[n]
        cut = lanes(384 * y, 384)
        grads = jnp.concatenate([dqkv[:, cut], dqkv_theirs[:, cut]], 0)
        got = mm(xt[...], grads).astype(BF16)
        fb[0, :, :, :, lanes(256 * y, 256)] = got[:, 0:256].reshape(4, 4, 16, 256)
        fb[1, :, :, :, lanes(256 * y, 128)] = got[:, 256:384].reshape(4, 4, 16, 128)
        if n < 3:
            b_sum.direct_y(n)
    b_sum.direct_x()
    go.drain(before_a // 2)
    a_sum.third_x()
    a_sum.third_y()
    go.drain(before_b)
    before_c = go.count
    b_sum.third_y()
    b_sum.third_x()
    a_sum.fourth(pack_reduce)
    b_sum.fourth(pack_qkv_out)
    go.drain(before_c)
    for copy in merged_back + grad_back:
        copy.wait_recv()
    oland[pl.ds(144, 112)] = back[pl.ds(0, 112)]
    ocland[pl.ds(144, 112)] = mb[pl.ds(0, 112)]
    gin_ref[...] = mm(t_unblock_ref[...], oland[...]).astype(BF16).reshape(8, 32, 512)
    got = mm(t_cunblock_ref[...], ocland[...]).astype(BF16)
    for q in range(4):
        merged_ref[:, :, 256 * q : 256 * q + 256] = got[64 * q : 64 * q + 64].reshape(4, 16, 256)
    factor = 1.0 / 256.0
    gr_ref[...] = a_sum.fifth() * factor
    go.drain()
    total = b_sum.fifth() * factor
    gq_ref[:, 0:128] = total[0:16]
    gq_ref[:, 128:192] = total[16:32, 0:64]
    go_ref[...] = total[16:32, 64:128]


def hand_on(*refs):
    for src, dst in zip(refs[:5], refs[5:]):
        dst[...] = src[...]


def on_device(
    stash_values, scale_exp, w_qkv, w_out, w_reduce, logit_scale, bias_table, rel_index, norm_gain, merge_gain, cotangent
):
    vmem = pl.BlockSpec(memory_space=pltpu.VMEM)
    sems = pltpu.SemaphoreType.DMA
    outputs = (
        jax.ShapeDtypeStruct((4, 16, 1024), BF16),
        jax.ShapeDtypeStruct((8, 32, 512), BF16),
        jax.ShapeDtypeStruct((16, 192), F32),
        jax.ShapeDtypeStruct((16, 64), F32),
        jax.ShapeDtypeStruct((64, 128), F32),
    )
    loads = (
        stash_values, scale_exp, const(T_BLOCK), cotangent, const(T_CBLOCK),
        bias_table.T, rel_index, const(WIN_ORDER), const(ROW_CUT, F32), const(COL_CUT, F32), logit_scale.reshape(1, 16),
        norm_gain.reshape(1, 512), merge_gain.reshape(1, 1024),
        const(T_MERGE), const(T_CMERGE), const(T_BLOCK.T), const(T_MERGE.T), const(T_CBLOCK.T), const(T_CMERGE.T),
        const(COLUMNS_64), const(COLUMNS_16),
        const(same_block(256, 64, 256, 64)), const(same_block(256, 32, 256, 32)), const(same_block(256, 64, 128, 32)),
    )
    tokens = lambda width, kind=BF16: pltpu.VMEM((256, width), kind)
    results = pl.pallas_call(
        block_kernel,
        out_shape=outputs,
        in_specs=[pl.BlockSpec(memory_space=pl.ANY)] * 27,
        out_specs=(vmem,) * 5,
        scratch_shapes=[
            tokens(768), tokens(768), tokens(512), tokens(512), tokens(256),
            pltpu.VMEM((4, 4, 2, 16, 1536), BF16),
            pltpu.VMEM((4, 4, 2, 16, 512), BF16),
            pltpu.VMEM((4, 4, 2, 64, 1024), BF16),
            tokens(512),
            pltpu.VMEM((64, 1024), BF16),
            tokens(1536), tokens(512), tokens(512), tokens(512, F32), tokens(512, F32),
            pltpu.VMEM((4, 4, 64, 256), F32),
            pltpu.VMEM((2, 4, 64, 256), F32),
            pltpu.VMEM((64, 16, 64), F32),
            pltpu.VMEM((16, 256), F32),
            tokens(512), tokens(512), tokens(512, F32), tokens(512, F32), tokens(1536),
            tokens(512, F32), tokens(1, F32), tokens(512), tokens(512), tokens(512),
            tokens(512), tokens(512),
            pltpu.VMEM((1, 512), F32),
            tokens(512),
            pltpu.VMEM((3, 256, 256), BF16),
            tokens(512), tokens(256), tokens(512), tokens(256),
            pltpu.VMEM((64, 1024), BF16),
            pltpu.VMEM((64, 1024), BF16),
            pltpu.VMEM((3, 64, 512), BF16),
            tokens(512), tokens(1536),
            pltpu.VMEM((2, 4, 4, 32, 512), BF16),
            pltpu.VMEM((2, 4, 4, 16, 1024), BF16),
            tokens(256),
            *[pltpu.VMEM(load.shape, load.dtype) for load in loads],
            *reduce_scratch(32, 64, 2, 128),
            *reduce_scratch(16, 32, 3, 256),
            sems((COPIES,)),
            sems((COPIES,)),
            sems((32,)),
        ],
        compiler_params=pltpu.CompilerParams(
            collective_id=0, has_side_effects=True, vmem_limit_bytes=60 * 1024 * 1024
        ),
        name="block_forward_backward",
    )(w_qkv, w_out, w_reduce, *loads)
    return pl.pallas_call(
        hand_on,
        out_shape=outputs,
        in_specs=[vmem] * 5,
        out_specs=(vmem,) * 5,
        name="hand_on",
    )(*results)


def solution(mesh):
    tile = P("wide", "narrow", None)
    rows = P("wide", None)
    both = P("wide", "narrow")
    return jax.shard_map(
        on_device,
        mesh=mesh,
        in_specs=(tile, both, rows, rows, rows, P(), P(), P(), P(), P(), tile),
        out_specs=(tile, tile, both, both, both),
        check_vma=False,
    )
```

```python
import jax
import jax.numpy as jnp
import numpy as np
from jax import lax
from jax.experimental import pallas as pl
from jax.experimental.pallas import tpu as pltpu
from jax.sharding import PartitionSpec as P

MESH = pl.DeviceIdType.MESH
F32 = jnp.float32
BF16 = jnp.bfloat16
NT = (((1,), (1,)), ((), ()))
TN = (((0,), (0,)), ((), ()))


def one_hot(sources):
    sources = np.asarray(sources).reshape(-1)
    table = np.zeros((len(sources), len(sources)), np.float32)
    table[np.arange(len(sources)), sources] = 1.0
    return table


def token_tables():
    i, j, r, c = np.meshgrid(*map(np.arange, (2, 8, 4, 4)), indexing="ij")
    block_from_natural = one_hot((4 * i + r) * 32 + 4 * j + c)
    k, win, mr, mc = np.meshgrid(*map(np.arange, (4, 4, 4, 4)), indexing="ij")
    i, r = mr // 2, 2 * (mr % 2) + k % 2
    j, c = 2 * win + mc // 2, 2 * (mc % 2) + k // 2
    merge_from_block = one_hot((i * 8 + j) * 16 + r * 4 + c)
    i, j, q, m = np.meshgrid(*map(np.arange, (2, 8, 4, 4)), indexing="ij")
    cot_block_from_natural = one_hot(q * 64 + (2 * i + m // 2) * 16 + 2 * j + m % 2)
    q, win, mr, mc = np.meshgrid(*map(np.arange, (4, 4, 4, 4)), indexing="ij")
    i, j, m = mr // 2, 2 * win + mc // 2, (mr % 2) * 2 + mc % 2
    cot_merge_from_block = one_hot((i * 8 + j) * 16 + q * 4 + m)
    return (
        block_from_natural,
        merge_from_block,
        cot_block_from_natural,
        cot_merge_from_block,
    )


def window_tables():
    k, mr, mc = np.meshgrid(*map(np.arange, (4, 4, 4)), indexing="ij")
    row, col = (2 * mr + k % 2).reshape(-1), (2 * mc + k // 2).reshape(-1)
    order = one_hot(row * 8 + col)
    row_cut = (row[:, None] >= 4) != (row[None, :] >= 4)
    col_cut = (col[:, None] >= 4) != (col[None, :] >= 4)
    tiled = lambda cut: np.tile(cut.astype(np.float32), (1, 4))
    return order, tiled(row_cut), tiled(col_cut)


def same_block(rows, row_size, cols, col_size):
    return (
        (np.arange(rows) // row_size)[:, None] == (np.arange(cols) // col_size)[None]
    ).astype(np.float32)


T_BLOCK, T_MERGE, T_CBLOCK, T_CMERGE = token_tables()
COLUMNS_64 = one_hot(np.arange(512).reshape(4, 2, 64).transpose(1, 0, 2)).T
COLUMNS_16 = one_hot(np.arange(512).reshape(16, 2, 16).transpose(1, 0, 2)).T
WIN_ORDER, ROW_CUT, COL_CUT = window_tables()


def const(table, dtype=BF16):
    return jnp.asarray(table, dtype)


class Place:
    def __init__(self):
        wide, narrow = lax.axis_index("wide"), lax.axis_index("narrow")
        self.wide, self.narrow = wide, narrow
        self.core = lax.rem(wide, 2)
        self.zh = lax.rem(lax.div(wide, 2), 4)
        self.x = lax.div(wide, 8)
        self.y = lax.div(narrow, 2)
        self.zl = lax.rem(narrow, 2)
        self.z = 2 * self.zh + self.zl
        self.sibling = (wide + 1 - 2 * self.core, narrow)

    def at_x(self, step):
        return ((lax.rem(self.x + step + 4, 4) * 4 + self.zh) * 2 + self.core, self.narrow)

    def at_y(self, step):
        return (self.wide, lax.rem(self.y + step + 4, 4) * 2 + self.zl)

    def at_z(self, step):
        z = lax.rem(self.z + step + 8, 8)
        return ((self.x * 4 + lax.div(z, 2)) * 2 + self.core, self.y * 2 + lax.rem(z, 2))

    def at_tile(self, rows, cols):
        return (lax.rem(self.wide + rows + 32, 32), lax.rem(self.narrow + cols + 8, 8))


class Sender:
    def __init__(self, send_sem, recv_sem, local_sem):
        self.send_sem, self.recv_sem, self.local_sem = send_sem, recv_sem, local_sem
        self.started, self.count, self.local_count, self.drained = [], 0, 0, 0

    def remote(self, src, dst, device):
        copy = pltpu.make_async_remote_copy(
            src_ref=src,
            dst_ref=dst,
            send_sem=self.send_sem.at[self.count],
            recv_sem=self.recv_sem.at[self.count],
            device_id=device,
            device_id_type=MESH,
        )
        self.count += 1
        copy.start()
        self.started.append(copy)
        return copy

    def local(self, src, dst):
        copy = pltpu.make_async_copy(src, dst, self.local_sem.at[self.local_count])
        self.local_count += 1
        copy.start()
        return copy

    def drain(self, until=None):
        until = self.count if until is None else until
        for copy in self.started[self.drained : until]:
            copy.wait_send()
        self.drained = until


def greet(devices):
    barrier = pltpu.get_barrier_semaphore()
    for device in devices:
        pl.semaphore_signal(barrier, inc=1, device_id=device, device_id_type=MESH)


def wait_for(devices):
    pl.semaphore_wait(pltpu.get_barrier_semaphore(), len(devices))


def lanes(start, size):
    return pl.ds(pl.multiple_of(start, 128), size)


def mm(a, b):
    return jnp.dot(a, b, preferred_element_type=F32)


def dg(a, b, dims):
    return lax.dot_general(a, b, dims, preferred_element_type=F32)


def add(*parts):
    total = parts[0].astype(F32)
    for one in parts[1:]:
        total = total + one.astype(F32)
    return total


def sums(values, table):
    return mm(values.astype(BF16), table)


def norm_parts(values):
    centred = values - jnp.mean(values, -1, keepdims=True)
    scale = lax.rsqrt(jnp.mean(centred * centred, -1, keepdims=True) + 1e-05)
    return centred * scale, scale


def norm_back(cot, normed, scale, gain):
    cot = cot * gain
    shared = jnp.mean(cot, -1, keepdims=True) + normed * jnp.mean(cot * normed, -1, keepdims=True)
    return scale * (cot - shared)


EVERY = pl.ds(0, 4)


class Gather:
    def __init__(self, at, go, shard, whole, cut, quarters=False, direct=False):
        self.at, self.go, self.shard, self.whole, self.cut = at, go, shard, whole, cut
        self.quarters, self.direct = quarters, direct
        self.x_left, self.x_right, self.x_far = (lax.rem(at.x + step, 4) for step in (3, 1, 2))
        self.y_left, self.y_right, self.y_far = (lax.rem(at.y + step, 4) for step in (3, 1, 2))
        self.shared = []

    def part(self, xs, zs, y=None):
        y = self.at.y if y is None else y
        return self.whole.at[(xs, zs, self.at.core) + self.cut(y)]

    def move(self, xs, zs, device, y=None):
        ref = self.part(xs, zs, y)
        return self.go.remote(ref, ref, device)

    def share(self, xs, zs, y=None):
        self.shared.append(self.move(xs, zs, self.at.sibling, y))

    def start(self):
        at = self.at
        own, there = self.shard.at[self.cut(at.y)], self.part(at.x, at.zh)
        way = 2 * at.zl - 1
        self.z = [self.go.remote(own, there, at.at_z(way * step)) for step in (1, 2, 3)]
        self.mine = self.go.local(own, there)

    def x1(self):
        at = self.at
        self.mine.wait()
        for copy in self.z:
            copy.wait_recv()
        steps = (1, 2, -1) if self.direct else (1, -1)
        self.x = [self.move(at.x, EVERY, at.at_x(step)) for step in steps]
        if not self.quarters:
            self.share(at.x, EVERY)

    def x2(self):
        at = self.at
        self.x[0].wait_recv()
        far = [self.move(self.x_left, pl.ds(0, 2), at.at_x(1))]
        self.x[1].wait_recv()
        far.append(self.move(self.x_right, pl.ds(2, 2), at.at_x(-1)))
        self.x = far
        if not self.quarters:
            self.share(self.x_left, EVERY)
            self.share(self.x_right, EVERY)

    def x3(self):
        if self.direct and not self.quarters:
            for copy, x in zip(self.x, (self.x_left, self.x_far, self.x_right)):
                copy.wait_recv()
                self.share(x, EVERY)
            return
        for copy in self.x:
            copy.wait_recv()
        if not self.quarters:
            self.share(self.x_far, EVERY)

    def y1(self):
        at = self.at
        self.x3()
        self.y = [self.move(EVERY, EVERY, at.at_y(step)) for step in (1, -1)]
        self.share(EVERY, EVERY)

    def y2(self):
        at = self.at
        self.y[0].wait_recv()
        far = [self.move(pl.ds(0, 2), EVERY, at.at_y(1), self.y_left)]
        self.y[1].wait_recv()
        far.append(self.move(pl.ds(2, 2), EVERY, at.at_y(-1), self.y_right))
        self.y = far
        self.share(EVERY, EVERY, self.y_left)
        self.share(EVERY, EVERY, self.y_right)

    def y3(self):
        for copy in self.y:
            copy.wait_recv()
        self.share(EVERY, EVERY, self.y_far)

    def done(self):
        for copy in self.shared:
            copy.wait_recv()


def y_cut(j):
    return lanes(j * 256, 256)


class Reduce:
    def __init__(self, at, go, m, bx1, bx2, by1, by2, cx, cy, dx, dy, zsend, zland, direct=False):
        self.at, self.go, self.m = at, go, m
        self.bx1, self.bx2, self.by1, self.by2 = bx1, bx2, by1, by2
        self.cx, self.cy = cx, cy
        self.dx, self.dy = dx, dy
        self.zsend, self.zland = zsend, zland
        self.xs = [lax.rem(at.x + step, 4) for step in (2, 1, 3, 0)]
        self.ys = [lax.rem(at.y + step, 4) for step in (2, 1, 3, 0)]
        self.direct, self.parts = direct, 3 if direct else 2
        self.d, self.d_y = [], []
        self.x_left, self.x_right = at.at_x(-1), at.at_x(1)
        self.y_left, self.y_right = at.at_y(-1), at.at_y(1)

    def both(self, src, dst, right, left, step):
        if step == 1:
            pairs = ((src(0, pl.ds(0, 2)), right), (src(0, pl.ds(2, 2)), left))
        else:
            pairs = ((src(1, EVERY), right), (src(2, EVERY), left))
        return [self.go.remote(ref, dst.at[n], device) for n, (ref, device) in enumerate(pairs)]

    def x_src(self, n, part):
        return self.m.at[0, self.xs[n], part]

    def y_src(self, n, part):
        return self.m.at[1, part, :, :, y_cut(self.ys[n])]

    def direct_y(self, n):
        self.d_y = self.d_y + [self.go.remote(self.y_src(n, EVERY), self.by2.at[n], self.at.at_y((2, 1, 3)[n]))]

    def direct_x(self):
        self.d_x = [
            self.go.remote(self.x_src(n, EVERY), self.bx2.at[n], self.at.at_x(step)) for n, step in ((0, 2), (1, 1), (2, 3))
        ]

    def first_x(self):
        self.b_x = self.both(self.x_src, self.bx1, self.x_right, self.x_left, 1)

    def first_y(self):
        self.b_y = self.both(self.y_src, self.by1, self.y_right, self.y_left, 1)

    def second_x(self):
        m, xs = self.m, self.xs
        for copy in self.b_x:
            copy.wait_recv()
        for s in range(2):
            m[0, xs[1], s] = add(m[0, xs[1], s], self.bx1[0, s]).astype(BF16)
            m[0, xs[2], 2 + s] = add(m[0, xs[2], 2 + s], self.bx1[1, s]).astype(BF16)
        self.b_x = self.both(self.x_src, self.bx2, self.x_right, self.x_left, 2)

    def second_y(self):
        m, ys = self.m, self.ys
        for copy in self.b_y:
            copy.wait_recv()
        for s in range(2):
            cut = y_cut(ys[1])
            m[1, s, :, :, cut] = add(m[1, s, :, :, cut], self.by1[0, s]).astype(BF16)
            cut = y_cut(ys[2])
            m[1, 2 + s, :, :, cut] = add(m[1, 2 + s, :, :, cut], self.by1[1, s]).astype(BF16)
        self.b_y = self.both(self.y_src, self.by2, self.y_right, self.y_left, 2)

    def third_x(self):
        at = self.at
        for copy in self.d_x if self.direct else self.b_x:
            copy.wait_recv()
        for s in range(4):
            self.cx[s] = add(self.m[0, at.x, s], *[self.bx2[n, s] for n in range(self.parts)]).astype(BF16)
        for n, step in ((0, 2), (1, 1), (2, 3)):
            src = self.cx.at[:, :, y_cut(self.ys[n])]
            self.d.append(self.go.remote(src, self.dx.at[n], at.at_y(step)))

    def third_y(self):
        at = self.at
        for copy in self.d_y if self.direct else self.b_y:
            copy.wait_recv()
        for s in range(4):
            own = self.m[1, s, :, :, y_cut(at.y)]
            self.cy[s] = add(own, *[self.by2[n, s] for n in range(self.parts)]).astype(BF16)
        for n, step in ((0, 2), (1, 1), (2, 3)):
            self.d.append(self.go.remote(self.cy.at[self.xs[n]], self.dy.at[n], at.at_x(step)))

    def fourth(self, pack):
        for copy in self.d:
            copy.wait_recv()
        for h in range(4):
            a = add(self.cx[h, :, y_cut(self.at.y)], *[self.dx[n, h] for n in range(3)])
            b = add(self.cy[self.at.x, h], *[self.dy[n, h] for n in range(3)])
            for low in range(2):
                self.zsend[h, low] = pack(a, b, low).astype(BF16)
        self.last = []
        for step in range(1, 8):
            z = lax.rem(self.at.z + step, 8)
            src = self.zsend.at[lax.div(z, 2), lax.rem(z, 2)]
            self.last.append(self.go.remote(src, self.zland.at[step - 1], self.at.at_z(step)))

    def fifth(self):
        total = self.zsend[self.at.zh, self.at.zl].astype(F32)
        for step in range(7):
            self.last[step].wait_recv()
            total = total + self.zland[step].astype(F32)
        return total


def pack_reduce(a, b, low):
    cut = slice(128 * low, 128 * low + 128)
    return jnp.concatenate([a[:, cut], b[:, cut]], 0)


def pack_qkv_out(a, b, low):
    if low == 0:
        rows = a[:, 0:128], jnp.concatenate([a[:, 128:192], b[:, 128:192]], 1)
    else:
        rows = (
            jnp.concatenate([a[:, 192:256], b[:, 0:64]], 1),
            jnp.concatenate([b[:, 64:128], b[:, 192:256]], 1),
        )
    return jnp.concatenate(rows, 0)


def reduce_scratch(rows, z_rows, parts):
    return [
        pltpu.VMEM((2, 2, rows, 1024), BF16),
        pltpu.VMEM((parts, 4, rows, 1024), BF16),
        pltpu.VMEM((2, 2, 4, rows, 256), BF16),
        pltpu.VMEM((parts, 4, 4, rows, 256), BF16),
        pltpu.VMEM((4, rows, 1024), BF16),
        pltpu.VMEM((4, 4, rows, 256), BF16),
        pltpu.VMEM((3, 4, rows, 256), BF16),
        pltpu.VMEM((3, 4, rows, 256), BF16),
        pltpu.VMEM((4, 2, z_rows, 128), BF16),
        pltpu.VMEM((7, z_rows, 128), BF16),
    ]


COPIES = 12 + 18 + 3 * 11 + 15 + 8 + 2 * (8 + 6 + 7) + 16


def block_kernel(
    wq_ref, wo_ref, wr_ref, *rest,
):
    loads, rest = rest[:24], rest[24:]
    (
    merged_ref, gin_ref, gq_ref, go_ref, gr_ref,
    blk, land, back, oland, ocland, wq, wo, wr,
    x_tok, cot_tok, qkv, qs, kh, rq, rk, probs, masked, bias_rows, table, att, d_att, dqs, dkh, dqkv,
    xhat, xscale, ro, dproj, dtok, xt, at_t, ls_row, ro_cols, ro_theirs, x_cols, x_theirs, at_cols, at_theirs,
    dred, dred_theirs, dproj_theirs, dqkv_theirs, fa, fb, mb,
    *rest,
    ) = rest
    held, rest = rest[:24], rest[24:]
    (
        stash_ref, exp_ref, t_block_ref, cot_ref, t_cblock_ref,
        table_ref, rel_ref, order_ref, row_cut_ref, col_cut_ref, ls_ref,
        ng_ref, mg_ref, t_merge_ref, t_cmerge_ref, t_unblock_ref, t_unmerge_ref, t_cunblock_ref, t_cunmerge_ref,
        columns_ref, columns_16_ref, bd64_ref, bd32_ref, heads_ref,
    ) = held
    a_bufs, b_bufs, (send_sem, recv_sem, local_sem) = rest[0:10], rest[10:20], rest[20:]
    go = Sender(send_sem, recv_sem, local_sem)
    at = Place()
    c = at.core
    partners = (
        [at.sibling]
        + [at.at_x(step) for step in (1, 2, 3)]
        + [at.at_y(step) for step in (1, 2, 3)]
        + [at.at_z(step) for step in range(1, 8)]
        + [at.at_tile(*step) for step in ((-1, 0), (0, -1), (-1, -1), (1, 0), (0, 1), (1, 1))]
    )
    greet(partners)
    arrivals = [go.local(src, dst) for src, dst in zip(loads, held)]

    def loaded(first, last):
        for copy in arrivals[first:last]:
            copy.wait()

    wait_for(partners)
    all_rows = pl.ds(0, 16)
    q_y = Gather(at, go, wq_ref, wq, lambda y: (all_rows, lanes(512 + 256 * y, 256)), True, True)
    q_x = Gather(at, go, wq_ref, wq, lambda y: (all_rows, pl.ds(0, 512)))
    o_x = Gather(at, go, wo_ref, wo, lambda y: (all_rows, pl.ds(0, 512)))
    r_x = Gather(at, go, wr_ref, wr, lambda y: (pl.ds(0, 64), pl.ds(0, 512)))
    r_y = Gather(at, go, wr_ref, wr, lambda y: (pl.ds(pl.multiple_of(16 * y, 16), 16), pl.ds(512, 512)), True, True)

    q_y.start()

    def roll(cut):
        return [
            go.remote(blk.at[pl.ds(first, rows), cut], land.at[pl.ds(to, rows), cut], device)
            for first, rows, to, device in (
                (16, 112, 128, at.at_tile(-1, 0)),
                (128, 16, 112, at.at_tile(0, -1)),
                (0, 16, 240, at.at_tile(-1, -1)),
            )
        ]

    loaded(0, 3)
    factor_of = exp_ref[...]
    factor_of = jnp.where(factor_of == -8, 2.0**-8, jnp.where(factor_of == -7, 2.0**-7, 2.0**-6))
    in_window = lax.broadcasted_iota(jnp.int32, (32, 512), 0) // 8
    factor = jnp.zeros((32, 512), F32)
    for w in range(4):
        factor = jnp.where(in_window == w, factor_of[:, w : w + 1], factor)
    inputs = stash_ref[...].astype(F32) * factor[None]
    blk[:, 0:512] = mm(t_block_ref[...], inputs.reshape(256, 512).astype(BF16)).astype(BF16)
    halo = roll(pl.ds(0, 512))
    r_y.start()

    loaded(3, 11)
    table[...] = jnp.zeros((16, 256), F32)
    table[:, 0:225] = 16.0 * jax.nn.sigmoid(table_ref[...])
    by_head = table[...]
    high = by_head.astype(BF16)
    low = (by_head - high.astype(F32)).astype(BF16)
    both = jnp.concatenate([high, low], 0)
    rel = mm(order_ref[...], rel_ref[...].astype(F32).astype(BF16)).astype(BF16)
    rel = dg(rel, order_ref[...], NT).astype(jnp.int32)
    rel = jnp.concatenate([rel[16 * j : 16 * j + 16] for j in range(4)], 1)
    entry = lax.broadcasted_iota(jnp.int32, (256, 256), 0)

    def bias_of(rows):
        for a in rows:
            chosen = jnp.where(entry == rel[a : a + 1], 1.0, 0.0).astype(BF16)
            got = mm(both, chosen)
            got = got[0:16] + got[16:32]
            for j in range(4):
                bias_rows[16 * j + a] = got[:, 64 * j : 64 * j + 64]

    bias_of(range(0, 5))
    o_x.start()

    q_x.start()
    q_y.x1()
    cot = cot_ref[...].astype(F32).reshape(64, 1024).astype(BF16)
    cot = jnp.concatenate([cot[:, 256 * q : 256 * q + 256] for q in range(4)], 0)
    blk[:, 512:768] = mm(t_cblock_ref[...], cot).astype(BF16)
    cot_halo = roll(pl.ds(512, 256))
    r_y.x1()
    r_x.start()
    q_x.x1()
    q_y.y1()
    o_x.x1()
    bias_of(range(5, 10))
    r_y.y1()
    q_x.x2()
    r_x.x1()
    bias_of(range(10, 16))
    q_y.y2()
    q_x.x3()
    o_x.x2()
    last_rows = (at.wide == 31).astype(F32)
    last_cols = (at.narrow == 7).astype(F32)
    mask = row_cut_ref[...] * last_rows * -100.0
    mask_end = jnp.maximum(row_cut_ref[...] * last_rows, col_cut_ref[...] * last_cols) * -100.0
    for g in range(4):
        bias = jnp.concatenate([bias_rows[:, 4 * g + h, :] for h in range(4)], 1)
        masked[0, g] = bias + mask
        masked[1, g] = bias + mask_end
    lane = lax.broadcasted_iota(jnp.int32, (1, 512), 1) // 32
    scales = jnp.zeros((1, 512), F32)
    for h in range(16):
        scales = jnp.where(lane == h, ls_ref[:, h : h + 1], scales)
    ls_row[...] = scales


    for copy in halo:
        copy.wait_recv()
    r_y.y2()
    q_y.y3()
    r_x.x2()
    o_x.x3()
    loaded(11, 24)
    land[pl.ds(0, 112), 0:512] = blk[pl.ds(144, 112), 0:512]
    x_tok[...] = mm(t_merge_ref[...], land[:, 0:512]).astype(BF16)
    x_cols[...] = mm(x_tok[...], columns_16_ref[...]).astype(BF16)
    not_mine = lanes(256 * (1 - c), 256)
    mine = lanes(256 * c, 256)
    x_swap = go.remote(x_cols.at[:, not_mine], x_theirs, at.sibling)

    q_x.done()
    q_y.done()

    qkv[...] = mm(x_tok[...], wq[...].reshape(512, 1536)).astype(BF16)
    r_y.y3()
    o_x.done()
    r_x.x3()
    for start, inverse, unit in ((0, rq, qs), (512, rk, kh)):
        for n in range(2):
            cut = slice(256 * n, 256 * n + 256)
            for row in range(0, 256, 128):
                rows = slice(row, row + 128)
                raw = qkv[rows, start + 256 * n : start + 256 * n + 256].astype(F32)
                inv = lax.rsqrt(jnp.maximum(sums(raw * raw, bd32_ref[...]), 1e-24))
                inverse[rows, cut] = inv
                raw = raw * inv
                if start == 0:
                    raw = raw * ls_row[:, cut]
                unit[rows, cut] = raw.astype(BF16)
    x_swap.wait_recv()
    xt[:, 0:256] = x_cols[:, mine].T
    xt[:, 256:512] = x_theirs[...].T

    def window(ref, win, cut):
        return jnp.concatenate([ref[pl.ds(64 * k + 16 * win, 16), cut] for k in range(4)], 0)

    def put_window(ref, win, cut, values):
        for k in range(4):
            ref[pl.ds(64 * k + 16 * win, 16), cut] = values[16 * k : 16 * k + 16]

    def spread(rows):
        return jnp.concatenate([rows] * 4, 0) * heads_ref[...]

    def fold(values):
        values = values * heads_ref[...].astype(F32)
        return (values[0:64] + values[64:128]) + (values[128:192] + values[192:256])

    def forward(g):
        cut = slice(g * 128, g * 128 + 128)
        v_cut = slice(g * 128 + 1024, g * 128 + 1152)
        weights = []
        for win in range(4):
            scores = dg(window(qs, win, cut), spread(window(kh, win, cut)), NT)
            weights.append(jnp.exp(scores + masked[1 if win == 3 else 0, g]))
        totals = sums(jnp.concatenate(weights, 0), bd64_ref[...])
        for win in range(4):
            p = weights[win] / totals[64 * win : 64 * win + 64]
            probs[g, win] = p
            values = spread(window(qkv, win, v_cut))
            put_window(att, win, cut, mm(p.astype(BF16), values).astype(BF16))

    for g in range(4):
        forward(g)
    at_cols[...] = mm(att[...], columns_16_ref[...]).astype(BF16)
    at_swap = go.remote(at_cols.at[:, not_mine], at_theirs, at.sibling)
    for copy in cot_halo:
        copy.wait_recv()
    land[pl.ds(0, 112), 512:768] = blk[pl.ds(144, 112), 512:768]
    cot = mm(t_cmerge_ref[...], land[:, 512:768]).astype(BF16)
    cot_tok[...] = jnp.concatenate([cot[64 * q : 64 * q + 64] for q in range(4)], 1)
    r_y.done()
    xhat[...] = mm(att[...], wo[...].reshape(512, 512))
    for row in range(0, 256, 64):
        rows = slice(row, row + 64)
        normed, scale = norm_parts(xhat[rows])
        xhat[rows] = normed
        xscale[rows] = scale
        ro[rows] = (x_tok[rows].astype(F32) + normed * ng_ref[...]).astype(BF16)
    ro_cols[...] = mm(ro[...], columns_ref[...]).astype(BF16)
    swap = [go.remote(ro_cols.at[:, not_mine], ro_theirs, at.sibling)]
    r_x.done()

    reduced = jnp.zeros((64, 1024), F32)
    for k in range(4):
        reduced += mm(ro[64 * k : 64 * k + 64], wr[k].reshape(512, 1024))
    normed, scale = norm_parts(reduced)
    dred[...] = norm_back(cot_tok[...].astype(F32), normed, scale, mg_ref[...]).astype(BF16)
    swap.append(go.remote(dred, dred_theirs, at.sibling))
    merged = (normed * mg_ref[...]).astype(BF16)
    merged = jnp.concatenate([merged[:, 256 * q : 256 * q + 256] for q in range(4)], 0)
    mb[...] = mm(t_cunmerge_ref[...], merged).astype(BF16)

    def send_back(tile, landing):
        return [
            go.remote(tile.at[pl.ds(128, 112)], landing.at[pl.ds(16, 112)], at.at_tile(1, 0)),
            go.remote(tile.at[pl.ds(112, 16)], landing.at[pl.ds(128, 16)], at.at_tile(0, 1)),
            go.remote(tile.at[pl.ds(240, 16)], landing.at[pl.ds(0, 16)], at.at_tile(1, 1)),
        ]

    for k in range(4):
        dtok[64 * k : 64 * k + 64] = dg(dred[...], wr[k].reshape(512, 1024), NT).astype(BF16)

    for row in range(0, 256, 64):
        rows = slice(row, row + 64)
        got = norm_back(dtok[rows].astype(F32), xhat[rows], xscale[rows], ng_ref[...])
        dproj[rows] = got.astype(BF16)
    dproj_swap = go.remote(dproj, dproj_theirs, at.sibling)
    d_att[...] = dg(dproj[...], wo[...].reshape(512, 512), NT).astype(BF16)

    for copy in swap:
        copy.wait_recv()
    before_a = go.count
    a_sum = Reduce(at, go, fa, *a_bufs)
    grads = jnp.concatenate([dred[...], dred_theirs[...]], 0)
    for n in range(4):
        k = a_sum.xs[n]
        rows = pl.ds(pl.multiple_of(64 * k, 64), 64)
        tokens = jnp.concatenate([ro_cols[rows, mine], ro_theirs[rows]], 0).T
        for cut in (slice(0, 512), slice(512, 1024)):
            got = mm(tokens, grads[:, cut]).astype(BF16).reshape(4, 64, 512)
            fa[0, k, :, :, cut] = got[:, 0:32]
            fa[1, k, :, :, cut] = got[:, 32:64]
        if n == 0:
            a_sum.first_x()
    a_sum.first_y()

    def backward(g):
        cut = slice(g * 128, g * 128 + 128)
        v_cut = slice(g * 128 + 1024, g * 128 + 1152)
        dps = []
        for win in range(4):
            dp = dg(window(d_att, win, cut), spread(window(qkv, win, v_cut)), NT)
            dps.append(dp.astype(BF16).astype(F32))
        alike = sums(jnp.concatenate([probs[g, win] * dps[win] for win in range(4)], 0), bd64_ref[...])
        for win in range(4):
            p = probs[g, win]
            ds = (p * (dps[win] - alike[64 * win : 64 * win + 64])).astype(BF16)
            put_window(dqs, win, cut, mm(ds, spread(window(kh, win, cut))))
            put_window(dkh, win, cut, fold(dg(ds, window(qs, win, cut), TN)))
            put_window(dqkv, win, v_cut, fold(dg(p.astype(BF16), window(d_att, win, cut), TN)).astype(BF16))

    for g in range(4):
        backward(g)

    def swap_dqkv(start):
        cut = pl.ds(start, 512)
        return go.remote(dqkv.at[:, cut], dqkv_theirs.at[:, cut], at.sibling)

    dqkv_swap = [swap_dqkv(1024)]
    a_sum.second_x()
    a_sum.second_y()
    for start, inverse, grad in ((0, rq, dqs), (512, rk, dkh)):
        for n in range(2):
            cut = slice(256 * n, 256 * n + 256)
            both_cut = slice(start + 256 * n, start + 256 * n + 256)
            for row in range(0, 256, 128):
                rows = slice(row, row + 128)
                inv = inverse[rows, cut]
                unit = qkv[rows, both_cut].astype(F32) * inv
                d_unit = grad[rows, cut]
                if start == 0:
                    d_unit = d_unit * ls_row[:, cut]
                along = sums(unit * d_unit, bd32_ref[...])
                along = jnp.where(inv < 1e12, along, 0.0)
                dqkv[rows, both_cut] = (inv * (d_unit - unit * along)).astype(BF16)
        dqkv_swap.append(swap_dqkv(start))
    at_swap.wait_recv()
    at_t[:, 0:256] = at_cols[:, mine].T
    at_t[:, 256:512] = at_theirs[...].T
    dproj_swap.wait_recv()
    d_out = jnp.concatenate([dproj[...], dproj_theirs[...]], 0)
    out = mm(at_t[...], d_out).astype(BF16)
    for y in range(4):
        fb[1, :, :, :, 256 * y + 128 : 256 * y + 256] = out[:, 128 * y : 128 * y + 128].reshape(4, 4, 16, 128)

    merged_back = send_back(mb, ocland)
    d_in = dtok[...].astype(F32) + dg(dqkv[...], wq[...].reshape(512, 1536), NT)
    back[...] = mm(t_unmerge_ref[...], d_in.astype(BF16)).astype(BF16)
    grad_back = send_back(back, oland)

    for copy in dqkv_swap:
        copy.wait_recv()
    before_b = go.count
    b_sum = Reduce(at, go, fb, *b_bufs, direct=True)
    for n in range(4):
        y = b_sum.ys[n]
        cut = lanes(384 * y, 384)
        grads = jnp.concatenate([dqkv[:, cut], dqkv_theirs[:, cut]], 0)
        got = mm(xt[...], grads).astype(BF16)
        fb[0, :, :, :, y_cut(y)] = got[:, 0:256].reshape(4, 4, 16, 256)
        fb[1, :, :, :, lanes(256 * y, 128)] = got[:, 256:384].reshape(4, 4, 16, 128)
        if n < 3:
            b_sum.direct_y(n)
    b_sum.direct_x()
    go.drain(before_a // 2)
    a_sum.third_x()
    a_sum.third_y()
    go.drain(before_b)
    before_c = go.count
    b_sum.third_y()
    b_sum.third_x()
    a_sum.fourth(pack_reduce)
    b_sum.fourth(pack_qkv_out)
    go.drain(before_c)
    for copy in merged_back + grad_back:
        copy.wait_recv()
    oland[pl.ds(144, 112)] = back[pl.ds(0, 112)]
    ocland[pl.ds(144, 112)] = mb[pl.ds(0, 112)]
    gin_ref[...] = mm(t_unblock_ref[...], oland[...]).astype(BF16).reshape(8, 32, 512)
    got = mm(t_cunblock_ref[...], ocland[...]).astype(BF16)
    for q in range(4):
        merged_ref[:, :, 256 * q : 256 * q + 256] = got[64 * q : 64 * q + 64].reshape(4, 16, 256)
    factor = 1.0 / 256.0
    gr_ref[...] = a_sum.fifth() * factor
    go.drain()
    total = b_sum.fifth() * factor
    gq_ref[:, 0:128] = total[0:16]
    gq_ref[:, 128:192] = total[16:32, 0:64]
    go_ref[...] = total[16:32, 64:128]


def hand_on(*refs):
    for src, dst in zip(refs[:5], refs[5:]):
        dst[...] = src[...]


def on_device(
    stash_values, scale_exp, w_qkv, w_out, w_reduce, logit_scale, bias_table, rel_index, norm_gain, merge_gain, cotangent
):
    vmem = pl.BlockSpec(memory_space=pltpu.VMEM)
    sems = pltpu.SemaphoreType.DMA
    outputs = (
        jax.ShapeDtypeStruct((4, 16, 1024), BF16),
        jax.ShapeDtypeStruct((8, 32, 512), BF16),
        jax.ShapeDtypeStruct((16, 192), F32),
        jax.ShapeDtypeStruct((16, 64), F32),
        jax.ShapeDtypeStruct((64, 128), F32),
    )
    loads = (
        stash_values, scale_exp, const(T_BLOCK), cotangent, const(T_CBLOCK),
        bias_table.T, rel_index, const(WIN_ORDER), const(ROW_CUT, F32), const(COL_CUT, F32), logit_scale.reshape(1, 16),
        norm_gain.reshape(1, 512), merge_gain.reshape(1, 1024),
        const(T_MERGE), const(T_CMERGE), const(T_BLOCK.T), const(T_MERGE.T), const(T_CBLOCK.T), const(T_CMERGE.T),
        const(COLUMNS_64), const(COLUMNS_16),
        const(same_block(256, 64, 256, 64)), const(same_block(256, 32, 256, 32)), const(same_block(256, 64, 128, 32)),
    )
    tokens = lambda width, kind=BF16: pltpu.VMEM((256, width), kind)
    results = pl.pallas_call(
        block_kernel,
        out_shape=outputs,
        in_specs=[pl.BlockSpec(memory_space=pl.ANY)] * 27,
        out_specs=(vmem,) * 5,
        scratch_shapes=[
            tokens(768), tokens(768), tokens(512), tokens(512), tokens(256),
            pltpu.VMEM((4, 4, 2, 16, 1536), BF16),
            pltpu.VMEM((4, 4, 2, 16, 512), BF16),
            pltpu.VMEM((4, 4, 2, 64, 1024), BF16),
            tokens(512),
            pltpu.VMEM((64, 1024), BF16),
            tokens(1536), tokens(512), tokens(512), tokens(512, F32), tokens(512, F32),
            pltpu.VMEM((4, 4, 64, 256), F32),
            pltpu.VMEM((2, 4, 64, 256), F32),
            pltpu.VMEM((64, 16, 64), F32),
            pltpu.VMEM((16, 256), F32),
            tokens(512), tokens(512), tokens(512, F32), tokens(512, F32), tokens(1536),
            tokens(512, F32), tokens(1, F32), tokens(512), tokens(512), tokens(512),
            tokens(512), tokens(512),
            pltpu.VMEM((1, 512), F32),
            tokens(512), tokens(256), tokens(512), tokens(256), tokens(512), tokens(256),
            pltpu.VMEM((64, 1024), BF16),
            pltpu.VMEM((64, 1024), BF16),
            tokens(512), tokens(1536),
            pltpu.VMEM((2, 4, 4, 32, 1024), BF16),
            pltpu.VMEM((2, 4, 4, 16, 1024), BF16),
            tokens(256),
            *[pltpu.VMEM(load.shape, load.dtype) for load in loads],
            *reduce_scratch(32, 64, 2),
            *reduce_scratch(16, 32, 3),
            sems((COPIES,)),
            sems((COPIES,)),
            sems((32,)),
        ],
        compiler_params=pltpu.CompilerParams(
            collective_id=0, has_side_effects=True, vmem_limit_bytes=60 * 1024 * 1024
        ),
        name="block_forward_backward",
    )(w_qkv, w_out, w_reduce, *loads)
    return pl.pallas_call(
        hand_on,
        out_shape=outputs,
        in_specs=[vmem] * 5,
        out_specs=(vmem,) * 5,
        name="hand_on",
    )(*results)


def solution(mesh):
    tile = P("wide", "narrow", None)
    rows = P("wide", None)
    both = P("wide", "narrow")
    return jax.shard_map(
        on_device,
        mesh=mesh,
        in_specs=(tile, both, rows, rows, rows, P(), P(), P(), P(), P(), tile),
        out_specs=(tile, tile, both, both, both),
        check_vma=False,
    )
```

```python
import jax
import jax.numpy as jnp
import numpy as np
from jax import lax
from jax.experimental import pallas as pl
from jax.experimental.pallas import tpu as pltpu
from jax.sharding import PartitionSpec as P

MESH = pl.DeviceIdType.MESH
F32 = jnp.float32
BF16 = jnp.bfloat16
NT = (((1,), (1,)), ((), ()))
TN = (((0,), (0,)), ((), ()))


def one_hot(sources):
    sources = np.asarray(sources).reshape(-1)
    table = np.zeros((len(sources), len(sources)), np.float32)
    table[np.arange(len(sources)), sources] = 1.0
    return table


def token_tables():
    i, j, r, c = np.meshgrid(*map(np.arange, (2, 8, 4, 4)), indexing="ij")
    block_from_natural = one_hot((4 * i + r) * 32 + 4 * j + c)
    k, win, mr, mc = np.meshgrid(*map(np.arange, (4, 4, 4, 4)), indexing="ij")
    i, r = mr // 2, 2 * (mr % 2) + k % 2
    j, c = 2 * win + mc // 2, 2 * (mc % 2) + k // 2
    merge_from_block = one_hot((i * 8 + j) * 16 + r * 4 + c)
    i, j, q, m = np.meshgrid(*map(np.arange, (2, 8, 4, 4)), indexing="ij")
    cot_block_from_natural = one_hot(q * 64 + (2 * i + m // 2) * 16 + 2 * j + m % 2)
    q, win, mr, mc = np.meshgrid(*map(np.arange, (4, 4, 4, 4)), indexing="ij")
    i, j, m = mr // 2, 2 * win + mc // 2, (mr % 2) * 2 + mc % 2
    cot_merge_from_block = one_hot((i * 8 + j) * 16 + q * 4 + m)
    return (
        block_from_natural,
        merge_from_block,
        cot_block_from_natural,
        cot_merge_from_block,
    )


def window_tables():
    k, mr, mc = np.meshgrid(*map(np.arange, (4, 4, 4)), indexing="ij")
    row, col = (2 * mr + k % 2).reshape(-1), (2 * mc + k // 2).reshape(-1)
    order = one_hot(row * 8 + col)
    row_cut = (row[:, None] >= 4) != (row[None, :] >= 4)
    col_cut = (col[:, None] >= 4) != (col[None, :] >= 4)
    tiled = lambda cut: np.tile(cut.astype(np.float32), (1, 4))
    return order, tiled(row_cut), tiled(col_cut)


def same_block(rows, row_size, cols, col_size):
    return (
        (np.arange(rows) // row_size)[:, None] == (np.arange(cols) // col_size)[None]
    ).astype(np.float32)


T_BLOCK, T_MERGE, T_CBLOCK, T_CMERGE = token_tables()
COLUMNS_64 = one_hot(np.arange(512).reshape(4, 2, 64).transpose(1, 0, 2)).T
COLUMNS_16 = one_hot(np.arange(512).reshape(16, 2, 16).transpose(1, 0, 2)).T
WIN_ORDER, ROW_CUT, COL_CUT = window_tables()


def const(table, dtype=BF16):
    return jnp.asarray(table, dtype)


class Place:
    def __init__(self):
        wide, narrow = lax.axis_index("wide"), lax.axis_index("narrow")
        self.wide, self.narrow = wide, narrow
        self.core = lax.rem(wide, 2)
        self.zh = lax.rem(lax.div(wide, 2), 4)
        self.x = lax.div(wide, 8)
        self.y = lax.div(narrow, 2)
        self.zl = lax.rem(narrow, 2)
        self.z = 2 * self.zh + self.zl
        self.sibling = (wide + 1 - 2 * self.core, narrow)

    def at_x(self, step):
        return ((lax.rem(self.x + step + 4, 4) * 4 + self.zh) * 2 + self.core, self.narrow)

    def at_y(self, step):
        return (self.wide, lax.rem(self.y + step + 4, 4) * 2 + self.zl)

    def at_z(self, step):
        z = lax.rem(self.z + step + 8, 8)
        return ((self.x * 4 + lax.div(z, 2)) * 2 + self.core, self.y * 2 + lax.rem(z, 2))

    def at_tile(self, rows, cols):
        return (lax.rem(self.wide + rows + 32, 32), lax.rem(self.narrow + cols + 8, 8))


class Sender:
    def __init__(self, send_sem, recv_sem, local_sem):
        self.send_sem, self.recv_sem, self.local_sem = send_sem, recv_sem, local_sem
        self.started, self.count, self.local_count, self.drained = [], 0, 0, 0

    def remote(self, src, dst, device):
        copy = pltpu.make_async_remote_copy(
            src_ref=src,
            dst_ref=dst,
            send_sem=self.send_sem.at[self.count],
            recv_sem=self.recv_sem.at[self.count],
            device_id=device,
            device_id_type=MESH,
        )
        self.count += 1
        copy.start()
        self.started.append(copy)
        return copy

    def local(self, src, dst):
        copy = pltpu.make_async_copy(src, dst, self.local_sem.at[self.local_count])
        self.local_count += 1
        copy.start()
        return copy

    def drain(self, until=None):
        until = self.count if until is None else until
        for copy in self.started[self.drained : until]:
            copy.wait_send()
        self.drained = until


def greet(devices):
    barrier = pltpu.get_barrier_semaphore()
    for device in devices:
        pl.semaphore_signal(barrier, inc=1, device_id=device, device_id_type=MESH)


def wait_for(devices):
    pl.semaphore_wait(pltpu.get_barrier_semaphore(), len(devices))


def lanes(start, size):
    return pl.ds(pl.multiple_of(start, 128), size)


def mm(a, b):
    return jnp.dot(a, b, preferred_element_type=F32)


def dg(a, b, dims):
    return lax.dot_general(a, b, dims, preferred_element_type=F32)


def add(*parts):
    total = parts[0].astype(F32)
    for one in parts[1:]:
        total = total + one.astype(F32)
    return total


def sums(values, table):
    return mm(values.astype(BF16), table)


def norm_parts(values):
    centred = values - jnp.mean(values, -1, keepdims=True)
    scale = lax.rsqrt(jnp.mean(centred * centred, -1, keepdims=True) + 1e-05)
    return centred * scale, scale


def norm_back(cot, normed, scale, gain):
    cot = cot * gain
    shared = jnp.mean(cot, -1, keepdims=True) + normed * jnp.mean(cot * normed, -1, keepdims=True)
    return scale * (cot - shared)


EVERY = pl.ds(0, 4)


class Gather:
    def __init__(self, at, go, shard, whole, cut, quarters=False, direct=False):
        self.at, self.go, self.shard, self.whole, self.cut = at, go, shard, whole, cut
        self.quarters, self.direct = quarters, direct
        self.x_left, self.x_right, self.x_far = (lax.rem(at.x + step, 4) for step in (3, 1, 2))
        self.y_left, self.y_right, self.y_far = (lax.rem(at.y + step, 4) for step in (3, 1, 2))
        self.shared = []

    def part(self, xs, zs, y=None):
        y = self.at.y if y is None else y
        return self.whole.at[(xs, zs, self.at.core) + self.cut(y)]

    def move(self, xs, zs, device, y=None):
        ref = self.part(xs, zs, y)
        return self.go.remote(ref, ref, device)

    def share(self, xs, zs, y=None):
        self.shared.append(self.move(xs, zs, self.at.sibling, y))

    def start(self):
        at = self.at
        own, there = self.shard.at[self.cut(at.y)], self.part(at.x, at.zh)
        way = 2 * at.zl - 1
        self.z = [self.go.remote(own, there, at.at_z(way * step)) for step in (1, 2, 3)]
        self.mine = self.go.local(own, there)

    def x1(self):
        at = self.at
        self.mine.wait()
        for copy in self.z:
            copy.wait_recv()
        steps = (1, 2, -1) if self.direct else (1, -1)
        self.x = [self.move(at.x, EVERY, at.at_x(step)) for step in steps]
        if not self.quarters:
            self.share(at.x, EVERY)

    def x2(self):
        at = self.at
        self.x[0].wait_recv()
        far = [self.move(self.x_left, pl.ds(0, 2), at.at_x(1))]
        self.x[1].wait_recv()
        far.append(self.move(self.x_right, pl.ds(2, 2), at.at_x(-1)))
        self.x = far
        if not self.quarters:
            self.share(self.x_left, EVERY)
            self.share(self.x_right, EVERY)

    def x3(self):
        if self.direct and not self.quarters:
            for copy, x in zip(self.x, (self.x_left, self.x_far, self.x_right)):
                copy.wait_recv()
                self.share(x, EVERY)
            return
        for copy in self.x:
            copy.wait_recv()
        if not self.quarters:
            self.share(self.x_far, EVERY)

    def y1(self):
        at = self.at
        self.x3()
        self.y = [self.move(EVERY, EVERY, at.at_y(step)) for step in (1, -1)]
        self.share(EVERY, EVERY)

    def y2(self):
        at = self.at
        self.y[0].wait_recv()
        far = [self.move(pl.ds(0, 2), EVERY, at.at_y(1), self.y_left)]
        self.y[1].wait_recv()
        far.append(self.move(pl.ds(2, 2), EVERY, at.at_y(-1), self.y_right))
        self.y = far
        self.share(EVERY, EVERY, self.y_left)
        self.share(EVERY, EVERY, self.y_right)

    def y3(self):
        for copy in self.y:
            copy.wait_recv()
        self.share(EVERY, EVERY, self.y_far)

    def done(self):
        for copy in self.shared:
            copy.wait_recv()


def y_cut(j):
    return lanes(j * 256, 256)


class Reduce:
    def __init__(self, at, go, m, bx1, bx2, by1, by2, cx, cy, dx, dy, zsend, zland, direct=False):
        self.at, self.go, self.m = at, go, m
        self.bx1, self.bx2, self.by1, self.by2 = bx1, bx2, by1, by2
        self.cx, self.cy = cx, cy
        self.dx, self.dy = dx, dy
        self.zsend, self.zland = zsend, zland
        self.xs = [lax.rem(at.x + step, 4) for step in (2, 1, 3, 0)]
        self.ys = [lax.rem(at.y + step, 4) for step in (2, 1, 3, 0)]
        self.direct, self.parts = direct, 3 if direct else 2
        self.d, self.d_y = [], []
        self.x_left, self.x_right = at.at_x(-1), at.at_x(1)
        self.y_left, self.y_right = at.at_y(-1), at.at_y(1)

    def both(self, src, dst, right, left, step):
        if step == 1:
            pairs = ((src(0, pl.ds(0, 2)), right), (src(0, pl.ds(2, 2)), left))
        else:
            pairs = ((src(1, EVERY), right), (src(2, EVERY), left))
        return [self.go.remote(ref, dst.at[n], device) for n, (ref, device) in enumerate(pairs)]

    def x_src(self, n, part):
        return self.m.at[0, self.xs[n], part]

    def y_src(self, n, part):
        return self.m.at[1, part, :, :, y_cut(self.ys[n])]

    def direct_y(self, n):
        self.d_y = self.d_y + [self.go.remote(self.y_src(n, EVERY), self.by2.at[n], self.at.at_y((2, 1, 3)[n]))]

    def direct_x(self):
        self.d_x = [
            self.go.remote(self.x_src(n, EVERY), self.bx2.at[n], self.at.at_x(step)) for n, step in ((0, 2), (1, 1), (2, 3))
        ]

    def first_x(self):
        self.b_x = self.both(self.x_src, self.bx1, self.x_right, self.x_left, 1)

    def first_y(self):
        self.b_y = self.both(self.y_src, self.by1, self.y_right, self.y_left, 1)

    def second_x(self):
        m, xs = self.m, self.xs
        for copy in self.b_x:
            copy.wait_recv()
        for s in range(2):
            m[0, xs[1], s] = add(m[0, xs[1], s], self.bx1[0, s]).astype(BF16)
            m[0, xs[2], 2 + s] = add(m[0, xs[2], 2 + s], self.bx1[1, s]).astype(BF16)
        self.b_x = self.both(self.x_src, self.bx2, self.x_right, self.x_left, 2)

    def second_y(self):
        m, ys = self.m, self.ys
        for copy in self.b_y:
            copy.wait_recv()
        for s in range(2):
            cut = y_cut(ys[1])
            m[1, s, :, :, cut] = add(m[1, s, :, :, cut], self.by1[0, s]).astype(BF16)
            cut = y_cut(ys[2])
            m[1, 2 + s, :, :, cut] = add(m[1, 2 + s, :, :, cut], self.by1[1, s]).astype(BF16)
        self.b_y = self.both(self.y_src, self.by2, self.y_right, self.y_left, 2)

    def third_x(self):
        at = self.at
        for copy in self.d_x if self.direct else self.b_x:
            copy.wait_recv()
        for s in range(4):
            self.cx[s] = add(self.m[0, at.x, s], *[self.bx2[n, s] for n in range(self.parts)]).astype(BF16)
        for n, step in ((0, 2), (1, 1), (2, 3)):
            src = self.cx.at[:, :, y_cut(self.ys[n])]
            self.d.append(self.go.remote(src, self.dx.at[n], at.at_y(step)))

    def third_y(self):
        at = self.at
        for copy in self.d_y if self.direct else self.b_y:
            copy.wait_recv()
        for s in range(4):
            own = self.m[1, s, :, :, y_cut(at.y)]
            self.cy[s] = add(own, *[self.by2[n, s] for n in range(self.parts)]).astype(BF16)
        for n, step in ((0, 2), (1, 1), (2, 3)):
            self.d.append(self.go.remote(self.cy.at[self.xs[n]], self.dy.at[n], at.at_x(step)))

    def fourth(self, pack):
        for copy in self.d:
            copy.wait_recv()
        for h in range(4):
            a = add(self.cx[h, :, y_cut(self.at.y)], *[self.dx[n, h] for n in range(3)])
            b = add(self.cy[self.at.x, h], *[self.dy[n, h] for n in range(3)])
            for low in range(2):
                self.zsend[h, low] = pack(a, b, low).astype(BF16)
        self.last = []
        for step in range(1, 8):
            z = lax.rem(self.at.z + step, 8)
            src = self.zsend.at[lax.div(z, 2), lax.rem(z, 2)]
            self.last.append(self.go.remote(src, self.zland.at[step - 1], self.at.at_z(step)))

    def fifth(self):
        total = self.zsend[self.at.zh, self.at.zl].astype(F32)
        for step in range(7):
            self.last[step].wait_recv()
            total = total + self.zland[step].astype(F32)
        return total


def pack_reduce(a, b, low):
    cut = slice(128 * low, 128 * low + 128)
    return jnp.concatenate([a[:, cut], b[:, cut]], 0)


def pack_qkv_out(a, b, low):
    if low == 0:
        rows = a[:, 0:128], jnp.concatenate([a[:, 128:192], b[:, 128:192]], 1)
    else:
        rows = (
            jnp.concatenate([a[:, 192:256], b[:, 0:64]], 1),
            jnp.concatenate([b[:, 64:128], b[:, 192:256]], 1),
        )
    return jnp.concatenate(rows, 0)


def reduce_scratch(rows, z_rows, parts):
    return [
        pltpu.VMEM((2, 2, rows, 1024), BF16),
        pltpu.VMEM((parts, 4, rows, 1024), BF16),
        pltpu.VMEM((2, 2, 4, rows, 256), BF16),
        pltpu.VMEM((parts, 4, 4, rows, 256), BF16),
        pltpu.VMEM((4, rows, 1024), BF16),
        pltpu.VMEM((4, 4, rows, 256), BF16),
        pltpu.VMEM((3, 4, rows, 256), BF16),
        pltpu.VMEM((3, 4, rows, 256), BF16),
        pltpu.VMEM((4, 2, z_rows, 128), BF16),
        pltpu.VMEM((7, z_rows, 128), BF16),
    ]


COPIES = 12 + 18 + 3 * 11 + 15 + 8 + 2 * (8 + 6 + 7) + 16


def block_kernel(
    wq_ref, wo_ref, wr_ref, *rest,
):
    loads, rest = rest[:24], rest[24:]
    (
    merged_ref, gin_ref, gq_ref, go_ref, gr_ref,
    blk, land, back, oland, ocland, wq, wo, wr,
    x_tok, cot_tok, qkv, qs, kh, rq, rk, probs, masked, bias_rows, table, att, d_att, dqs, dkh, dqkv,
    xhat, xscale, ro, dproj, dtok, xt, at_t, ls_row, ro_cols, ro_theirs, x_cols, x_theirs, at_cols, at_theirs,
    dred, dred_theirs, dproj_theirs, dqkv_theirs, fa, fb, mb,
    *rest,
    ) = rest
    held, rest = rest[:24], rest[24:]
    (
        stash_ref, exp_ref, t_block_ref, cot_ref, t_cblock_ref,
        table_ref, rel_ref, order_ref, row_cut_ref, col_cut_ref, ls_ref,
        ng_ref, mg_ref, t_merge_ref, t_cmerge_ref, t_unblock_ref, t_unmerge_ref, t_cunblock_ref, t_cunmerge_ref,
        columns_ref, columns_16_ref, bd64_ref, bd32_ref, heads_ref,
    ) = held
    a_bufs, b_bufs, (send_sem, recv_sem, local_sem) = rest[0:10], rest[10:20], rest[20:]
    go = Sender(send_sem, recv_sem, local_sem)
    at = Place()
    c = at.core
    partners = (
        [at.sibling]
        + [at.at_x(step) for step in (1, 2, 3)]
        + [at.at_y(step) for step in (1, 2, 3)]
        + [at.at_z(step) for step in range(1, 8)]
        + [at.at_tile(*step) for step in ((-1, 0), (0, -1), (-1, -1), (1, 0), (0, 1), (1, 1))]
    )
    greet(partners)
    arrivals = [go.local(src, dst) for src, dst in zip(loads, held)]

    def loaded(first, last):
        for copy in arrivals[first:last]:
            copy.wait()

    wait_for(partners)
    all_rows = pl.ds(0, 16)
    q_y = Gather(at, go, wq_ref, wq, lambda y: (all_rows, lanes(512 + 256 * y, 256)), True, True)
    q_x = Gather(at, go, wq_ref, wq, lambda y: (all_rows, pl.ds(0, 512)))
    o_x = Gather(at, go, wo_ref, wo, lambda y: (all_rows, pl.ds(0, 512)))
    r_x = Gather(at, go, wr_ref, wr, lambda y: (pl.ds(0, 64), pl.ds(0, 640)))
    r_y = Gather(at, go, wr_ref, wr, lambda y: (pl.ds(pl.multiple_of(16 * y, 16), 16), pl.ds(640, 384)), True, True)

    r_y.start()
    q_y.start()

    loaded(0, 11)
    table[...] = jnp.zeros((16, 256), F32)
    table[:, 0:225] = 16.0 * jax.nn.sigmoid(table_ref[...])
    by_head = table[...]
    high = by_head.astype(BF16)
    low = (by_head - high.astype(F32)).astype(BF16)
    both = jnp.concatenate([high, low], 0)
    rel = mm(order_ref[...], rel_ref[...].astype(F32).astype(BF16)).astype(BF16)
    rel = dg(rel, order_ref[...], NT).astype(jnp.int32)
    rel = jnp.concatenate([rel[16 * j : 16 * j + 16] for j in range(4)], 1)
    entry = lax.broadcasted_iota(jnp.int32, (256, 256), 0)

    def bias_of(rows):
        for a in rows:
            chosen = jnp.where(entry == rel[a : a + 1], 1.0, 0.0).astype(BF16)
            got = mm(both, chosen)
            got = got[0:16] + got[16:32]
            for j in range(4):
                bias_rows[16 * j + a] = got[:, 64 * j : 64 * j + 64]

    bias_of(range(0, 5))
    o_x.start()

    factor_of = exp_ref[...]
    factor_of = jnp.where(factor_of == -8, 2.0**-8, jnp.where(factor_of == -7, 2.0**-7, 2.0**-6))
    in_window = lax.broadcasted_iota(jnp.int32, (32, 512), 0) // 8
    factor = jnp.zeros((32, 512), F32)
    for w in range(4):
        factor = jnp.where(in_window == w, factor_of[:, w : w + 1], factor)
    inputs = stash_ref[...].astype(F32) * factor[None]
    blk[:, 0:512] = mm(t_block_ref[...], inputs.reshape(256, 512).astype(BF16)).astype(BF16)
    q_x.start()
    r_y.x1()
    q_y.x1()
    cot = cot_ref[...].astype(F32).reshape(64, 1024).astype(BF16)
    cot = jnp.concatenate([cot[:, 256 * q : 256 * q + 256] for q in range(4)], 0)
    blk[:, 512:768] = mm(t_cblock_ref[...], cot).astype(BF16)
    r_x.start()
    q_x.x1()
    q_y.y1()
    o_x.x1()
    halo = [
        go.remote(blk.at[pl.ds(16, 112)], land.at[pl.ds(128, 112)], at.at_tile(-1, 0)),
        go.remote(blk.at[pl.ds(128, 16)], land.at[pl.ds(112, 16)], at.at_tile(0, -1)),
        go.remote(blk.at[pl.ds(0, 16)], land.at[pl.ds(240, 16)], at.at_tile(-1, -1)),
    ]
    bias_of(range(5, 10))
    r_y.y1()
    q_x.x2()
    r_x.x1()
    bias_of(range(10, 16))
    q_y.y2()
    q_x.x3()
    o_x.x2()
    last_rows = (at.wide == 31).astype(F32)
    last_cols = (at.narrow == 7).astype(F32)
    mask = row_cut_ref[...] * last_rows * -100.0
    mask_end = jnp.maximum(row_cut_ref[...] * last_rows, col_cut_ref[...] * last_cols) * -100.0
    for g in range(4):
        bias = jnp.concatenate([bias_rows[:, 4 * g + h, :] for h in range(4)], 1)
        masked[0, g] = bias + mask
        masked[1, g] = bias + mask_end
    lane = lax.broadcasted_iota(jnp.int32, (1, 512), 1) // 32
    scales = jnp.zeros((1, 512), F32)
    for h in range(16):
        scales = jnp.where(lane == h, ls_ref[:, h : h + 1], scales)
    ls_row[...] = scales


    for copy in halo:
        copy.wait_recv()
    r_y.y2()
    q_y.y3()
    r_x.x2()
    o_x.x3()
    loaded(11, 24)
    land[pl.ds(0, 112)] = blk[pl.ds(144, 112)]
    x_tok[...] = mm(t_merge_ref[...], land[:, 0:512]).astype(BF16)
    cot = mm(t_cmerge_ref[...], land[:, 512:768]).astype(BF16)
    cot_tok[...] = jnp.concatenate([cot[64 * q : 64 * q + 64] for q in range(4)], 1)
    x_cols[...] = mm(x_tok[...], columns_16_ref[...]).astype(BF16)
    not_mine = lanes(256 * (1 - c), 256)
    mine = lanes(256 * c, 256)
    x_swap = go.remote(x_cols.at[:, not_mine], x_theirs, at.sibling)

    q_x.done()
    q_y.done()

    qkv[...] = mm(x_tok[...], wq[...].reshape(512, 1536)).astype(BF16)
    r_y.y3()
    o_x.done()
    r_x.x3()
    for start, inverse, unit in ((0, rq, qs), (512, rk, kh)):
        for n in range(2):
            cut = slice(256 * n, 256 * n + 256)
            for row in range(0, 256, 128):
                rows = slice(row, row + 128)
                raw = qkv[rows, start + 256 * n : start + 256 * n + 256].astype(F32)
                inv = lax.rsqrt(jnp.maximum(sums(raw * raw, bd32_ref[...]), 1e-24))
                inverse[rows, cut] = inv
                raw = raw * inv
                if start == 0:
                    raw = raw * ls_row[:, cut]
                unit[rows, cut] = raw.astype(BF16)
    x_swap.wait_recv()
    xt[:, 0:256] = x_cols[:, mine].T
    xt[:, 256:512] = x_theirs[...].T

    def window(ref, win, cut):
        return jnp.concatenate([ref[pl.ds(64 * k + 16 * win, 16), cut] for k in range(4)], 0)

    def put_window(ref, win, cut, values):
        for k in range(4):
            ref[pl.ds(64 * k + 16 * win, 16), cut] = values[16 * k : 16 * k + 16]

    def spread(rows):
        return jnp.concatenate([rows] * 4, 0) * heads_ref[...]

    def fold(values):
        values = values * heads_ref[...].astype(F32)
        return (values[0:64] + values[64:128]) + (values[128:192] + values[192:256])

    def forward(g):
        cut = slice(g * 128, g * 128 + 128)
        v_cut = slice(g * 128 + 1024, g * 128 + 1152)
        weights = []
        for win in range(4):
            scores = dg(window(qs, win, cut), spread(window(kh, win, cut)), NT)
            weights.append(jnp.exp(scores + masked[1 if win == 3 else 0, g]))
        totals = sums(jnp.concatenate(weights, 0), bd64_ref[...])
        for win in range(4):
            p = weights[win] / totals[64 * win : 64 * win + 64]
            probs[g, win] = p
            values = spread(window(qkv, win, v_cut))
            put_window(att, win, cut, mm(p.astype(BF16), values).astype(BF16))

    for g in range(4):
        forward(g)
    at_cols[...] = mm(att[...], columns_16_ref[...]).astype(BF16)
    at_swap = go.remote(at_cols.at[:, not_mine], at_theirs, at.sibling)
    r_y.done()
    xhat[...] = mm(att[...], wo[...].reshape(512, 512))
    for row in range(0, 256, 64):
        rows = slice(row, row + 64)
        normed, scale = norm_parts(xhat[rows])
        xhat[rows] = normed
        xscale[rows] = scale
        ro[rows] = (x_tok[rows].astype(F32) + normed * ng_ref[...]).astype(BF16)
    ro_cols[...] = mm(ro[...], columns_ref[...]).astype(BF16)
    swap = [go.remote(ro_cols.at[:, not_mine], ro_theirs, at.sibling)]
    r_x.done()

    reduced = jnp.zeros((64, 1024), F32)
    for k in range(4):
        reduced += mm(ro[64 * k : 64 * k + 64], wr[k].reshape(512, 1024))
    normed, scale = norm_parts(reduced)
    dred[...] = norm_back(cot_tok[...].astype(F32), normed, scale, mg_ref[...]).astype(BF16)
    swap.append(go.remote(dred, dred_theirs, at.sibling))
    merged = (normed * mg_ref[...]).astype(BF16)
    merged = jnp.concatenate([merged[:, 256 * q : 256 * q + 256] for q in range(4)], 0)
    mb[...] = mm(t_cunmerge_ref[...], merged).astype(BF16)

    def send_back(tile, landing):
        return [
            go.remote(tile.at[pl.ds(128, 112)], landing.at[pl.ds(16, 112)], at.at_tile(1, 0)),
            go.remote(tile.at[pl.ds(112, 16)], landing.at[pl.ds(128, 16)], at.at_tile(0, 1)),
            go.remote(tile.at[pl.ds(240, 16)], landing.at[pl.ds(0, 16)], at.at_tile(1, 1)),
        ]

    for k in range(4):
        dtok[64 * k : 64 * k + 64] = dg(dred[...], wr[k].reshape(512, 1024), NT).astype(BF16)

    for row in range(0, 256, 64):
        rows = slice(row, row + 64)
        got = norm_back(dtok[rows].astype(F32), xhat[rows], xscale[rows], ng_ref[...])
        dproj[rows] = got.astype(BF16)
    dproj_swap = go.remote(dproj, dproj_theirs, at.sibling)
    d_att[...] = dg(dproj[...], wo[...].reshape(512, 512), NT).astype(BF16)

    for copy in swap:
        copy.wait_recv()
    before_a = go.count
    a_sum = Reduce(at, go, fa, *a_bufs)
    grads = jnp.concatenate([dred[...], dred_theirs[...]], 0)
    for n in range(4):
        k = a_sum.xs[n]
        rows = pl.ds(pl.multiple_of(64 * k, 64), 64)
        tokens = jnp.concatenate([ro_cols[rows, mine], ro_theirs[rows]], 0).T
        for cut in (slice(0, 512), slice(512, 1024)):
            got = mm(tokens, grads[:, cut]).astype(BF16).reshape(4, 64, 512)
            fa[0, k, :, :, cut] = got[:, 0:32]
            fa[1, k, :, :, cut] = got[:, 32:64]
        if n == 0:
            a_sum.first_x()
    a_sum.first_y()

    def backward(g):
        cut = slice(g * 128, g * 128 + 128)
        v_cut = slice(g * 128 + 1024, g * 128 + 1152)
        dps = []
        for win in range(4):
            dp = dg(window(d_att, win, cut), spread(window(qkv, win, v_cut)), NT)
            dps.append(dp.astype(BF16).astype(F32))
        alike = sums(jnp.concatenate([probs[g, win] * dps[win] for win in range(4)], 0), bd64_ref[...])
        for win in range(4):
            p = probs[g, win]
            ds = (p * (dps[win] - alike[64 * win : 64 * win + 64])).astype(BF16)
            put_window(dqs, win, cut, mm(ds, spread(window(kh, win, cut))))
            put_window(dkh, win, cut, fold(dg(ds, window(qs, win, cut), TN)))
            put_window(dqkv, win, v_cut, fold(dg(p.astype(BF16), window(d_att, win, cut), TN)).astype(BF16))

    for g in range(4):
        backward(g)

    def swap_dqkv(start):
        cut = pl.ds(start, 512)
        return go.remote(dqkv.at[:, cut], dqkv_theirs.at[:, cut], at.sibling)

    dqkv_swap = [swap_dqkv(1024)]
    a_sum.second_x()
    a_sum.second_y()
    for start, inverse, grad in ((0, rq, dqs), (512, rk, dkh)):
        for n in range(2):
            cut = slice(256 * n, 256 * n + 256)
            both_cut = slice(start + 256 * n, start + 256 * n + 256)
            for row in range(0, 256, 128):
                rows = slice(row, row + 128)
                inv = inverse[rows, cut]
                unit = qkv[rows, both_cut].astype(F32) * inv
                d_unit = grad[rows, cut]
                if start == 0:
                    d_unit = d_unit * ls_row[:, cut]
                along = sums(unit * d_unit, bd32_ref[...])
                along = jnp.where(inv < 1e12, along, 0.0)
                dqkv[rows, both_cut] = (inv * (d_unit - unit * along)).astype(BF16)
        dqkv_swap.append(swap_dqkv(start))
    at_swap.wait_recv()
    at_t[:, 0:256] = at_cols[:, mine].T
    at_t[:, 256:512] = at_theirs[...].T
    dproj_swap.wait_recv()
    d_out = jnp.concatenate([dproj[...], dproj_theirs[...]], 0)
    out = mm(at_t[...], d_out).astype(BF16)
    for y in range(4):
        fb[1, :, :, :, 256 * y + 128 : 256 * y + 256] = out[:, 128 * y : 128 * y + 128].reshape(4, 4, 16, 128)

    merged_back = send_back(mb, ocland)
    d_in = dtok[...].astype(F32) + dg(dqkv[...], wq[...].reshape(512, 1536), NT)
    back[...] = mm(t_unmerge_ref[...], d_in.astype(BF16)).astype(BF16)
    grad_back = send_back(back, oland)

    for copy in dqkv_swap:
        copy.wait_recv()
    before_b = go.count
    b_sum = Reduce(at, go, fb, *b_bufs, direct=True)
    for n in range(4):
        y = b_sum.ys[n]
        cut = lanes(384 * y, 384)
        grads = jnp.concatenate([dqkv[:, cut], dqkv_theirs[:, cut]], 0)
        got = mm(xt[...], grads).astype(BF16)
        fb[0, :, :, :, y_cut(y)] = got[:, 0:256].reshape(4, 4, 16, 256)
        fb[1, :, :, :, lanes(256 * y, 128)] = got[:, 256:384].reshape(4, 4, 16, 128)
        if n < 3:
            b_sum.direct_y(n)
    b_sum.direct_x()
    go.drain(before_a // 2)
    a_sum.third_x()
    a_sum.third_y()
    go.drain(before_b)
    before_c = go.count
    b_sum.third_y()
    b_sum.third_x()
    a_sum.fourth(pack_reduce)
    b_sum.fourth(pack_qkv_out)
    go.drain(before_c)
    for copy in merged_back + grad_back:
        copy.wait_recv()
    oland[pl.ds(144, 112)] = back[pl.ds(0, 112)]
    ocland[pl.ds(144, 112)] = mb[pl.ds(0, 112)]
    gin_ref[...] = mm(t_unblock_ref[...], oland[...]).astype(BF16).reshape(8, 32, 512)
    got = mm(t_cunblock_ref[...], ocland[...]).astype(BF16)
    for q in range(4):
        merged_ref[:, :, 256 * q : 256 * q + 256] = got[64 * q : 64 * q + 64].reshape(4, 16, 256)
    factor = 1.0 / 256.0
    gr_ref[...] = a_sum.fifth() * factor
    go.drain()
    total = b_sum.fifth() * factor
    gq_ref[:, 0:128] = total[0:16]
    gq_ref[:, 128:192] = total[16:32, 0:64]
    go_ref[...] = total[16:32, 64:128]


def hand_on(*refs):
    for src, dst in zip(refs[:5], refs[5:]):
        dst[...] = src[...]


def on_device(
    stash_values, scale_exp, w_qkv, w_out, w_reduce, logit_scale, bias_table, rel_index, norm_gain, merge_gain, cotangent
):
    vmem = pl.BlockSpec(memory_space=pltpu.VMEM)
    sems = pltpu.SemaphoreType.DMA
    outputs = (
        jax.ShapeDtypeStruct((4, 16, 1024), BF16),
        jax.ShapeDtypeStruct((8, 32, 512), BF16),
        jax.ShapeDtypeStruct((16, 192), F32),
        jax.ShapeDtypeStruct((16, 64), F32),
        jax.ShapeDtypeStruct((64, 128), F32),
    )
    loads = (
        stash_values, scale_exp, const(T_BLOCK), cotangent, const(T_CBLOCK),
        bias_table.T, rel_index, const(WIN_ORDER), const(ROW_CUT, F32), const(COL_CUT, F32), logit_scale.reshape(1, 16),
        norm_gain.reshape(1, 512), merge_gain.reshape(1, 1024),
        const(T_MERGE), const(T_CMERGE), const(T_BLOCK.T), const(T_MERGE.T), const(T_CBLOCK.T), const(T_CMERGE.T),
        const(COLUMNS_64), const(COLUMNS_16),
        const(same_block(256, 64, 256, 64)), const(same_block(256, 32, 256, 32)), const(same_block(256, 64, 128, 32)),
    )
    tokens = lambda width, kind=BF16: pltpu.VMEM((256, width), kind)
    results = pl.pallas_call(
        block_kernel,
        out_shape=outputs,
        in_specs=[pl.BlockSpec(memory_space=pl.ANY)] * 27,
        out_specs=(vmem,) * 5,
        scratch_shapes=[
            tokens(768), tokens(768), tokens(512), tokens(512), tokens(256),
            pltpu.VMEM((4, 4, 2, 16, 1536), BF16),
            pltpu.VMEM((4, 4, 2, 16, 512), BF16),
            pltpu.VMEM((4, 4, 2, 64, 1024), BF16),
            tokens(512),
            pltpu.VMEM((64, 1024), BF16),
            tokens(1536), tokens(512), tokens(512), tokens(512, F32), tokens(512, F32),
            pltpu.VMEM((4, 4, 64, 256), F32),
            pltpu.VMEM((2, 4, 64, 256), F32),
            pltpu.VMEM((64, 16, 64), F32),
            pltpu.VMEM((16, 256), F32),
            tokens(512), tokens(512), tokens(512, F32), tokens(512, F32), tokens(1536),
            tokens(512, F32), tokens(1, F32), tokens(512), tokens(512), tokens(512),
            tokens(512), tokens(512),
            pltpu.VMEM((1, 512), F32),
            tokens(512), tokens(256), tokens(512), tokens(256), tokens(512), tokens(256),
            pltpu.VMEM((64, 1024), BF16),
            pltpu.VMEM((64, 1024), BF16),
            tokens(512), tokens(1536),
            pltpu.VMEM((2, 4, 4, 32, 1024), BF16),
            pltpu.VMEM((2, 4, 4, 16, 1024), BF16),
            tokens(256),
            *[pltpu.VMEM(load.shape, load.dtype) for load in loads],
            *reduce_scratch(32, 64, 2),
            *reduce_scratch(16, 32, 3),
            sems((COPIES,)),
            sems((COPIES,)),
            sems((32,)),
        ],
        compiler_params=pltpu.CompilerParams(
            collective_id=0, has_side_effects=True, vmem_limit_bytes=60 * 1024 * 1024
        ),
        name="block_forward_backward",
    )(w_qkv, w_out, w_reduce, *loads)
    return pl.pallas_call(
        hand_on,
        out_shape=outputs,
        in_specs=[vmem] * 5,
        out_specs=(vmem,) * 5,
        name="hand_on",
    )(*results)


def solution(mesh):
    tile = P("wide", "narrow", None)
    rows = P("wide", None)
    both = P("wide", "narrow")
    return jax.shard_map(
        on_device,
        mesh=mesh,
        in_specs=(tile, both, rows, rows, rows, P(), P(), P(), P(), P(), tile),
        out_specs=(tile, tile, both, both, both),
        check_vma=False,
    )
```

```python
import jax
import jax.numpy as jnp
import numpy as np
from jax import lax
from jax.experimental import pallas as pl
from jax.experimental.pallas import tpu as pltpu
from jax.sharding import PartitionSpec as P

MESH = pl.DeviceIdType.MESH
F32 = jnp.float32
BF16 = jnp.bfloat16
NT = (((1,), (1,)), ((), ()))
TN = (((0,), (0,)), ((), ()))


def one_hot(sources):
    sources = np.asarray(sources).reshape(-1)
    table = np.zeros((len(sources), len(sources)), np.float32)
    table[np.arange(len(sources)), sources] = 1.0
    return table


def token_tables():
    i, j, r, c = np.meshgrid(*map(np.arange, (2, 8, 4, 4)), indexing="ij")
    block_from_natural = one_hot((4 * i + r) * 32 + 4 * j + c)
    k, win, mr, mc = np.meshgrid(*map(np.arange, (4, 4, 4, 4)), indexing="ij")
    i, r = mr // 2, 2 * (mr % 2) + k % 2
    j, c = 2 * win + mc // 2, 2 * (mc % 2) + k // 2
    merge_from_block = one_hot((i * 8 + j) * 16 + r * 4 + c)
    i, j, q, m = np.meshgrid(*map(np.arange, (2, 8, 4, 4)), indexing="ij")
    cot_block_from_natural = one_hot(q * 64 + (2 * i + m // 2) * 16 + 2 * j + m % 2)
    q, win, mr, mc = np.meshgrid(*map(np.arange, (4, 4, 4, 4)), indexing="ij")
    i, j, m = mr // 2, 2 * win + mc // 2, (mr % 2) * 2 + mc % 2
    cot_merge_from_block = one_hot((i * 8 + j) * 16 + q * 4 + m)
    return (
        block_from_natural,
        merge_from_block,
        cot_block_from_natural,
        cot_merge_from_block,
    )


def window_tables():
    k, mr, mc = np.meshgrid(*map(np.arange, (4, 4, 4)), indexing="ij")
    row, col = (2 * mr + k % 2).reshape(-1), (2 * mc + k // 2).reshape(-1)
    order = one_hot(row * 8 + col)
    row_cut = (row[:, None] >= 4) != (row[None, :] >= 4)
    col_cut = (col[:, None] >= 4) != (col[None, :] >= 4)
    tiled = lambda cut: np.tile(cut.astype(np.float32), (1, 4))
    return order, tiled(row_cut), tiled(col_cut)


def same_block(rows, row_size, cols, col_size):
    return (
        (np.arange(rows) // row_size)[:, None] == (np.arange(cols) // col_size)[None]
    ).astype(np.float32)


T_BLOCK, T_MERGE, T_CBLOCK, T_CMERGE = token_tables()
COLUMNS_64 = one_hot(np.arange(512).reshape(4, 2, 64).transpose(1, 0, 2)).T
COLUMNS_16 = one_hot(np.arange(512).reshape(16, 2, 16).transpose(1, 0, 2)).T
WIN_ORDER, ROW_CUT, COL_CUT = window_tables()


def const(table, dtype=BF16):
    return jnp.asarray(table, dtype)


class Place:
    def __init__(self):
        wide, narrow = lax.axis_index("wide"), lax.axis_index("narrow")
        self.wide, self.narrow = wide, narrow
        self.core = lax.rem(wide, 2)
        self.zh = lax.rem(lax.div(wide, 2), 4)
        self.x = lax.div(wide, 8)
        self.y = lax.div(narrow, 2)
        self.zl = lax.rem(narrow, 2)
        self.z = 2 * self.zh + self.zl
        self.sibling = (wide + 1 - 2 * self.core, narrow)

    def at_x(self, step):
        return ((lax.rem(self.x + step + 4, 4) * 4 + self.zh) * 2 + self.core, self.narrow)

    def at_y(self, step):
        return (self.wide, lax.rem(self.y + step + 4, 4) * 2 + self.zl)

    def at_z(self, step):
        z = lax.rem(self.z + step + 8, 8)
        return ((self.x * 4 + lax.div(z, 2)) * 2 + self.core, self.y * 2 + lax.rem(z, 2))

    def at_tile(self, rows, cols):
        return (lax.rem(self.wide + rows + 32, 32), lax.rem(self.narrow + cols + 8, 8))


class Sender:
    def __init__(self, send_sem, recv_sem, local_sem):
        self.send_sem, self.recv_sem, self.local_sem = send_sem, recv_sem, local_sem
        self.started, self.count, self.local_count, self.drained = [], 0, 0, 0

    def remote(self, src, dst, device):
        copy = pltpu.make_async_remote_copy(
            src_ref=src,
            dst_ref=dst,
            send_sem=self.send_sem.at[self.count],
            recv_sem=self.recv_sem.at[self.count],
            device_id=device,
            device_id_type=MESH,
        )
        self.count += 1
        copy.start()
        self.started.append(copy)
        return copy

    def local(self, src, dst):
        copy = pltpu.make_async_copy(src, dst, self.local_sem.at[self.local_count])
        self.local_count += 1
        copy.start()
        return copy

    def drain(self, until=None):
        until = self.count if until is None else until
        for copy in self.started[self.drained : until]:
            copy.wait_send()
        self.drained = until


def greet(devices):
    barrier = pltpu.get_barrier_semaphore()
    for device in devices:
        pl.semaphore_signal(barrier, inc=1, device_id=device, device_id_type=MESH)


def wait_for(devices):
    pl.semaphore_wait(pltpu.get_barrier_semaphore(), len(devices))


def lanes(start, size):
    return pl.ds(pl.multiple_of(start, 128), size)


def mm(a, b):
    return jnp.dot(a, b, preferred_element_type=F32)


def dg(a, b, dims):
    return lax.dot_general(a, b, dims, preferred_element_type=F32)


def add(*parts):
    total = parts[0].astype(F32)
    for one in parts[1:]:
        total = total + one.astype(F32)
    return total


def sums(values, table):
    return mm(values.astype(BF16), table)


def norm_parts(values):
    centred = values - jnp.mean(values, -1, keepdims=True)
    scale = lax.rsqrt(jnp.mean(centred * centred, -1, keepdims=True) + 1e-05)
    return centred * scale, scale


def norm_back(cot, normed, scale, gain):
    cot = cot * gain
    shared = jnp.mean(cot, -1, keepdims=True) + normed * jnp.mean(cot * normed, -1, keepdims=True)
    return scale * (cot - shared)


EVERY = pl.ds(0, 4)


class Gather:
    def __init__(self, at, go, shard, whole, cut, quarters=False, direct=False):
        self.at, self.go, self.shard, self.whole, self.cut = at, go, shard, whole, cut
        self.quarters, self.direct = quarters, direct
        self.x_left, self.x_right, self.x_far = (lax.rem(at.x + step, 4) for step in (3, 1, 2))
        self.y_left, self.y_right, self.y_far = (lax.rem(at.y + step, 4) for step in (3, 1, 2))
        self.shared = []

    def part(self, xs, zs, y=None):
        y = self.at.y if y is None else y
        return self.whole.at[(xs, zs, self.at.core) + self.cut(y)]

    def move(self, xs, zs, device, y=None):
        ref = self.part(xs, zs, y)
        return self.go.remote(ref, ref, device)

    def share(self, xs, zs, y=None):
        self.shared.append(self.move(xs, zs, self.at.sibling, y))

    def start(self):
        at = self.at
        own, there = self.shard.at[self.cut(at.y)], self.part(at.x, at.zh)
        way = 2 * at.zl - 1
        self.z = [self.go.remote(own, there, at.at_z(way * step)) for step in (1, 2, 3)]
        self.mine = self.go.local(own, there)

    def x1(self):
        at = self.at
        self.mine.wait()
        for copy in self.z:
            copy.wait_recv()
        steps = (1, 2, -1) if self.direct else (1, -1)
        self.x = [self.move(at.x, EVERY, at.at_x(step)) for step in steps]
        if not self.quarters:
            self.share(at.x, EVERY)

    def x2(self):
        at = self.at
        self.x[0].wait_recv()
        far = [self.move(self.x_left, pl.ds(0, 2), at.at_x(1))]
        self.x[1].wait_recv()
        far.append(self.move(self.x_right, pl.ds(2, 2), at.at_x(-1)))
        self.x = far
        if not self.quarters:
            self.share(self.x_left, EVERY)
            self.share(self.x_right, EVERY)

    def x3(self):
        if self.direct and not self.quarters:
            for copy, x in zip(self.x, (self.x_left, self.x_far, self.x_right)):
                copy.wait_recv()
                self.share(x, EVERY)
            return
        for copy in self.x:
            copy.wait_recv()
        if not self.quarters:
            self.share(self.x_far, EVERY)

    def y1(self):
        at = self.at
        self.x3()
        self.y = [self.move(EVERY, EVERY, at.at_y(step)) for step in (1, -1)]
        self.share(EVERY, EVERY)

    def y2(self):
        at = self.at
        self.y[0].wait_recv()
        far = [self.move(pl.ds(0, 2), EVERY, at.at_y(1), self.y_left)]
        self.y[1].wait_recv()
        far.append(self.move(pl.ds(2, 2), EVERY, at.at_y(-1), self.y_right))
        self.y = far
        self.share(EVERY, EVERY, self.y_left)
        self.share(EVERY, EVERY, self.y_right)

    def y3(self):
        for copy in self.y:
            copy.wait_recv()
        self.share(EVERY, EVERY, self.y_far)

    def done(self):
        for copy in self.shared:
            copy.wait_recv()


def y_cut(j):
    return lanes(j * 256, 256)


class Reduce:
    def __init__(self, at, go, m, bx1, bx2, by1, by2, cx, cy, dx, dy, zsend, zland, direct=False):
        self.at, self.go, self.m = at, go, m
        self.bx1, self.bx2, self.by1, self.by2 = bx1, bx2, by1, by2
        self.cx, self.cy = cx, cy
        self.dx, self.dy = dx, dy
        self.zsend, self.zland = zsend, zland
        self.xs = [lax.rem(at.x + step, 4) for step in (2, 1, 3, 0)]
        self.ys = [lax.rem(at.y + step, 4) for step in (2, 1, 3, 0)]
        self.direct, self.parts = direct, 3 if direct else 2
        self.d, self.d_y = [], []
        self.x_left, self.x_right = at.at_x(-1), at.at_x(1)
        self.y_left, self.y_right = at.at_y(-1), at.at_y(1)

    def both(self, src, dst, right, left, step):
        if step == 1:
            pairs = ((src(0, pl.ds(0, 2)), right), (src(0, pl.ds(2, 2)), left))
        else:
            pairs = ((src(1, EVERY), right), (src(2, EVERY), left))
        return [self.go.remote(ref, dst.at[n], device) for n, (ref, device) in enumerate(pairs)]

    def x_src(self, n, part):
        return self.m.at[0, self.xs[n], part]

    def y_src(self, n, part):
        return self.m.at[1, part, :, :, y_cut(self.ys[n])]

    def direct_y(self, n):
        self.d_y = self.d_y + [self.go.remote(self.y_src(n, EVERY), self.by2.at[n], self.at.at_y((2, 1, 3)[n]))]

    def direct_x(self):
        self.d_x = [
            self.go.remote(self.x_src(n, EVERY), self.bx2.at[n], self.at.at_x(step)) for n, step in ((0, 2), (1, 1), (2, 3))
        ]

    def first_x(self):
        self.b_x = self.both(self.x_src, self.bx1, self.x_right, self.x_left, 1)

    def first_y(self):
        self.b_y = self.both(self.y_src, self.by1, self.y_right, self.y_left, 1)

    def second_x(self):
        m, xs = self.m, self.xs
        for copy in self.b_x:
            copy.wait_recv()
        for s in range(2):
            m[0, xs[1], s] = add(m[0, xs[1], s], self.bx1[0, s]).astype(BF16)
            m[0, xs[2], 2 + s] = add(m[0, xs[2], 2 + s], self.bx1[1, s]).astype(BF16)
        self.b_x = self.both(self.x_src, self.bx2, self.x_right, self.x_left, 2)

    def second_y(self):
        m, ys = self.m, self.ys
        for copy in self.b_y:
            copy.wait_recv()
        for s in range(2):
            cut = y_cut(ys[1])
            m[1, s, :, :, cut] = add(m[1, s, :, :, cut], self.by1[0, s]).astype(BF16)
            cut = y_cut(ys[2])
            m[1, 2 + s, :, :, cut] = add(m[1, 2 + s, :, :, cut], self.by1[1, s]).astype(BF16)
        self.b_y = self.both(self.y_src, self.by2, self.y_right, self.y_left, 2)

    def third_x(self):
        at = self.at
        for copy in self.d_x if self.direct else self.b_x:
            copy.wait_recv()
        for s in range(4):
            self.cx[s] = add(self.m[0, at.x, s], *[self.bx2[n, s] for n in range(self.parts)]).astype(BF16)
        for n, step in ((0, 2), (1, 1), (2, 3)):
            src = self.cx.at[:, :, y_cut(self.ys[n])]
            self.d.append(self.go.remote(src, self.dx.at[n], at.at_y(step)))

    def third_y(self):
        at = self.at
        for copy in self.d_y if self.direct else self.b_y:
            copy.wait_recv()
        for s in range(4):
            own = self.m[1, s, :, :, y_cut(at.y)]
            self.cy[s] = add(own, *[self.by2[n, s] for n in range(self.parts)]).astype(BF16)
        for n, step in ((0, 2), (1, 1), (2, 3)):
            self.d.append(self.go.remote(self.cy.at[self.xs[n]], self.dy.at[n], at.at_x(step)))

    def fourth(self, pack):
        for copy in self.d:
            copy.wait_recv()
        for h in range(4):
            a = add(self.cx[h, :, y_cut(self.at.y)], *[self.dx[n, h] for n in range(3)])
            b = add(self.cy[self.at.x, h], *[self.dy[n, h] for n in range(3)])
            for low in range(2):
                self.zsend[h, low] = pack(a, b, low).astype(BF16)
        self.last = []
        for step in range(1, 8):
            z = lax.rem(self.at.z + step, 8)
            src = self.zsend.at[lax.div(z, 2), lax.rem(z, 2)]
            self.last.append(self.go.remote(src, self.zland.at[step - 1], self.at.at_z(step)))

    def fifth(self):
        total = self.zsend[self.at.zh, self.at.zl].astype(F32)
        for step in range(7):
            self.last[step].wait_recv()
            total = total + self.zland[step].astype(F32)
        return total


def pack_reduce(a, b, low):
    cut = slice(128 * low, 128 * low + 128)
    return jnp.concatenate([a[:, cut], b[:, cut]], 0)


def pack_qkv_out(a, b, low):
    if low == 0:
        rows = a[:, 0:128], jnp.concatenate([a[:, 128:192], b[:, 128:192]], 1)
    else:
        rows = (
            jnp.concatenate([a[:, 192:256], b[:, 0:64]], 1),
            jnp.concatenate([b[:, 64:128], b[:, 192:256]], 1),
        )
    return jnp.concatenate(rows, 0)


def reduce_scratch(rows, z_rows, parts):
    return [
        pltpu.VMEM((2, 2, rows, 1024), BF16),
        pltpu.VMEM((parts, 4, rows, 1024), BF16),
        pltpu.VMEM((2, 2, 4, rows, 256), BF16),
        pltpu.VMEM((parts, 4, 4, rows, 256), BF16),
        pltpu.VMEM((4, rows, 1024), BF16),
        pltpu.VMEM((4, 4, rows, 256), BF16),
        pltpu.VMEM((3, 4, rows, 256), BF16),
        pltpu.VMEM((3, 4, rows, 256), BF16),
        pltpu.VMEM((4, 2, z_rows, 128), BF16),
        pltpu.VMEM((7, z_rows, 128), BF16),
    ]


COPIES = 12 + 18 + 3 * 11 + 15 + 8 + 2 * (8 + 6 + 7) + 16


def block_kernel(
    wq_ref, wo_ref, wr_ref, *rest,
):
    loads, rest = rest[:24], rest[24:]
    (
    merged_ref, gin_ref, gq_ref, go_ref, gr_ref,
    blk, land, back, oland, ocland, wq, wo, wr,
    x_tok, cot_tok, qkv, qs, kh, rq, rk, probs, masked, bias_rows, table, att, d_att, dqs, dkh, dqkv,
    xhat, xscale, ro, dproj, dtok, xt, at_t, ls_row, ro_cols, ro_theirs, x_cols, x_theirs, at_cols, at_theirs,
    dred, dred_theirs, dproj_theirs, dqkv_theirs, fa, fb, mb,
    *rest,
    ) = rest
    held, rest = rest[:24], rest[24:]
    (
        stash_ref, exp_ref, t_block_ref, cot_ref, t_cblock_ref,
        table_ref, rel_ref, order_ref, row_cut_ref, col_cut_ref, ls_ref,
        ng_ref, mg_ref, t_merge_ref, t_cmerge_ref, t_unblock_ref, t_unmerge_ref, t_cunblock_ref, t_cunmerge_ref,
        columns_ref, columns_16_ref, bd64_ref, bd32_ref, heads_ref,
    ) = held
    a_bufs, b_bufs, (send_sem, recv_sem, local_sem) = rest[0:10], rest[10:20], rest[20:]
    go = Sender(send_sem, recv_sem, local_sem)
    at = Place()
    c = at.core
    partners = (
        [at.sibling]
        + [at.at_x(step) for step in (1, 2, 3)]
        + [at.at_y(step) for step in (1, 2, 3)]
        + [at.at_z(step) for step in range(1, 8)]
        + [at.at_tile(*step) for step in ((-1, 0), (0, -1), (-1, -1), (1, 0), (0, 1), (1, 1))]
    )
    greet(partners)
    arrivals = [go.local(src, dst) for src, dst in zip(loads, held)]

    def loaded(first, last):
        for copy in arrivals[first:last]:
            copy.wait()

    wait_for(partners)
    all_rows = pl.ds(0, 16)
    q_y = Gather(at, go, wq_ref, wq, lambda y: (all_rows, lanes(512 + 256 * y, 256)), True, True)
    q_x = Gather(at, go, wq_ref, wq, lambda y: (all_rows, pl.ds(0, 512)))
    o_x = Gather(at, go, wo_ref, wo, lambda y: (all_rows, pl.ds(0, 512)))
    r_x = Gather(at, go, wr_ref, wr, lambda y: (pl.ds(0, 64), pl.ds(0, 512)))
    r_y = Gather(at, go, wr_ref, wr, lambda y: (pl.ds(pl.multiple_of(16 * y, 16), 16), pl.ds(512, 512)), True, True)

    q_y.start()
    r_y.start()

    loaded(0, 11)
    table[...] = jnp.zeros((16, 256), F32)
    table[:, 0:225] = 16.0 * jax.nn.sigmoid(table_ref[...])
    by_head = table[...]
    high = by_head.astype(BF16)
    low = (by_head - high.astype(F32)).astype(BF16)
    both = jnp.concatenate([high, low], 0)
    rel = mm(order_ref[...], rel_ref[...].astype(F32).astype(BF16)).astype(BF16)
    rel = dg(rel, order_ref[...], NT).astype(jnp.int32)
    rel = jnp.concatenate([rel[16 * j : 16 * j + 16] for j in range(4)], 1)
    entry = lax.broadcasted_iota(jnp.int32, (256, 256), 0)

    def bias_of(rows):
        for a in rows:
            chosen = jnp.where(entry == rel[a : a + 1], 1.0, 0.0).astype(BF16)
            got = mm(both, chosen)
            got = got[0:16] + got[16:32]
            for j in range(4):
                bias_rows[16 * j + a] = got[:, 64 * j : 64 * j + 64]

    bias_of(range(0, 5))
    o_x.start()

    factor_of = exp_ref[...]
    factor_of = jnp.where(factor_of == -8, 2.0**-8, jnp.where(factor_of == -7, 2.0**-7, 2.0**-6))
    in_window = lax.broadcasted_iota(jnp.int32, (32, 512), 0) // 8
    factor = jnp.zeros((32, 512), F32)
    for w in range(4):
        factor = jnp.where(in_window == w, factor_of[:, w : w + 1], factor)
    inputs = stash_ref[...].astype(F32) * factor[None]
    blk[:, 0:512] = mm(t_block_ref[...], inputs.reshape(256, 512).astype(BF16)).astype(BF16)
    q_x.start()
    q_y.x1()
    cot = cot_ref[...].astype(F32).reshape(64, 1024).astype(BF16)
    cot = jnp.concatenate([cot[:, 256 * q : 256 * q + 256] for q in range(4)], 0)
    blk[:, 512:768] = mm(t_cblock_ref[...], cot).astype(BF16)
    r_y.x1()
    r_x.start()
    q_x.x1()
    q_y.y1()
    o_x.x1()
    halo = [
        go.remote(blk.at[pl.ds(16, 112)], land.at[pl.ds(128, 112)], at.at_tile(-1, 0)),
        go.remote(blk.at[pl.ds(128, 16)], land.at[pl.ds(112, 16)], at.at_tile(0, -1)),
        go.remote(blk.at[pl.ds(0, 16)], land.at[pl.ds(240, 16)], at.at_tile(-1, -1)),
    ]
    bias_of(range(5, 10))
    r_y.y1()
    q_x.x2()
    r_x.x1()
    bias_of(range(10, 16))
    q_y.y2()
    q_x.x3()
    o_x.x2()
    last_rows = (at.wide == 31).astype(F32)
    last_cols = (at.narrow == 7).astype(F32)
    mask = row_cut_ref[...] * last_rows * -100.0
    mask_end = jnp.maximum(row_cut_ref[...] * last_rows, col_cut_ref[...] * last_cols) * -100.0
    for g in range(4):
        bias = jnp.concatenate([bias_rows[:, 4 * g + h, :] for h in range(4)], 1)
        masked[0, g] = bias + mask
        masked[1, g] = bias + mask_end
    lane = lax.broadcasted_iota(jnp.int32, (1, 512), 1) // 32
    scales = jnp.zeros((1, 512), F32)
    for h in range(16):
        scales = jnp.where(lane == h, ls_ref[:, h : h + 1], scales)
    ls_row[...] = scales


    for copy in halo:
        copy.wait_recv()
    r_y.y2()
    q_y.y3()
    r_x.x2()
    o_x.x3()
    loaded(11, 24)
    land[pl.ds(0, 112)] = blk[pl.ds(144, 112)]
    x_tok[...] = mm(t_merge_ref[...], land[:, 0:512]).astype(BF16)
    cot = mm(t_cmerge_ref[...], land[:, 512:768]).astype(BF16)
    cot_tok[...] = jnp.concatenate([cot[64 * q : 64 * q + 64] for q in range(4)], 1)
    x_cols[...] = mm(x_tok[...], columns_16_ref[...]).astype(BF16)
    not_mine = lanes(256 * (1 - c), 256)
    mine = lanes(256 * c, 256)
    x_swap = go.remote(x_cols.at[:, not_mine], x_theirs, at.sibling)

    q_x.done()
    q_y.done()

    qkv[...] = mm(x_tok[...], wq[...].reshape(512, 1536)).astype(BF16)
    r_y.y3()
    o_x.done()
    r_x.x3()
    for start, inverse, unit in ((0, rq, qs), (512, rk, kh)):
        for n in range(2):
            cut = slice(256 * n, 256 * n + 256)
            for row in range(0, 256, 128):
                rows = slice(row, row + 128)
                raw = qkv[rows, start + 256 * n : start + 256 * n + 256].astype(F32)
                inv = lax.rsqrt(jnp.maximum(sums(raw * raw, bd32_ref[...]), 1e-24))
                inverse[rows, cut] = inv
                raw = raw * inv
                if start == 0:
                    raw = raw * ls_row[:, cut]
                unit[rows, cut] = raw.astype(BF16)
    x_swap.wait_recv()
    xt[:, 0:256] = x_cols[:, mine].T
    xt[:, 256:512] = x_theirs[...].T

    def window(ref, win, cut):
        return jnp.concatenate([ref[pl.ds(64 * k + 16 * win, 16), cut] for k in range(4)], 0)

    def put_window(ref, win, cut, values):
        for k in range(4):
            ref[pl.ds(64 * k + 16 * win, 16), cut] = values[16 * k : 16 * k + 16]

    def spread(rows):
        return jnp.concatenate([rows] * 4, 0) * heads_ref[...]

    def fold(values):
        values = values * heads_ref[...].astype(F32)
        return (values[0:64] + values[64:128]) + (values[128:192] + values[192:256])

    def forward(g):
        cut = slice(g * 128, g * 128 + 128)
        v_cut = slice(g * 128 + 1024, g * 128 + 1152)
        weights = []
        for win in range(4):
            scores = dg(window(qs, win, cut), spread(window(kh, win, cut)), NT)
            weights.append(jnp.exp(scores + masked[1 if win == 3 else 0, g]))
        totals = sums(jnp.concatenate(weights, 0), bd64_ref[...])
        for win in range(4):
            p = weights[win] / totals[64 * win : 64 * win + 64]
            probs[g, win] = p
            values = spread(window(qkv, win, v_cut))
            put_window(att, win, cut, mm(p.astype(BF16), values).astype(BF16))

    for g in range(4):
        forward(g)
    at_cols[...] = mm(att[...], columns_16_ref[...]).astype(BF16)
    at_swap = go.remote(at_cols.at[:, not_mine], at_theirs, at.sibling)
    r_y.done()
    xhat[...] = mm(att[...], wo[...].reshape(512, 512))
    for row in range(0, 256, 64):
        rows = slice(row, row + 64)
        normed, scale = norm_parts(xhat[rows])
        xhat[rows] = normed
        xscale[rows] = scale
        ro[rows] = (x_tok[rows].astype(F32) + normed * ng_ref[...]).astype(BF16)
    ro_cols[...] = mm(ro[...], columns_ref[...]).astype(BF16)
    swap = [go.remote(ro_cols.at[:, not_mine], ro_theirs, at.sibling)]
    r_x.done()

    reduced = jnp.zeros((64, 1024), F32)
    for k in range(4):
        reduced += mm(ro[64 * k : 64 * k + 64], wr[k].reshape(512, 1024))
    normed, scale = norm_parts(reduced)
    dred[...] = norm_back(cot_tok[...].astype(F32), normed, scale, mg_ref[...]).astype(BF16)
    swap.append(go.remote(dred, dred_theirs, at.sibling))
    merged = (normed * mg_ref[...]).astype(BF16)
    merged = jnp.concatenate([merged[:, 256 * q : 256 * q + 256] for q in range(4)], 0)
    mb[...] = mm(t_cunmerge_ref[...], merged).astype(BF16)

    def send_back(tile, landing):
        return [
            go.remote(tile.at[pl.ds(128, 112)], landing.at[pl.ds(16, 112)], at.at_tile(1, 0)),
            go.remote(tile.at[pl.ds(112, 16)], landing.at[pl.ds(128, 16)], at.at_tile(0, 1)),
            go.remote(tile.at[pl.ds(240, 16)], landing.at[pl.ds(0, 16)], at.at_tile(1, 1)),
        ]

    for k in range(4):
        dtok[64 * k : 64 * k + 64] = dg(dred[...], wr[k].reshape(512, 1024), NT).astype(BF16)

    for row in range(0, 256, 64):
        rows = slice(row, row + 64)
        got = norm_back(dtok[rows].astype(F32), xhat[rows], xscale[rows], ng_ref[...])
        dproj[rows] = got.astype(BF16)
    dproj_swap = go.remote(dproj, dproj_theirs, at.sibling)
    d_att[...] = dg(dproj[...], wo[...].reshape(512, 512), NT).astype(BF16)

    for copy in swap:
        copy.wait_recv()
    before_a = go.count
    a_sum = Reduce(at, go, fa, *a_bufs)
    grads = jnp.concatenate([dred[...], dred_theirs[...]], 0)
    for n in range(4):
        k = a_sum.xs[n]
        rows = pl.ds(pl.multiple_of(64 * k, 64), 64)
        tokens = jnp.concatenate([ro_cols[rows, mine], ro_theirs[rows]], 0).T
        for cut in (slice(0, 512), slice(512, 1024)):
            got = mm(tokens, grads[:, cut]).astype(BF16).reshape(4, 64, 512)
            fa[0, k, :, :, cut] = got[:, 0:32]
            fa[1, k, :, :, cut] = got[:, 32:64]
        if n == 0:
            a_sum.first_x()
    a_sum.first_y()

    def backward(g):
        cut = slice(g * 128, g * 128 + 128)
        v_cut = slice(g * 128 + 1024, g * 128 + 1152)
        dps = []
        for win in range(4):
            dp = dg(window(d_att, win, cut), spread(window(qkv, win, v_cut)), NT)
            dps.append(dp.astype(BF16).astype(F32))
        alike = sums(jnp.concatenate([probs[g, win] * dps[win] for win in range(4)], 0), bd64_ref[...])
        for win in range(4):
            p = probs[g, win]
            ds = (p * (dps[win] - alike[64 * win : 64 * win + 64])).astype(BF16)
            put_window(dqs, win, cut, mm(ds, spread(window(kh, win, cut))))
            put_window(dkh, win, cut, fold(dg(ds, window(qs, win, cut), TN)))
            put_window(dqkv, win, v_cut, fold(dg(p.astype(BF16), window(d_att, win, cut), TN)).astype(BF16))

    for g in range(4):
        backward(g)

    def swap_dqkv(start):
        cut = pl.ds(start, 512)
        return go.remote(dqkv.at[:, cut], dqkv_theirs.at[:, cut], at.sibling)

    dqkv_swap = [swap_dqkv(1024)]
    a_sum.second_x()
    a_sum.second_y()
    for start, inverse, grad in ((0, rq, dqs), (512, rk, dkh)):
        for n in range(2):
            cut = slice(256 * n, 256 * n + 256)
            both_cut = slice(start + 256 * n, start + 256 * n + 256)
            for row in range(0, 256, 128):
                rows = slice(row, row + 128)
                inv = inverse[rows, cut]
                unit = qkv[rows, both_cut].astype(F32) * inv
                d_unit = grad[rows, cut]
                if start == 0:
                    d_unit = d_unit * ls_row[:, cut]
                along = sums(unit * d_unit, bd32_ref[...])
                along = jnp.where(inv < 1e12, along, 0.0)
                dqkv[rows, both_cut] = (inv * (d_unit - unit * along)).astype(BF16)
        dqkv_swap.append(swap_dqkv(start))
    at_swap.wait_recv()
    at_t[:, 0:256] = at_cols[:, mine].T
    at_t[:, 256:512] = at_theirs[...].T
    dproj_swap.wait_recv()
    d_out = jnp.concatenate([dproj[...], dproj_theirs[...]], 0)
    out = mm(at_t[...], d_out).astype(BF16)
    for y in range(4):
        fb[1, :, :, :, 256 * y + 128 : 256 * y + 256] = out[:, 128 * y : 128 * y + 128].reshape(4, 4, 16, 128)

    merged_back = send_back(mb, ocland)
    d_in = dtok[...].astype(F32) + dg(dqkv[...], wq[...].reshape(512, 1536), NT)
    back[...] = mm(t_unmerge_ref[...], d_in.astype(BF16)).astype(BF16)
    grad_back = send_back(back, oland)

    for copy in dqkv_swap:
        copy.wait_recv()
    before_b = go.count
    b_sum = Reduce(at, go, fb, *b_bufs, direct=True)
    for n in range(4):
        y = b_sum.ys[n]
        cut = lanes(384 * y, 384)
        grads = jnp.concatenate([dqkv[:, cut], dqkv_theirs[:, cut]], 0)
        got = mm(xt[...], grads).astype(BF16)
        fb[0, :, :, :, y_cut(y)] = got[:, 0:256].reshape(4, 4, 16, 256)
        fb[1, :, :, :, lanes(256 * y, 128)] = got[:, 256:384].reshape(4, 4, 16, 128)
        if n < 3:
            b_sum.direct_y(n)
    b_sum.direct_x()
    go.drain(before_a // 2)
    a_sum.third_x()
    a_sum.third_y()
    go.drain(before_b)
    before_c = go.count
    b_sum.third_y()
    b_sum.third_x()
    a_sum.fourth(pack_reduce)
    b_sum.fourth(pack_qkv_out)
    go.drain(before_c)
    for copy in merged_back + grad_back:
        copy.wait_recv()
    oland[pl.ds(144, 112)] = back[pl.ds(0, 112)]
    ocland[pl.ds(144, 112)] = mb[pl.ds(0, 112)]
    gin_ref[...] = mm(t_unblock_ref[...], oland[...]).astype(BF16).reshape(8, 32, 512)
    got = mm(t_cunblock_ref[...], ocland[...]).astype(BF16)
    for q in range(4):
        merged_ref[:, :, 256 * q : 256 * q + 256] = got[64 * q : 64 * q + 64].reshape(4, 16, 256)
    factor = 1.0 / 256.0
    gr_ref[...] = a_sum.fifth() * factor
    go.drain()
    total = b_sum.fifth() * factor
    gq_ref[:, 0:128] = total[0:16]
    gq_ref[:, 128:192] = total[16:32, 0:64]
    go_ref[...] = total[16:32, 64:128]


def hand_on(*refs):
    for src, dst in zip(refs[:5], refs[5:]):
        dst[...] = src[...]


def on_device(
    stash_values, scale_exp, w_qkv, w_out, w_reduce, logit_scale, bias_table, rel_index, norm_gain, merge_gain, cotangent
):
    vmem = pl.BlockSpec(memory_space=pltpu.VMEM)
    sems = pltpu.SemaphoreType.DMA
    outputs = (
        jax.ShapeDtypeStruct((4, 16, 1024), BF16),
        jax.ShapeDtypeStruct((8, 32, 512), BF16),
        jax.ShapeDtypeStruct((16, 192), F32),
        jax.ShapeDtypeStruct((16, 64), F32),
        jax.ShapeDtypeStruct((64, 128), F32),
    )
    loads = (
        stash_values, scale_exp, const(T_BLOCK), cotangent, const(T_CBLOCK),
        bias_table.T, rel_index, const(WIN_ORDER), const(ROW_CUT, F32), const(COL_CUT, F32), logit_scale.reshape(1, 16),
        norm_gain.reshape(1, 512), merge_gain.reshape(1, 1024),
        const(T_MERGE), const(T_CMERGE), const(T_BLOCK.T), const(T_MERGE.T), const(T_CBLOCK.T), const(T_CMERGE.T),
        const(COLUMNS_64), const(COLUMNS_16),
        const(same_block(256, 64, 256, 64)), const(same_block(256, 32, 256, 32)), const(same_block(256, 64, 128, 32)),
    )
    tokens = lambda width, kind=BF16: pltpu.VMEM((256, width), kind)
    results = pl.pallas_call(
        block_kernel,
        out_shape=outputs,
        in_specs=[pl.BlockSpec(memory_space=pl.ANY)] * 27,
        out_specs=(vmem,) * 5,
        scratch_shapes=[
            tokens(768), tokens(768), tokens(512), tokens(512), tokens(256),
            pltpu.VMEM((4, 4, 2, 16, 1536), BF16),
            pltpu.VMEM((4, 4, 2, 16, 512), BF16),
            pltpu.VMEM((4, 4, 2, 64, 1024), BF16),
            tokens(512),
            pltpu.VMEM((64, 1024), BF16),
            tokens(1536), tokens(512), tokens(512), tokens(512, F32), tokens(512, F32),
            pltpu.VMEM((4, 4, 64, 256), F32),
            pltpu.VMEM((2, 4, 64, 256), F32),
            pltpu.VMEM((64, 16, 64), F32),
            pltpu.VMEM((16, 256), F32),
            tokens(512), tokens(512), tokens(512, F32), tokens(512, F32), tokens(1536),
            tokens(512, F32), tokens(1, F32), tokens(512), tokens(512), tokens(512),
            tokens(512), tokens(512),
            pltpu.VMEM((1, 512), F32),
            tokens(512), tokens(256), tokens(512), tokens(256), tokens(512), tokens(256),
            pltpu.VMEM((64, 1024), BF16),
            pltpu.VMEM((64, 1024), BF16),
            tokens(512), tokens(1536),
            pltpu.VMEM((2, 4, 4, 32, 1024), BF16),
            pltpu.VMEM((2, 4, 4, 16, 1024), BF16),
            tokens(256),
            *[pltpu.VMEM(load.shape, load.dtype) for load in loads],
            *reduce_scratch(32, 64, 2),
            *reduce_scratch(16, 32, 3),
            sems((COPIES,)),
            sems((COPIES,)),
            sems((32,)),
        ],
        compiler_params=pltpu.CompilerParams(
            collective_id=0, has_side_effects=True, vmem_limit_bytes=60 * 1024 * 1024
        ),
        name="block_forward_backward",
    )(w_qkv, w_out, w_reduce, *loads)
    return pl.pallas_call(
        hand_on,
        out_shape=outputs,
        in_specs=[vmem] * 5,
        out_specs=(vmem,) * 5,
        name="hand_on",
    )(*results)


def solution(mesh):
    tile = P("wide", "narrow", None)
    rows = P("wide", None)
    both = P("wide", "narrow")
    return jax.shard_map(
        on_device,
        mesh=mesh,
        in_specs=(tile, both, rows, rows, rows, P(), P(), P(), P(), P(), tile),
        out_specs=(tile, tile, both, both, both),
        check_vma=False,
    )
```
